32 devices in a mesh: dp: 8 (over y, x, core), tensor: 4 (over z).
Axes of the slice: x: 2, y: 2, z: 4, core: 2. Of those that a mesh axis runs over, the one named last changes fastest.
Arguments:
- tokens: bfloat16 [48, 256, 768], P('dp', 'tensor'), may hold values from -6 to 6
- cotangent: bfloat16 [48, 256, 768], P('dp', 'tensor'), may hold values from -6 to 6
- task_ids: int32 [48, 2], P('dp'), may hold values from 0 to 7
- key_mask: int32 [48, 256], P('dp'), may hold values from 0 to 1, as said below
- prompts: bfloat16 [2, 8, 50, 768], replicated, may hold values from -6 to 6
- norm_gain: bfloat16 [2, 2, 768], replicated, may hold values from 0.099609375 to 1.8984375
- norm_bias: bfloat16 [2, 2, 768], replicated, may hold values from -4 to 4
- qkv_weight: bfloat16 [2, 768, 2304], P(None, None, 'tensor'), may hold values from -0.21875 to 0.21875
- qv_bias: bfloat16 [2, 1536], P(None, 'tensor'), may hold values from -4 to 4
- out_weight: bfloat16 [2, 768, 768], P(None, 'tensor'), may hold values from -0.625 to 0.625
- branch_bias: bfloat16 [2, 2, 768], replicated, may hold values from -4 to 4
- up_weight: bfloat16 [2, 768, 3072], P(None, None, 'tensor'), may hold values from -0.21875 to 0.21875
- up_bias: bfloat16 [2, 3072], P(None, 'tensor'), may hold values from -4 to 4
- down_weight: bfloat16 [2, 3072, 768], P(None, 'tensor'), may hold values from -0.109375 to 0.109375
Outputs:
- out: bfloat16 [48, 256, 768], P('dp', 'tensor')
- grad_tokens: bfloat16 [48, 256, 768], P('dp', 'tensor')
- grad_prompts: float32 [2, 8, 50, 768], P(None, 'dp', None, 'tensor')
- grad_norm_gain: float32 [2, 2, 768], P(None, None, 'tensor')
- grad_norm_bias: float32 [2, 2, 768], P(None, None, 'tensor')
- grad_qkv_weight: float32 [2, 768, 2304], P(None, None, 'tensor')
- grad_qv_bias: float32 [2, 1536], P(None, 'tensor')
- grad_out_weight: float32 [2, 768, 768], P(None, 'tensor')
- grad_branch_bias: float32 [2, 2, 768], P(None, None, 'tensor')
- grad_up_weight: float32 [2, 768, 3072], P(None, None, 'tensor')
- grad_up_bias: float32 [2, 3072], P(None, 'tensor')
- grad_down_weight: float32 [2, 3072, 768], P(None, 'tensor')
The draws below stay inside these ranges and needn't reach their ends.
Inputs may be any that keep to these rules, and one draw needn't show every extreme that they name: `key_mask`: each image's rows are 1 for its first 51 + n rows and 0 after, with 98 <= n <= 196; the first image has n = 196.
All inputs are finite; a program needn't handle non-finite values.
Results may differ from the reference program's by a relative error of at most 0.025.
Values may be sent and summed in bfloat16 or wider, within the bound.
No kernel may reach another device: no remote copies, remote signals or barrier semaphores. Data moves between devices by JAX's collectives and lax.ppermute only.
A program may use at most 192 MiB of HBM per device.

```python
import math
import jax
import jax.numpy as jnp
import numpy as np
from jax import lax

D = 768
HEADS = 12
HEAD_DIM = 64
FF = 3072
LAYERS = 2
PROMPTS = 50
PATCHES = 196
SEQ = 256
IMG_DEV = 6
IMAGES = 48
TASKS = 8


def draw_key_mask(key, part):
    key = jax.random.fold_in(key, 7)
    counts = jax.random.randint(key, (IMAGES,), PATCHES // 2, PATCHES + 1)
    counts = counts.at[0].set(PATCHES)
    places = jnp.arange(SEQ)
    return (places[None, :] < (1 + PROMPTS + counts)[:, None]).astype(jnp.int32)


def touch_ends(drawn, own_key, least, high):
    dims = drawn.shape
    place = [jax.random.randint(jax.random.fold_in(own_key, axis), (), 0, dims[axis]) for axis in range(len(dims))]
    drawn = drawn.at[tuple(place)].set(least)
    longest = dims.index(max(dims))
    place[longest] = (place[longest] + 1) % dims[longest]
    return drawn.at[tuple(place)].set(high)


def levels(key, shape, split, least, high):
    def one(axis_at, parts):
        heights = jax.random.uniform(jax.random.fold_in(jax.random.fold_in(key, 6), axis_at), (parts,), jnp.float32, least / len(split), high / len(split))
        return jnp.repeat(jnp.exp(heights), shape[axis_at] // parts).reshape((-1,) + (1,) * (len(shape) - axis_at - 1))

    gain = one(*split[0])
    for cut in split[1:]:
        gain = gain * one(*cut)
    return gain


def rank_bounds(number_of, skew):
    portions = [(1 << 20) // math.isqrt(grade ** skew) + 1 for grade in range(1, number_of + 1)]
    deviation = 1 + sum(portions) // (1 << 30)
    return np.cumsum(np.array([max(1, weight // deviation) for weight in portions]))


def skewed_ids(rng, dims, count, lean):
    listing = rank_bounds(count, lean)
    pick = jax.random.randint(jax.random.fold_in(rng, 1), dims, 0, int(listing[count - 1]))
    rank = jnp.searchsorted(jnp.asarray(listing, jnp.int32), pick, side="right")
    return jax.random.permutation(jax.random.fold_in(rng, 2), count)[rank].astype(jnp.int32)


def normal_values(own_key, extent, width, most, pieces=(), held_as=jnp.bfloat16):
    drawn = width * jax.random.normal(own_key, extent, jnp.float32)
    if pieces:
        drawn = drawn * levels(own_key, extent, pieces, -0.22, 0.18)
    return jnp.clip(drawn, -most, most).astype(held_as)


def setup_inputs(seed: int = 0) -> dict:
    streams_of = jax.random.split(jax.random.key(seed), 15)
    tokens = normal_values(streams_of[0], (IMAGES, SEQ, D), 1.0, 6.0, ((0, 8), (1, 4)))
    cotangent = normal_values(streams_of[1], (IMAGES, SEQ, D), 1.0, 6.0, ((0, 8), (1, 4)))
    task_ids = touch_ends(skewed_ids(streams_of[2], (IMAGES, LAYERS), TASKS, 2), jax.random.fold_in(streams_of[2], 3), 0, TASKS - 1).astype(jnp.int32)
    key_mask = draw_key_mask(jax.random.fold_in(streams_of[14], 71), 0)
    prompts = normal_values(streams_of[4], (LAYERS, TASKS, PROMPTS, D), 1.0, 6.0)
    norm_gain = jnp.clip(1.0 + 0.18 * jax.random.normal(streams_of[5], (LAYERS, 2, D), jnp.float32), 0.099609375, 1.8984375).astype(jnp.bfloat16)
    norm_bias = normal_values(streams_of[6], (LAYERS, 2, D), 0.3, 4.0)
    qkv_weight = normal_values(streams_of[7], (LAYERS, D, 3 * D), D ** -0.5, 0.21875, ((2, 4),))
    qv_bias = normal_values(streams_of[8], (LAYERS, 2 * D), 0.3, 4.0, ((1, 4),))
    out_weight = normal_values(streams_of[9], (LAYERS, D, D), (D // 8) ** -0.5, 0.625, ((1, 4),))
    branch_bias = normal_values(streams_of[10], (LAYERS, 2, D), 0.3, 4.0)
    up_weight = normal_values(streams_of[11], (LAYERS, D, FF), D ** -0.5, 0.21875, ((2, 4),))
    up_bias = normal_values(streams_of[12], (LAYERS, FF), 0.3, 4.0, ((1, 4),))
    down_weight = normal_values(streams_of[13], (LAYERS, FF, D), FF ** -0.5, 0.109375, ((1, 4),))
    return {"tokens": tokens, "cotangent": cotangent, "task_ids": task_ids, "key_mask": key_mask, "prompts": prompts, "norm_gain": norm_gain, "norm_bias": norm_bias, "qkv_weight": qkv_weight, "qv_bias": qv_bias, "out_weight": out_weight, "branch_bias": branch_bias, "up_weight": up_weight, "up_bias": up_bias, "down_weight": down_weight}


@jax.custom_vjp
def low(v):
    return lax.optimization_barrier(v.astype(jnp.bfloat16)).astype(jnp.float32)

@jax.custom_vjp
def low_back(v):
    return v

def low_keep(v):
    return (low(v), None)

def low_pass(kept, grad):
    return (grad,)

def back_keep(v):
    return (v, None)

def back_low(kept, grad):
    return (low(grad),)
low.defvjp(low_keep, low_pass)
low_back.defvjp(back_keep, back_low)
epsilon = 1e-06
highest = lax.Precision.HIGHEST

def layer_norm(tok_rows, gain_vec, shift_vec):
    centre = tok_rows - lax.optimization_barrier(jnp.mean(tok_rows, axis=-1, keepdims=True))
    spread = lax.optimization_barrier(jnp.mean(centre * centre, axis=-1, keepdims=True))
    return centre * lax.rsqrt(spread + epsilon) * gain_vec + shift_vec

def vpt_block(layer_idx, tok_rows, params, task_col, valid_rows):
    prompts, norm_gain, norm_bias, qkv_weight, qv_bias, out_weight, branch_bias, up_weight, up_bias, down_weight = params
    images = tok_rows.shape[0]
    chosen = prompts[layer_idx][task_col]
    placed = jnp.pad(chosen, ((0, 0), (1, SEQ - 1 - PROMPTS), (0, 0)))
    places = jnp.arange(SEQ)
    is_prompt = (places >= 1) & (places <= PROMPTS)
    tok_rows = jnp.where(is_prompt[None, :, None], placed, tok_rows)
    first_in = low(layer_norm(tok_rows, norm_gain[layer_idx, 0], norm_bias[layer_idx, 0]))
    qkv_all = jnp.einsum('gsd,dhce->gshce', first_in, qkv_weight[layer_idx].reshape(D, HEADS, 3, HEAD_DIM), precision=highest)
    pair_bias = qv_bias[layer_idx].reshape(HEADS, 2, HEAD_DIM)
    score_scale = HEAD_DIM ** (-0.5)
    query_rows = low(low_back((qkv_all[:, :, :, 0] + pair_bias[:, 0]) * score_scale))
    key_rows = low(low_back(qkv_all[:, :, :, 1]))
    value_rows = low(low_back(qkv_all[:, :, :, 2] + pair_bias[:, 1]))
    scores = jnp.einsum('gqhe,gkhe->ghqk', query_rows, key_rows, precision=highest)
    scores = low_back(jnp.where(valid_rows[:, None, None, :] > 0, scores, -1000000000.0))
    attn_probs = low(jax.nn.softmax(scores, axis=-1))
    mixed_heads = jnp.einsum('ghqk,gkhe->gqhe', attn_probs, value_rows, precision=highest)
    mixed_heads = low(low_back(mixed_heads.reshape(images, SEQ, D)))
    attn_out = low_back(jnp.einsum('gsc,cd->gsd', mixed_heads, out_weight[layer_idx], precision=highest))
    tok_rows = tok_rows + (attn_out + branch_bias[layer_idx, 0])
    second = low(layer_norm(tok_rows, norm_gain[layer_idx, 1], norm_bias[layer_idx, 1]))
    hidden = low_back(jnp.einsum('gsd,df->gsf', second, up_weight[layer_idx], precision=highest) + up_bias[layer_idx])
    active = low(jax.nn.gelu(hidden, approximate=False))
    branch = low_back(jnp.einsum('gsf,fd->gsd', active, down_weight[layer_idx], precision=highest))
    return tok_rows + (branch + branch_bias[layer_idx, 1])

def stack_forward(params, tok_rows, task_rows, valid_rows):
    for layer_idx in range(LAYERS):
        tok_rows = vpt_block(layer_idx, tok_rows, params, task_rows[:, layer_idx], valid_rows)
    return tok_rows * valid_rows[:, :, None].astype(tok_rows.dtype)

def add_up(left_sum, right_sum):
    return left_sum + right_sum

def reference(tokens, cotangent, task_ids, key_mask, prompts, norm_gain, norm_bias, qkv_weight, qv_bias, out_weight, branch_bias, up_weight, up_bias, down_weight):
    params = tuple((weight_arr.astype(jnp.float32) for weight_arr in (prompts, norm_gain, norm_bias, qkv_weight, qv_bias, out_weight, branch_bias, up_weight, up_bias, down_weight)))
    groups = tokens.shape[0] // IMG_DEV

    def shaped(array_in):
        return array_in.reshape((groups, IMG_DEV) + array_in.shape[1:])

    def group_step(totals, group_item):
        tok_rows, cot_rows, task_rows, valid_rows = group_item

        def run_group(param_set, row_set):
            return stack_forward(param_set, row_set, task_rows, valid_rows)
        result, pull_back = jax.vjp(run_group, params, tok_rows)
        grad_params, grad_in = pull_back(cot_rows)
        totals = jax.tree.map(add_up, totals, grad_params)
        return (totals, (result, grad_in))
    zero_sums = jax.tree.map(jnp.zeros_like, params)
    inputs = (shaped(tokens.astype(jnp.float32)), shaped(cotangent.astype(jnp.float32)), shaped(task_ids), shaped(key_mask))
    totals, (out_rows, grad_rows) = lax.scan(group_step, zero_sums, inputs)
    out_rows = out_rows.reshape(tokens.shape).astype(jnp.bfloat16)
    grad_rows = grad_rows.reshape(tokens.shape).astype(jnp.bfloat16)
    return (out_rows, grad_rows, totals[0], totals[1], totals[2], totals[3], totals[4], totals[5], totals[6], totals[7], totals[8], totals[9])
```

```python
import jax
import jax.numpy as jnp
from jax import lax
from jax.sharding import PartitionSpec as P

HEAD_DIM = 64
LAYERS = 2
PROMPTS = 50
AXES = ("dp", "tensor")
epsilon = 1e-06
bf16 = jnp.bfloat16
f32 = jnp.float32


def dot(left, right, left_dim, right_dim):
    return lax.dot_general(
        left, right, (((left_dim,), (right_dim,)), ((), ())), preferred_element_type=f32
    )


def norm_parts(rows):
    centre = rows - jnp.mean(rows, axis=-1, keepdims=True)
    spread = jnp.mean(centre * centre, axis=-1, keepdims=True)
    scale = lax.rsqrt(spread + epsilon)
    return centre * scale, scale


def norm_back(hat, scale, gain, grad):
    inner = grad * gain
    along = jnp.mean(inner * hat, axis=-1, keepdims=True)
    return scale * (inner - jnp.mean(inner, axis=-1, keepdims=True) - hat * along)


def gate_pair(pre):
    half = 0.5 * (1.0 + lax.erf(pre * (0.5**0.5)))
    slope = half + pre * jnp.exp(-0.5 * pre * pre) * 0.3989422804014327
    return (pre * half).astype(bf16), slope.astype(bf16)


def reversed_bits(value, bits):
    return sum(((value >> b) & 1) << (bits - 1 - b) for b in range(bits))


def xor_order(arr, axis, index, bits):
    for b in range(bits):
        shape = arr.shape
        split = shape[:axis] + (shape[axis] >> (b + 1), 2, 1 << b) + shape[axis + 1 :]
        parts = arr.reshape(split)
        arr = jnp.where(((index >> b) & 1) == 1, jnp.flip(parts, axis + 1), parts).reshape(shape)
    return arr


def build(dp_size, tensor_size):
    planes = dp_size // 2
    bits = planes.bit_length() - 1
    zbits = tensor_size.bit_length() - 1

    def send(arr, target):
        pairs = []
        for dp in range(dp_size):
            for z in range(tensor_size):
                to = target(dp >> 1, dp & 1, z)
                if to is not None:
                    plane, core, depth = to
                    pairs.append((dp * tensor_size + z, (plane * 2 + core) * tensor_size + depth))
        return lax.ppermute(arr, AXES, pairs)

    def other_core(p, c, z):
        return p, 1 - c, z

    def along(k):
        return lambda p, c, z: (p, c, z ^ k)

    def flip(step, turned, only=None):
        def target(p, c, z):
            if only is not None and c != only:
                return None
            back = turned(c)
            return p ^ (1 << ((bits - 1 - step) if back else step)), c, z

        return target

    def plane_gather(piece, turned, only=None):
        acc = piece[None]
        for step in range(bits):
            got = send(acc, flip(step, turned, only))
            acc = jnp.concatenate([acc, got], axis=0)
        return acc

    def plane_scatter(acc, turned, extra=None):
        for step in range(bits):
            pairs = acc.reshape((acc.shape[0] // 2, 2) + acc.shape[1:])
            got = send(pairs[:, 1], flip(step, turned))
            acc = (pairs[:, 0].astype(f32) + got.astype(f32)).astype(bf16)
        return acc[0]

    def by_core(c):
        return c

    def per_device(
        tokens,
        cotangent,
        task_ids,
        key_mask,
        prompts,
        norm_gain,
        norm_bias,
        qkv_weight,
        qv_bias,
        out_weight,
        branch_bias,
        up_weight,
        up_bias,
        down_weight,
    ):
        group, rows_local, width = tokens.shape
        images = group // 2
        seq = rows_local * tensor_size
        heads = qkv_weight.shape[2] // (3 * HEAD_DIM)
        hidden = up_weight.shape[2]
        half_units = hidden // 2
        unit_q = half_units // planes
        dim_q = HEAD_DIM // planes
        task_count = prompts.shape[1]
        per_dev = task_count // dp_size
        score_scale = HEAD_DIM ** (-0.5)
        place = lax.axis_index("dp")
        z = lax.axis_index("tensor")
        core = place & 1
        plane = place >> 1
        plane_back = reversed_bits(plane, bits)
        first_core = core == 0
        odd = z & 1
        all_rows = images * seq

        def pick(arr, index, axis):
            return lax.dynamic_index_in_dim(arr, index, axis, keepdims=False)

        def ordered(arr, axis, index):
            parts = [pick(arr, index ^ r, axis) for r in range(planes)]
            return jnp.stack(parts, axis=0)

        def join(mine, theirs, axis):
            return jnp.where(
                first_core,
                jnp.concatenate([mine, theirs], axis),
                jnp.concatenate([theirs, mine], axis),
            )

        def gather_images(arr):
            one = lax.dynamic_slice_in_dim(arr, odd * images, images, 0)
            two = lax.dynamic_slice_in_dim(arr, (1 - odd) * images, images, 0)
            got_one = send(one, lambda p, c, d: (p, d >> 1, 2 * c + (d & 1)))
            got_two = send(two, lambda p, c, d: (p, d >> 1, 2 * c + 1 - (d & 1)))
            half = jnp.where(
                odd == 0,
                jnp.concatenate([got_one, got_two], 1),
                jnp.concatenate([got_two, got_one], 1),
            )
            return join(half, send(half, other_core), 1)

        def spread_images(arr):
            one = lax.dynamic_slice_in_dim(arr, rows_local * (2 * core + odd), rows_local, 1)
            two = lax.dynamic_slice_in_dim(arr, rows_local * (2 * core + 1 - odd), rows_local, 1)
            got_one = send(one, lambda p, c, d: (p, d >> 1, 2 * c + (d & 1)))
            got_two = send(two, lambda p, c, d: (p, d >> 1, 2 * c + 1 - (d & 1)))
            return jnp.where(
                odd == 0,
                jnp.concatenate([got_one, got_two], 0),
                jnp.concatenate([got_two, got_one], 0),
            )

        def exchange(part):
            part = part.astype(bf16)
            return part.astype(f32) + send(part, other_core).astype(f32)

        facts = jnp.concatenate([key_mask, task_ids], axis=1)
        facts = lax.dynamic_slice_in_dim(facts, odd * images, images, 0)
        facts = jnp.where(core == (z >> 1), facts, send(facts, other_core))
        mask, tasks = facts[:, :seq], facts[:, seq:]
        valid = (mask > 0)[:, None, None, :]
        row_mask = mask.astype(f32)[:, :, None]

        gains = norm_gain.astype(f32)
        shifts = norm_bias.astype(f32)
        biases = branch_bias.astype(f32)

        bias_pack = jnp.concatenate([up_bias, qv_bias], axis=1)
        bias_all = lax.all_gather(bias_pack, "tensor", axis=0)
        bias_all = xor_order(bias_all, 0, z, zbits).astype(f32)

        def turned_attn(layer):
            return lambda c: layer % 2

        def attn_place(layer):
            return plane_back if layer % 2 else plane

        unit_place = jnp.where(first_core, plane, plane_back)
        unit_place_other = jnp.where(first_core, plane_back, plane)

        def attn_weights(layer):
            qkv_rows = qkv_weight[layer].T.reshape(heads, 3, HEAD_DIM, width).swapaxes(0, 1)
            out_rows = out_weight[layer].reshape(1, heads, HEAD_DIM, width)
            own = jnp.concatenate([qkv_rows, out_rows], axis=0)
            own = own.reshape(4, heads, planes, dim_q, width)
            own = ordered(own, 2, attn_place(layer))
            piece = own[0]
            turned = turned_attn(layer)
            near = send(piece, lambda p, c, d: (p, c, d ^ (1 + c)))
            far = send(piece, lambda p, c, d: (p, c, d ^ 3) if c else None)
            near = plane_gather(near, turned)
            far = plane_gather(far, turned, only=1)
            whole = jnp.stack([jnp.where(first_core, own, far), near])
            whole = whole.transpose(2, 0, 3, 1, 4, 5)
            whole = whole.reshape(4, 2 * heads * HEAD_DIM, width)
            pair = bias_all[:, layer, hidden:].reshape(tensor_size, heads, 2, planes, dim_q)
            pair = xor_order(pair, 3, attn_place(layer), bits)
            pair = jnp.where(first_core, pair[:2], jnp.flip(pair[2:], 0))
            pair = pair.transpose(2, 0, 1, 3, 4).reshape(2, 2 * heads * HEAD_DIM)
            return whole[:3].reshape(-1, width), whole[3], pair[0], pair[1]

        def mlp_weights(layer):
            own = jnp.stack([up_weight[layer].T, down_weight[layer]])
            own = own.reshape(2, 2, planes, unit_q, width)
            own = ordered(pick(own, core, 1), 1, unit_place)
            piece = own[0]
            got = jnp.stack([send(piece, along(k)) for k in range(1, tensor_size)])
            got = plane_gather(got, by_core)
            whole = jnp.concatenate([own[:, None], got], axis=1)
            whole = whole.transpose(2, 0, 1, 3, 4).reshape(2, -1, width)
            bias = bias_all[:, layer, :hidden].reshape(tensor_size, 2, planes, unit_q)
            bias = xor_order(pick(bias, core, 1), 1, unit_place, bits)
            return whole[0], whole[1], bias.swapaxes(0, 1).reshape(-1)

        def heads_of(arr):
            return arr.reshape(images, seq, 2 * heads, HEAD_DIM)

        def scores_of(query, key):
            raw = jnp.einsum("iqhe,ikhe->ihqk", query, key, preferred_element_type=f32)
            return jnp.where(valid, raw, -1000000000.0)

        inner = 2 * heads * HEAD_DIM
        x = gather_images(tokens).astype(f32)
        kept = []
        for layer in range(LAYERS):
            chosen = jnp.stack(
                [pick(prompts[layer], tasks[i, layer], 0) for i in range(images)]
            ).astype(f32)
            xp = jnp.concatenate([x[:, :1], chosen, x[:, 1 + PROMPTS :]], axis=1)
            xp = xp.reshape(all_rows, width)
            hat, scale = norm_parts(xp)
            first_in = (hat * gains[layer, 0] + shifts[layer, 0]).astype(bf16)
            w_qkv, w_out, q_bias, v_bias = attn_weights(layer)
            qkv = dot(first_in, w_qkv, 1, 1)
            query = heads_of(((qkv[:, :inner] + q_bias) * score_scale).astype(bf16))
            key = heads_of(qkv[:, inner : 2 * inner].astype(bf16))
            value = heads_of((qkv[:, 2 * inner :] + v_bias).astype(bf16))
            scores = scores_of(query, key)
            peak = jnp.max(scores, axis=-1, keepdims=True)
            exps = jnp.exp(scores - peak)
            total = jnp.sum(exps, axis=-1, keepdims=True)
            probs = (exps / total).astype(bf16)
            log_total = peak + jnp.log(total)
            mixed = jnp.einsum("ihqk,ikhe->iqhe", probs, value, preferred_element_type=f32)
            mixed = mixed.astype(bf16).reshape(all_rows, inner)
            middle = xp + (exchange(dot(mixed, w_out, 1, 0)) + biases[layer, 0])
            hat_two, scale_two = norm_parts(middle)
            second_in = (hat_two * gains[layer, 1] + shifts[layer, 1]).astype(bf16)
            w_up, w_down, u_bias = mlp_weights(layer)
            active, slope = gate_pair(dot(second_in, w_up, 1, 1) + u_bias)
            result = middle + (exchange(dot(active, w_down, 1, 0)) + biases[layer, 1])
            x = result.reshape(images, seq, width)
            kept.append(
                (xp, middle, first_in, query, key, value, log_total, mixed, second_in, active, slope)
                + (w_qkv, w_out, w_up, w_down)
            )
        out = spread_images((x * row_mask).astype(bf16))

        grad_x = (gather_images(cotangent).astype(f32) * row_mask).reshape(all_rows, width)
        weight_grads = [None] * LAYERS
        small = [None] * LAYERS
        prompt_parts = [None] * LAYERS
        for layer in reversed(range(LAYERS)):
            (xp, middle, first_in, query, key, value, log_total, mixed, second_in, active, slope) = kept[
                layer
            ][:11]
            w_qkv, w_out, w_up, w_down = kept[layer][11:]
            bias_mlp = jnp.sum(grad_x, axis=0)
            down_in = grad_x.astype(bf16)
            grad_down = dot(active, down_in, 0, 0).astype(bf16)
            grad_hidden = (dot(down_in, w_down, 1, 1) * slope.astype(f32)).astype(bf16)
            grad_upb = jnp.sum(grad_hidden.astype(f32), axis=0)
            grad_up = dot(grad_hidden, second_in, 0, 0).astype(bf16)
            back = exchange(dot(grad_hidden, w_up, 1, 0))
            hat, scale = norm_parts(middle)
            grad_mid = grad_x + norm_back(hat, scale, gains[layer, 1], back)
            gain_two, shift_two = jnp.sum(back * hat, axis=0), jnp.sum(back, axis=0)
            bias_attn = jnp.sum(grad_mid, axis=0)
            attn_in = grad_mid.astype(bf16)
            grad_out = dot(mixed, attn_in, 0, 0).astype(bf16)
            grad_mixed = heads_of(dot(attn_in, w_out, 1, 1).astype(bf16))
            probs = jnp.exp(scores_of(query, key) - log_total)
            probs_low = probs.astype(bf16)
            grad_value = jnp.einsum(
                "ihqk,iqhe->ikhe", probs_low, grad_mixed, preferred_element_type=f32
            ).astype(bf16)
            grad_probs = jnp.einsum(
                "iqhe,ikhe->ihqk", grad_mixed, value, preferred_element_type=f32
            )
            grad_scores = (
                probs * (grad_probs - jnp.sum(probs * grad_probs, axis=-1, keepdims=True))
            ).astype(bf16)
            grad_query = jnp.einsum(
                "ihqk,ikhe->iqhe", grad_scores, key, preferred_element_type=f32
            ).astype(bf16) * bf16(score_scale)
            grad_key = jnp.einsum(
                "ihqk,iqhe->ikhe", grad_scores, query, preferred_element_type=f32
            ).astype(bf16)
            grad_qkv = jnp.concatenate(
                [g.reshape(all_rows, inner) for g in (grad_query, grad_key, grad_value)], axis=1
            )
            grad_qkvw = dot(grad_qkv, first_in, 0, 0).astype(bf16)
            grad_qb = jnp.sum(grad_qkv[:, :inner].astype(f32), axis=0)
            grad_vb = jnp.sum(grad_qkv[:, 2 * inner :].astype(f32), axis=0)
            back = exchange(dot(grad_qkv, w_qkv, 1, 0))
            hat, scale = norm_parts(xp)
            grad_in = grad_mid + norm_back(hat, scale, gains[layer, 0], back)
            gain_one, shift_one = jnp.sum(back * hat, axis=0), jnp.sum(back, axis=0)
            grad_in = grad_in.reshape(images, seq, width)
            at_prompts = grad_in[:, 1 : 1 + PROMPTS]
            grad_x = jnp.concatenate(
                [grad_in[:, :1], jnp.zeros_like(at_prompts), grad_in[:, 1 + PROMPTS :]], axis=1
            ).reshape(all_rows, width)

            units = jnp.stack([grad_up, grad_down]).reshape(2, planes, tensor_size, unit_q, width)
            units = plane_scatter(units.transpose(1, 2, 0, 3, 4), by_core)
            total = units[0].astype(f32)
            for k in range(1, tensor_size):
                total = total + send(units[k], along(k)).astype(f32)
            units = plane_gather(total.astype(bf16), by_core)
            units = xor_order(units, 0, unit_place, bits).swapaxes(0, 1)
            units = units.reshape(2, half_units, width)
            units = join(units, send(units, other_core), 1).astype(f32)
            full_up, full_down = units[0].T, units[1]

            turned = turned_attn(layer)
            parts = jnp.concatenate([grad_qkvw, grad_out], axis=0)
            parts = parts.reshape(4, 2, heads, planes, dim_q, width).transpose(3, 1, 0, 2, 4, 5)
            parts = plane_scatter(parts, turned)
            near = send(parts[1], lambda p, c, d: (p, c, d ^ (1 + c)))
            far = send(parts[0], lambda p, c, d: (p, c, d ^ 3) if c else None)
            total = jnp.where(first_core, parts[0], far).astype(f32) + near.astype(f32)
            total = total.astype(bf16)
            theirs = jnp.where(first_core, total[2:], total[:2])
            mine = jnp.where(first_core, total[:2], total[2:])
            mine = (mine.astype(f32) + send(theirs, other_core).astype(f32)).astype(bf16)
            parts = plane_gather(mine, turned)
            parts = xor_order(parts, 0, attn_place(layer), bits).transpose(1, 2, 0, 3, 4)
            parts = parts.reshape(2, heads, HEAD_DIM, width)
            parts = join(parts, send(parts, other_core), 0).astype(f32)
            full_qkv = parts[:3].swapaxes(0, 1).reshape(heads * 3 * HEAD_DIM, width).T
            full_out = parts[3].reshape(heads * HEAD_DIM, width)
            weight_grads[layer] = (full_qkv, full_out, full_up, full_down)

            norms = jnp.stack([gain_one, gain_two, shift_one, shift_two, bias_attn, bias_mlp])
            norms = 0.5 * norms.reshape(6, tensor_size, width // tensor_size)
            upb = grad_upb.reshape(planes, tensor_size, unit_q)
            upb = xor_order(xor_order(upb, 0, unit_place, bits), 1, z, zbits).swapaxes(0, 1)
            upb = upb.reshape(tensor_size, half_units)
            upb = join(upb, jnp.zeros_like(upb), 1)
            pair = jnp.stack([grad_qb, grad_vb]).reshape(2, 2, heads, planes, dim_q)
            pair = xor_order(pair, 3, attn_place(layer), bits).transpose(1, 2, 0, 3, 4)
            pair = pair.reshape(2, heads * 2 * HEAD_DIM)
            pair = join(pair, jnp.zeros_like(pair), 0)
            pair = jnp.where(
                first_core, pair, jnp.concatenate([pair[:2], jnp.flip(pair[2:], 0)], axis=0)
            )
            pair = xor_order(pair, 0, z, zbits)
            block = width // tensor_size
            small[layer] = jnp.concatenate(
                [
                    norms,
                    upb.reshape(tensor_size, -1, block).swapaxes(0, 1),
                    pair.reshape(tensor_size, -1, block).swapaxes(0, 1),
                ],
                axis=0,
            )
            owner = (plane ^ jnp.arange(planes)) * 2 + core
            task_list = owner[:, None] * per_dev + jnp.arange(per_dev)[None, :]
            hot = (task_list[:, :, None] == tasks[None, None, :, layer]).astype(f32)
            picked = sum(
                hot[:, :, i, None, None] * at_prompts[i][None, None] for i in range(images)
            )
            prompt_parts[layer] = picked.reshape(planes, per_dev * PROMPTS, tensor_size, block)

        grad_tokens = spread_images(grad_x.reshape(images, seq, width).astype(bf16))

        small_all = jnp.concatenate(small, axis=0)
        small_rows = small_all.shape[0]
        small_all = exchange(small_all)
        wanted = jnp.concatenate(prompt_parts, axis=1).astype(bf16)
        for step in range(bits):
            pairs = wanted.reshape((wanted.shape[0] // 2, 2) + wanted.shape[1:])
            flat = pairs[:, 1].reshape(-1, tensor_size, block)
            got = send(
                jnp.concatenate([flat, small_all.astype(bf16)], axis=0), flip(step, lambda c: 0)
            )
            small_all = small_all.astype(bf16).astype(f32) + got[-small_rows:].astype(f32)
            wanted = (
                pairs[:, 0].astype(f32) + got[:-small_rows].reshape(pairs[:, 0].shape).astype(f32)
            ).astype(bf16)
        tail = jnp.concatenate([wanted[0].astype(f32), small_all], axis=0)
        tail = xor_order(tail, 1, z, zbits)
        for step in reversed(range(zbits)):
            size = 1 << step
            got = send(tail[:, size:].astype(bf16), along(size))
            tail = tail[:, :size] + got.astype(f32)
        tail = tail[:, 0]
        prompt_rows = LAYERS * per_dev * PROMPTS
        grad_prompts = tail[:prompt_rows].reshape(LAYERS, per_dev, PROMPTS, block)
        sums = tail[prompt_rows:].reshape(LAYERS, -1, block)
        up_rows = hidden // block
        grad_upb = sums[:, 6 : 6 + up_rows].reshape(LAYERS, hidden)
        grad_pair = sums[:, 6 + up_rows :].reshape(LAYERS, heads * 2 * HEAD_DIM)
        full_qkv, full_out, full_up, full_down = (
            jnp.stack(both) for both in zip(*weight_grads)
        )
        return (
            out,
            grad_tokens,
            grad_prompts,
            sums[:, 0:2],
            sums[:, 2:4],
            full_qkv,
            grad_pair,
            full_out,
            sums[:, 4:6],
            full_up,
            grad_upb,
            full_down,
        )

    return per_device


def solution(mesh):
    placed = (
        P("dp", "tensor", None),
        P("dp", "tensor", None),
        P("dp", None),
        P("dp", None),
        P(),
        P(),
        P(),
        P(None, None, "tensor"),
        P(None, "tensor"),
        P(None, "tensor", None),
        P(),
        P(None, None, "tensor"),
        P(None, "tensor"),
        P(None, "tensor", None),
    )
    return jax.shard_map(
        build(mesh.shape["dp"], mesh.shape["tensor"]),
        mesh=mesh,
        in_specs=placed,
        out_specs=(
            P("dp", "tensor", None),
            P("dp", "tensor", None),
            P(None, "dp", None, "tensor"),
            P(None, None, "tensor"),
            P(None, None, "tensor"),
            P(None, None, "tensor"),
            P(None, "tensor"),
            P(None, "tensor", None),
            P(None, None, "tensor"),
            P(None, None, "tensor"),
            P(None, "tensor"),
            P(None, "tensor", None),
        ),
        check_vma=False,
    )
```

```python
import functools

import jax
import jax.numpy as jnp
from jax import lax
from jax.experimental import pallas as pl
from jax.experimental.pallas import tpu as pltpu
from jax.sharding import PartitionSpec as P

HEAD_DIM = 64
LAYERS = 2
PROMPTS = 50
QUARTERS = 4
PAD = 16
AXES = ("dp", "tensor")
epsilon = 1e-06
bf16 = jnp.bfloat16
f32 = jnp.float32
ANY = pl.BlockSpec(memory_space=pl.ANY)
SMEM = pl.BlockSpec(memory_space=pltpu.SMEM)
NEGATIVE = -1000000000.0


def nn(left, right):
    return lax.dot_general(left, right, (((1,), (0,)), ((), ())), preferred_element_type=f32)


def nt(left, right):
    return lax.dot_general(left, right, (((1,), (1,)), ((), ())), preferred_element_type=f32)


def turn(arr):
    return arr.astype(f32).T.astype(bf16)


def norm_parts(rows):
    centre = rows - jnp.mean(rows, axis=-1, keepdims=True)
    spread = jnp.mean(centre * centre, axis=-1, keepdims=True)
    scale = lax.rsqrt(spread + epsilon)
    return centre * scale, scale


def norm_back(hat, scale, gain, grad):
    inner = grad * gain
    along = jnp.mean(inner * hat, axis=-1, keepdims=True)
    return scale * (inner - jnp.mean(inner, axis=-1, keepdims=True) - hat * along)


def gate_pair(pre):
    size = jnp.abs(pre)
    t = 1.0 / (1.0 + 0.2316418882 * size)
    bell = jnp.exp(-0.5 * pre * pre)
    poly = 0.5307027145 * t - 0.7265760135
    poly = poly * t + 0.7107068705
    poly = poly * t - 0.142248368
    poly = poly * t + 0.127414796
    rest = poly * t * bell
    below = jnp.where(pre >= 0.0, 1.0 - rest, rest)
    return pre * below, below + pre * bell * 0.3989422804014327


def cost(flops, size, trans=0):
    return pl.CostEstimate(flops=flops, bytes_accessed=size, transcendentals=trans)


def params(mib):
    return pltpu.CompilerParams(vmem_limit_bytes=mib << 20)


def fetch(copies, sems, first=0):
    made = [pltpu.make_async_copy(src, dst, sems.at[first + i]) for i, (src, dst) in enumerate(copies)]
    for copy in made:
        copy.start()
    for copy in made:
        copy.wait()


def rows16(start, size):
    return pl.ds(pl.multiple_of(start, 16), size)


def attn_fetch(info, own_qkv, own_out, near, far, w_qkv, w_out, sems):
    rows_in, rows_out = own_qkv.shape[0], own_out.shape[0]
    part_in, part_out = rows_in // QUARTERS, rows_out // QUARTERS

    def pieces(bufs, block):
        copies = []
        for i in range(QUARTERS):
            quarter = info[2 + i]
            src = bufs[i]
            copies.append(
                (
                    src.at[pl.ds(0, part_in)],
                    w_qkv.at[rows16(block * rows_in + part_in * quarter, part_in)],
                )
            )
            copies.append(
                (
                    src.at[pl.ds(part_in, part_out)],
                    w_out.at[rows16(block * rows_out + part_out * quarter, part_out)],
                )
            )
        return copies

    @pl.when(info[0] == 0)
    def _():
        own = [
            (own_qkv, w_qkv.at[pl.ds(0, rows_in)]),
            (own_out, w_out.at[pl.ds(0, rows_out)]),
        ]
        fetch(own + pieces(near, 1), sems)

    @pl.when(info[0] != 0)
    def _():
        fetch(pieces(far, 0) + pieces(near, 1), sems)


def mlp_fetch(info, own_up, own_down, bufs, w_up, w_down, sems):
    width = own_up.shape[0]
    half = own_up.shape[1] // 2
    wide, tall = width // QUARTERS, half // QUARTERS
    split = width // 2
    start = info[0] * half
    copies = [
        (own_up.at[:, pl.ds(pl.multiple_of(start, 128), half)], w_up.at[:, pl.ds(0, half)]),
        (own_down.at[rows16(start, half)], w_down.at[pl.ds(0, half)]),
    ]
    for i in range(QUARTERS):
        quarter = info[2 + i]
        for k in range(bufs[i].shape[0]):
            src = bufs[i].at[k]
            units = rows16((k + 1) * half + tall * quarter, tall)
            copies.append(
                (
                    src.at[pl.ds(0, wide)],
                    w_up.at[rows16(wide * quarter, wide), pl.ds((k + 1) * half, half)],
                )
            )
            copies.append((src.at[pl.ds(wide, tall)], w_down.at[units, pl.ds(0, split)]))
            copies.append((src.at[pl.ds(wide + tall, tall)], w_down.at[units, pl.ds(split, split)]))
    fetch(copies, sems)


def head_masks(rows, cols, axis):
    place = lax.broadcasted_iota(jnp.int32, (rows, cols), axis)
    return place < HEAD_DIM


def attn_forward_kernel(later, info, *refs):
    if later:
        x_ref, own_ref, oth_ref = refs[:3]
        refs = refs[3:]
    else:
        x_ref = refs[0]
        refs = refs[1:]
    placed_ref, vec_ref, row_ref, own_qkv, own_out = refs[:5]
    near, far = refs[5:9], refs[9:13]
    xp_ref, a_ref, qkv_ref, mix_ref, lse_ref, part_ref = refs[13:19]
    w_qkv, w_out, sems = refs[19:]
    step = pl.program_id(0)

    @pl.when(step == 0)
    def _():
        attn_fetch(info, own_qkv, own_out, near, far, w_qkv, w_out, sems)

    rows = x_ref[0].astype(f32)
    if later:
        rows = rows + (own_ref[0].astype(f32) + oth_ref[0].astype(f32) + vec_ref[2:3, :])
    top = placed_ref.shape[1]
    place = lax.broadcasted_iota(jnp.int32, (top, rows.shape[1]), 0)
    here = (place >= 1) & (place <= PROMPTS)
    rows = jnp.concatenate(
        [jnp.where(here, placed_ref[0].astype(f32), rows[:top]), rows[top:]], axis=0
    )
    xp_ref[0] = rows
    hat, _ = norm_parts(rows)
    normed = (hat * vec_ref[0:1, :] + vec_ref[1:2, :]).astype(bf16)
    a_ref[0] = normed
    qkv = (nt(normed, w_qkv[...]) + row_ref[0:1, :]) * row_ref[1:2, :]
    seq = rows.shape[0]
    low = head_masks(seq, 128, 1)
    low_t = head_masks(128, seq, 0)
    count = info[6 + step]
    valid = lax.broadcasted_iota(jnp.int32, (seq, seq), 0) < count
    pairs = w_out.shape[0] // 128
    for p in range(pairs):
        blocks = [qkv[:, 384 * p + 128 * j : 384 * p + 128 * (j + 1)] for j in range(3)]
        query = jnp.where(low, blocks[0], blocks[1]).astype(bf16)
        key = pltpu.roll(jnp.where(low, blocks[2], blocks[0]), HEAD_DIM, 1).astype(bf16)
        value_t = jnp.where(low, blocks[1], blocks[2])
        qkv_ref[0, :, 384 * p : 384 * p + 128] = query
        qkv_ref[0, :, 384 * p + 128 : 384 * p + 256] = key
        qkv_ref[0, :, 384 * p + 256 : 384 * p + 384] = value_t.astype(bf16)
        value_t = value_t.T.astype(bf16)
        outs = []
        for h in range(2):
            mine = low if h == 0 else jnp.logical_not(low)
            one_key = jnp.where(mine, key, jnp.zeros_like(key))
            scores = jnp.where(valid, nt(one_key, query), NEGATIVE)
            peak = jnp.max(scores, axis=0, keepdims=True)
            exps = jnp.exp(scores - peak)
            total = jnp.sum(exps, axis=0, keepdims=True)
            lse_ref[0, 2 * p + h : 2 * p + h + 1, :] = peak + jnp.log(total)
            outs.append(nn(value_t, exps.astype(bf16)) * (1.0 / total))
        mixed = jnp.where(low_t, outs[0], outs[1]).T.astype(bf16)
        mix_ref[0, :, 128 * p : 128 * (p + 1)] = mixed
    part_ref[0] = nn(mix_ref[0], w_out[...]).astype(bf16)


def mlp_forward_kernel(info, xp_ref, own_ref, oth_ref, vec_ref, bias_ref, own_up, own_down, *refs):
    bufs = refs[:4]
    xm_ref, c_ref, act_ref, slope_ref, part_ref = refs[4:9]
    w_up, w_down, sems = refs[9:]

    @pl.when(pl.program_id(0) == 0)
    def _():
        mlp_fetch(info, own_up, own_down, bufs, w_up, w_down, sems)

    rows = xp_ref[0] + (own_ref[0].astype(f32) + oth_ref[0].astype(f32) + vec_ref[2:3, :])
    xm_ref[0] = rows
    hat, _ = norm_parts(rows)
    normed = (hat * vec_ref[0:1, :] + vec_ref[1:2, :]).astype(bf16)
    c_ref[0] = normed
    units = w_up.shape[1]
    for at in range(0, units, 384):
        pre = nn(normed, w_up[:, at : at + 384]) + bias_ref[:, at : at + 384]
        act, slope = gate_pair(pre)
        act_ref[0, :, at : at + 384] = act.astype(bf16)
        slope_ref[0, :, at : at + 384] = slope.astype(bf16)
    part_ref[0] = nn(act_ref[0], w_down[...]).astype(bf16)


def mlp_backward_kernel(masked, info, dx_ref, slope_ref, own_up, own_down, *refs):
    bufs = refs[:4]
    dz_ref, dh_ref, part_ref, sum_ref, upb_ref = refs[4:9]
    w_up, w_down, sems = refs[9:]
    step = pl.program_id(0)

    @pl.when(step == 0)
    def _():
        mlp_fetch(info, own_up, own_down, bufs, w_up, w_down, sems)
        sum_ref[...] = jnp.zeros_like(sum_ref)
        upb_ref[...] = jnp.zeros_like(upb_ref)

    grad = dx_ref[0].astype(f32)
    if masked:
        place = lax.broadcasted_iota(jnp.int32, grad.shape, 0)
        grad = jnp.where(place < info[6 + step], grad, 0.0)
    sum_ref[0:1, :] += jnp.sum(grad, axis=0, keepdims=True)
    low = grad.astype(bf16)
    dz_ref[0] = low
    units = w_up.shape[1]
    for at in range(0, units, 384):
        hidden = nt(low, w_down[at : at + 384, :]) * slope_ref[0, :, at : at + 384].astype(f32)
        hidden = hidden.astype(bf16)
        dh_ref[0, :, at : at + 384] = hidden
        upb_ref[0:1, at : at + 384] += jnp.sum(hidden.astype(f32), axis=0, keepdims=True)
    part_ref[0] = nt(dh_ref[0], w_up[...]).astype(bf16)


def mlp_weight_kernel(info, c_ref, dz_ref, act_ref, dh_ref, s1_ref, s2_ref, keep_ref, c_t, up, down):
    @pl.when(pl.program_id(0) == 0)
    def _():
        c_t[...] = turn(c_ref[...])

    up[...] = nn(c_t[...], dh_ref[...]).astype(bf16)
    down[...] = nn(turn(act_ref[...]), dz_ref[...]).astype(bf16)
    wide, tall = up.shape[0] // QUARTERS, down.shape[0] // QUARTERS
    split = down.shape[1] // 2
    for i, out in enumerate((keep_ref.at[0], s1_ref.at[0, 0], s2_ref.at[0], s1_ref.at[1, 0])):
        quarter = info[2 + i]
        out[0:wide, :] = up[rows16(wide * quarter, wide), :]
        rows = down[rows16(tall * quarter, tall), :]
        out[wide : wide + tall, :] = rows[:, :split]
        out[wide + tall :, :] = rows[:, split:]


def attn_backward_kernel(info, dx_ref, own_ref, oth_ref, xm_ref, vec_ref, qkv_ref, lse_ref, *refs):
    own_qkv, own_out = refs[:2]
    near, far = refs[2:6], refs[6:10]
    mid_ref, dy_ref, dqkv_ref, part_ref, sum_ref, pair_ref = refs[10:16]
    w_qkv, w_out, sems = refs[16:]
    step = pl.program_id(0)

    @pl.when(step == 0)
    def _():
        attn_fetch(info, own_qkv, own_out, near, far, w_qkv, w_out, sems)
        sum_ref[...] = jnp.zeros_like(sum_ref)
        pair_ref[...] = jnp.zeros_like(pair_ref)

    back = own_ref[0].astype(f32) + oth_ref[0].astype(f32)
    hat, scale = norm_parts(xm_ref[0])
    grad = dx_ref[0].astype(f32) + norm_back(hat, scale, vec_ref[0:1, :], back)
    mid_ref[0] = grad
    sum_ref[0:1, :] += jnp.sum(back * hat, axis=0, keepdims=True)
    sum_ref[1:2, :] += jnp.sum(back, axis=0, keepdims=True)
    sum_ref[2:3, :] += jnp.sum(grad, axis=0, keepdims=True)
    low_grad = grad.astype(bf16)
    dy_ref[0] = low_grad
    seq = grad.shape[0]
    d_mixed = nt(low_grad, w_out[...]).astype(bf16)
    low = head_masks(seq, 128, 1)
    low_t = head_masks(128, seq, 0)
    valid = lax.broadcasted_iota(jnp.int32, (seq, seq), 0) < info[6 + step]
    pairs = w_out.shape[0] // 128
    for p in range(pairs):
        query = qkv_ref[0, :, 384 * p : 384 * p + 128]
        key = qkv_ref[0, :, 384 * p + 128 : 384 * p + 256]
        value = qkv_ref[0, :, 384 * p + 256 : 384 * p + 384]
        grad_o = d_mixed[:, 128 * p : 128 * (p + 1)]
        key_t = turn(key)
        d_query, d_key, d_value = [], [], []
        for h in range(2):
            mine = low if h == 0 else jnp.logical_not(low)
            none = jnp.zeros_like(key)
            scores = jnp.where(valid, nt(jnp.where(mine, key, none), query), NEGATIVE)
            probs = jnp.exp(scores - lse_ref[0, 2 * p + h : 2 * p + h + 1, :])
            d_probs = nt(jnp.where(mine, value, none), grad_o)
            along = jnp.sum(probs * d_probs, axis=0, keepdims=True)
            d_scores = (probs * (d_probs - along)).astype(bf16)
            d_value.append(nn(probs.astype(bf16), grad_o))
            d_key.append(nn(d_scores, query))
            d_query.append(nn(key_t, d_scores))
        d_query = jnp.where(low_t, d_query[0], d_query[1]).T * (HEAD_DIM**-0.5)
        d_key = pltpu.roll(jnp.where(low, d_key[0], d_key[1]), HEAD_DIM, 1)
        d_value = jnp.where(low, d_value[0], d_value[1])
        for j, block in enumerate(
            (
                jnp.where(low, d_query, d_key),
                jnp.where(low, d_value, d_query),
                jnp.where(low, d_key, d_value),
            )
        ):
            block = block.astype(bf16)
            at = 384 * p + 128 * j
            dqkv_ref[0, :, at : at + 128] = block
            pair_ref[0:1, at : at + 128] += jnp.sum(block.astype(f32), axis=0, keepdims=True)
    part_ref[0] = nn(dqkv_ref[0], w_qkv[...]).astype(bf16)


def attn_weight_kernel(info, a_ref, dqkv_ref, dy_ref, mix_ref, s1_ref, s2_ref, keep_ref, w_in, w_out):
    for at in range(0, w_in.shape[0], 384):
        w_in[at : at + 384, :] = nn(turn(dqkv_ref[:, at : at + 384]), a_ref[...]).astype(bf16)
    w_out[...] = nn(turn(mix_ref[...]), dy_ref[...]).astype(bf16)
    rows_in, rows_out = w_in.shape[0] // 2, w_out.shape[0] // 2
    part_in, part_out = rows_in // QUARTERS, rows_out // QUARTERS
    for i, out in enumerate((keep_ref, s1_ref.at[0], s2_ref, s1_ref.at[1])):
        quarter = info[2 + i]
        for b in range(2):
            out[b, 0:part_in, :] = w_in[rows16(b * rows_in + part_in * quarter, part_in), :]
            out[b, part_in:, :] = w_out[rows16(b * rows_out + part_out * quarter, part_out), :]


def norm_backward_kernel(last, mid_ref, own_ref, oth_ref, xp_ref, vec_ref, dx_ref, at_ref, sum_ref):
    @pl.when(pl.program_id(0) == 0)
    def _():
        sum_ref[...] = jnp.zeros_like(sum_ref)

    back = own_ref[0].astype(f32) + oth_ref[0].astype(f32)
    hat, scale = norm_parts(xp_ref[0])
    grad = mid_ref[0] + norm_back(hat, scale, vec_ref[0:1, :], back)
    sum_ref[0:1, :] += jnp.sum(back * hat, axis=0, keepdims=True)
    sum_ref[1:2, :] += jnp.sum(back, axis=0, keepdims=True)
    top = at_ref.shape[1]
    place = lax.broadcasted_iota(jnp.int32, (top, grad.shape[1]), 0)
    here = (place >= 1) & (place <= PROMPTS)
    at_ref[0] = grad[:top]
    dx_ref[0, 0:top, :] = jnp.where(here, 0.0, grad[:top]).astype(dx_ref.dtype)
    dx_ref[0, top:, :] = grad[top:].astype(dx_ref.dtype)


def reversed_bits(value, bits):
    return sum(((value >> b) & 1) << (bits - 1 - b) for b in range(bits))


def xor_order(arr, axis, index, bits):
    for b in range(bits):
        shape = arr.shape
        split = shape[:axis] + (shape[axis] >> (b + 1), 2, 1 << b) + shape[axis + 1 :]
        parts = arr.reshape(split)
        arr = jnp.where(((index >> b) & 1) == 1, jnp.flip(parts, axis + 1), parts).reshape(shape)
    return arr


def build(dp_size, tensor_size):
    planes = dp_size // 2
    bits = planes.bit_length() - 1
    zbits = tensor_size.bit_length() - 1

    def send(arr, target):
        pairs = []
        for dp in range(dp_size):
            for z in range(tensor_size):
                to = target(dp >> 1, dp & 1, z)
                if to is not None:
                    plane, core, depth = to
                    pairs.append((dp * tensor_size + z, (plane * 2 + core) * tensor_size + depth))
        return lax.ppermute(arr, AXES, pairs)

    def other_core(p, c, z):
        return p, 1 - c, z

    def along(k):
        return lambda p, c, z: (p, c, z ^ k)

    def across(bit):
        return lambda p, c, z: (p ^ (1 << bit), c, z)

    def flip(step, only=None):
        def target(p, c, z):
            if only is not None and c != only:
                return None
            return p ^ (1 << ((1 - step) if c else step)), c, z

        return target

    def near_of(p, c, z):
        return p, c, z ^ (1 + c)

    def far_of(p, c, z):
        return (p, c, z ^ 3) if c else None

    def plane_gather(piece, only=None):
        one = send(piece, flip(0, only))
        two = send(piece, flip(1, only))
        return [piece, one, two, send(one, flip(1, only))]

    def plane_reduce(s1, s2, keep):
        got = send(s1, flip(0))
        two = (s2.astype(f32) + got[1].astype(f32)).astype(bf16)
        last = send(two, flip(1))
        return keep.astype(f32) + got[0].astype(f32) + last.astype(f32)

    def per_device(
        tokens,
        cotangent,
        task_ids,
        key_mask,
        prompts,
        norm_gain,
        norm_bias,
        qkv_weight,
        qv_bias,
        out_weight,
        branch_bias,
        up_weight,
        up_bias,
        down_weight,
    ):
        group, rows_local, width = tokens.shape
        images = group // 2
        seq = rows_local * tensor_size
        in_rows = qkv_weight.shape[2]
        heads = in_rows // (3 * HEAD_DIM)
        out_rows = heads * HEAD_DIM
        inner = 2 * out_rows
        hidden = up_weight.shape[2]
        half_units = hidden // 2
        units = half_units * tensor_size
        wide, tall = width // QUARTERS, half_units // QUARTERS
        task_count = prompts.shape[1]
        per_dev = task_count // dp_size
        place = lax.axis_index("dp")
        z = lax.axis_index("tensor")
        core = place & 1
        plane = place >> 1
        quarter = plane & 3
        first_core = core == 0
        odd = z & 1
        all_rows = images * seq
        top = 64

        def pick(arr, index, axis):
            return lax.dynamic_index_in_dim(arr, index, axis, keepdims=False)

        def cut(arr, start, size, axis):
            return lax.dynamic_slice_in_dim(arr, start, size, axis)

        def join(mine, theirs, axis):
            return jnp.where(
                first_core,
                jnp.concatenate([mine, theirs], axis),
                jnp.concatenate([theirs, mine], axis),
            )

        def gather_images(arr):
            one = cut(arr, odd * images, images, 0)
            two = cut(arr, (1 - odd) * images, images, 0)
            got_one = send(one, lambda p, c, d: (p, d >> 1, 2 * c + (d & 1)))
            got_two = send(two, lambda p, c, d: (p, d >> 1, 2 * c + 1 - (d & 1)))
            half = jnp.where(
                odd == 0,
                jnp.concatenate([got_one, got_two], 1),
                jnp.concatenate([got_two, got_one], 1),
            )
            return join(half, send(half, other_core), 1)

        def spread_images(rows_of):
            one = rows_of(rows_local * (2 * core + odd))
            two = rows_of(rows_local * (2 * core + 1 - odd))
            got_one = send(one, lambda p, c, d: (p, d >> 1, 2 * c + (d & 1)))
            got_two = send(two, lambda p, c, d: (p, d >> 1, 2 * c + 1 - (d & 1)))
            return jnp.where(
                odd == 0,
                jnp.concatenate([got_one, got_two], 0),
                jnp.concatenate([got_two, got_one], 0),
            )

        facts = jnp.concatenate([jnp.sum(key_mask, axis=1, keepdims=True), task_ids], axis=1)
        facts = cut(facts, odd * images, images, 0)
        facts = jnp.where(core == (z >> 1), facts, send(facts, other_core))
        counts, tasks = facts[:, 0], facts[:, 1:]
        ranks = [
            quarter ^ jnp.where(first_core, r, reversed_bits(r, 2)) for r in range(QUARTERS)
        ]
        info = jnp.concatenate(
            [jnp.stack([core, z] + ranks), counts, jnp.zeros((16 - 6 - images,), jnp.int32)]
        ).astype(jnp.int32)

        gains = norm_gain.astype(f32)
        shifts = norm_bias.astype(f32)
        biases = branch_bias.astype(f32)

        def vec(*vectors):
            return jnp.pad(jnp.stack(vectors), ((0, 8 - len(vectors)), (0, 0)))

        own_qkv = [qkv_weight[layer].T for layer in range(LAYERS)]

        def attn_gather(layer):
            bias = jnp.pad(qv_bias[layer][None], ((0, PAD - 1), (0, width - qv_bias.shape[1])))
            piece = jnp.concatenate(
                [
                    cut(own_qkv[layer], quarter * (in_rows // 4), in_rows // 4, 0),
                    cut(out_weight[layer], quarter * (out_rows // 4), out_rows // 4, 0),
                    bias,
                ],
                axis=0,
            )
            near = plane_gather(send(piece, near_of))
            far = plane_gather(send(piece, far_of), only=1)
            size = qv_bias.shape[1]
            last = in_rows // 4 + out_rows // 4
            near_bias = near[0][last, :size]
            first_bias = jnp.where(first_core, qv_bias[layer], far[0][last, :size])
            pair = jnp.stack([first_bias, near_bias]).astype(f32)
            pair = pair.reshape(2 * heads, 2, HEAD_DIM)
            pair = jnp.stack([pair[:, 0], jnp.zeros_like(pair[:, 0]), pair[:, 1]], axis=1)
            scale = jnp.broadcast_to(
                jnp.array([HEAD_DIM**-0.5, 1.0, 1.0], f32)[None, :, None], pair.shape
            )
            rows = vec(pair.reshape(-1), scale.reshape(-1))
            return near, far, rows

        def mlp_gather(layer):
            bias = jnp.pad(up_bias[layer].reshape(2, half_units), ((0, PAD - 2), (0, 0)))
            mine = cut(down_weight[layer], core * half_units + quarter * tall, tall, 0)
            piece = jnp.concatenate(
                [
                    cut(
                        cut(up_weight[layer], quarter * wide, wide, 0),
                        core * half_units,
                        half_units,
                        1,
                    ),
                    mine[:, : width // 2],
                    mine[:, width // 2 :],
                    bias,
                ],
                axis=0,
            )
            got = [send(piece, along(k)) for k in range(1, tensor_size)]
            size = wide + 2 * tall
            bufs = plane_gather(jnp.stack([g[:size] for g in got]))
            rows = [pick(up_bias[layer].reshape(2, half_units), core, 0)]
            rows += [pick(g[size : size + 2], core, 0) for g in got]
            return bufs, jnp.concatenate(rows)[None].astype(f32)

        def image_block(size):
            return pl.BlockSpec((1, seq, size), lambda i: (i, 0, 0))

        def fixed(*shape):
            return pl.BlockSpec(shape, lambda i: (0,) * len(shape))

        def out_of(*shape, dtype=bf16):
            return jax.ShapeDtypeStruct(shape, dtype)

        rows_w, rows_w32 = out_of(images, seq, width), out_of(images, seq, width, dtype=f32)
        wide_block = image_block(width)
        attn_scratch = [
            pltpu.VMEM((2 * in_rows, width), bf16),
            pltpu.VMEM((inner, width), bf16),
            pltpu.SemaphoreType.DMA((16,)),
        ]
        mlp_scratch = [
            pltpu.VMEM((width, units), bf16),
            pltpu.VMEM((units, width), bf16),
            pltpu.SemaphoreType.DMA((2 + 12 * (tensor_size - 1),)),
        ]
        mm = 2 * all_rows * width
        heads_flops = 2 * images * 2 * heads * seq * seq * 128

        def attn_forward(layer, x, placed, vecs, rows, near, far):
            later = len(x) > 1
            return pl.pallas_call(
                functools.partial(attn_forward_kernel, later),
                grid=(images,),
                in_specs=[SMEM]
                + [wide_block] * len(x)
                + [pl.BlockSpec((1, top, width), lambda i: (i, 0, 0))]
                + [fixed(8, width), fixed(8, 2 * in_rows)]
                + [ANY] * 10,
                out_specs=[
                    wide_block,
                    wide_block,
                    image_block(2 * in_rows),
                    image_block(inner),
                    pl.BlockSpec((1, 8, seq), lambda i: (i, 0, 0)),
                    wide_block,
                ],
                out_shape=[
                    rows_w32,
                    rows_w,
                    out_of(images, seq, 2 * in_rows),
                    out_of(images, seq, inner),
                    out_of(images, 8, seq, dtype=f32),
                    rows_w,
                ],
                scratch_shapes=attn_scratch,
                compiler_params=params(40),
                cost_estimate=cost(mm * (3 * inner + inner) + 2 * heads_flops, 12 << 20, 1 << 20),
                name="attn_forward",
            )(info, *x, placed, vecs, rows, own_qkv[layer], out_weight[layer], *near, *far)

        def mlp_forward(layer, xp, own, oth, vecs, bias, bufs):
            return pl.pallas_call(
                mlp_forward_kernel,
                grid=(images,),
                in_specs=[SMEM]
                + [wide_block] * 3
                + [fixed(8, width), fixed(1, units)]
                + [ANY] * 6,
                out_specs=[wide_block, wide_block, image_block(units), image_block(units), wide_block],
                out_shape=[
                    rows_w32,
                    rows_w,
                    out_of(images, seq, units),
                    out_of(images, seq, units),
                    rows_w,
                ],
                scratch_shapes=mlp_scratch,
                compiler_params=params(48),
                cost_estimate=cost(mm * 2 * units, 18 << 20, 1 << 20),
                name="mlp_forward",
            )(info, xp, own, oth, vecs, bias, up_weight[layer], down_weight[layer], *bufs)

        def mlp_backward(layer, dx, slope, bufs):
            return pl.pallas_call(
                functools.partial(mlp_backward_kernel, dx.dtype == bf16),
                grid=(images,),
                in_specs=[SMEM, wide_block, image_block(units)] + [ANY] * 6,
                out_specs=[
                    wide_block,
                    image_block(units),
                    wide_block,
                    fixed(8, width),
                    fixed(8, units),
                ],
                out_shape=[
                    rows_w,
                    out_of(images, seq, units),
                    rows_w,
                    out_of(8, width, dtype=f32),
                    out_of(8, units, dtype=f32),
                ],
                scratch_shapes=mlp_scratch,
                compiler_params=params(48),
                cost_estimate=cost(mm * 2 * units, 16 << 20),
                name="mlp_backward",
            )(info, dx, slope, up_weight[layer], down_weight[layer], *bufs)

        piece_rows = wide + 2 * tall

        def mlp_weights(c, dz, act, dh):
            flat = lambda arr: arr.reshape(all_rows, arr.shape[2])
            by_shard = pl.BlockSpec((all_rows, half_units), lambda k: (0, k))
            return pl.pallas_call(
                mlp_weight_kernel,
                grid=(tensor_size,),
                in_specs=[SMEM, fixed(all_rows, width), fixed(all_rows, width), by_shard, by_shard],
                out_specs=[
                    pl.BlockSpec((2, 1, piece_rows, half_units), lambda k: (0, k, 0, 0)),
                    pl.BlockSpec((1, piece_rows, half_units), lambda k: (k, 0, 0)),
                    pl.BlockSpec((1, piece_rows, half_units), lambda k: (k, 0, 0)),
                ],
                out_shape=[
                    out_of(2, tensor_size, piece_rows, half_units),
                    out_of(tensor_size, piece_rows, half_units),
                    out_of(tensor_size, piece_rows, half_units),
                ],
                scratch_shapes=[
                    pltpu.VMEM((width, all_rows), bf16),
                    pltpu.VMEM((width, half_units), bf16),
                    pltpu.VMEM((half_units, width), bf16),
                ],
                compiler_params=params(40),
                cost_estimate=cost(mm * 2 * units, 14 << 20),
                name="mlp_weights",
            )(info, flat(c), flat(dz), flat(act), flat(dh))

        def attn_backward(layer, dx, own, oth, xm, vecs, qkv, lse, near, far):
            return pl.pallas_call(
                attn_backward_kernel,
                grid=(images,),
                in_specs=[SMEM]
                + [wide_block] * 4
                + [fixed(8, width), image_block(2 * in_rows)]
                + [pl.BlockSpec((1, 8, seq), lambda i: (i, 0, 0))]
                + [ANY] * 10,
                out_specs=[
                    wide_block,
                    wide_block,
                    image_block(2 * in_rows),
                    wide_block,
                    fixed(8, width),
                    fixed(8, 2 * in_rows),
                ],
                out_shape=[
                    rows_w32,
                    rows_w,
                    out_of(images, seq, 2 * in_rows),
                    rows_w,
                    out_of(8, width, dtype=f32),
                    out_of(8, 2 * in_rows, dtype=f32),
                ],
                scratch_shapes=attn_scratch,
                compiler_params=params(40),
                cost_estimate=cost(mm * (3 * inner + inner) + 5 * heads_flops, 15 << 20, 1 << 20),
                name="attn_backward",
            )(
                info, dx, own, oth, xm, vecs, qkv, lse,
                own_qkv[layer], out_weight[layer], *near, *far,
            )

        attn_rows = in_rows // 4 + out_rows // 4

        def attn_weights(a, dqkv, dy, mixed):
            flat = lambda arr: arr.reshape(all_rows, arr.shape[2])
            whole = pl.BlockSpec(memory_space=pltpu.VMEM)
            return pl.pallas_call(
                attn_weight_kernel,
                in_specs=[SMEM] + [whole] * 4,
                out_specs=[whole] * 3,
                out_shape=[
                    out_of(2, 2, attn_rows, width),
                    out_of(2, attn_rows, width),
                    out_of(2, attn_rows, width),
                ],
                scratch_shapes=[
                    pltpu.VMEM((2 * in_rows, width), bf16),
                    pltpu.VMEM((inner, width), bf16),
                ],
                compiler_params=params(40),
                cost_estimate=cost(mm * (3 * inner + inner), 10 << 20),
                name="attn_weights",
            )(info, flat(a), flat(dqkv), flat(dy), flat(mixed))

        def norm_backward(last, mid, own, oth, xp, vecs):
            return pl.pallas_call(
                functools.partial(norm_backward_kernel, last),
                grid=(images,),
                in_specs=[wide_block] * 4 + [fixed(8, width)],
                out_specs=[
                    wide_block,
                    pl.BlockSpec((1, top, width), lambda i: (i, 0, 0)),
                    fixed(8, width),
                ],
                out_shape=[
                    rows_w if last else rows_w32,
                    out_of(images, top, width, dtype=f32),
                    out_of(8, width, dtype=f32),
                ],
                compiler_params=params(32),
                cost_estimate=cost(20 * all_rows * width, 9 << 20),
                name="norm_backward",
            )(mid, own, oth, xp, vecs)

        tok = gather_images(tokens)
        placed = [
            jnp.pad(
                jnp.stack([pick(prompts[layer], tasks[i, layer], 0) for i in range(images)]),
                ((0, 0), (1, top - 1 - PROMPTS), (0, 0)),
            )
            for layer in range(LAYERS)
        ]
        attn_w = [attn_gather(layer) for layer in range(LAYERS)]
        mlp_w = [mlp_gather(layer) for layer in range(LAYERS)]
        kept = []
        x = (tok,)
        for layer in range(LAYERS):
            near, far, rows = attn_w[layer]
            bufs, up_row = mlp_w[layer]
            before = biases[layer - 1, 1]
            xp, a, qkv, mixed, lse, part = attn_forward(
                layer, x, placed[layer], vec(gains[layer, 0], shifts[layer, 0], before), rows, near, far
            )
            xm, c, act, slope, part_two = mlp_forward(
                layer, xp, part, send(part, other_core),
                vec(gains[layer, 1], shifts[layer, 1], biases[layer, 0]), up_row, bufs,
            )
            x = (xm, part_two, send(part_two, other_core))
            kept.append((xp, a, qkv, mixed, lse, xm, c, act, slope))

        def out_rows_at(start):
            rows, own, oth = (cut(arr, start, rows_local, 1).astype(f32) for arr in x)
            here = (start + jnp.arange(rows_local))[None, :] < counts[:, None]
            rows = rows + (own + oth + biases[LAYERS - 1, 1])
            return jnp.where(here[:, :, None], rows, 0.0).astype(bf16)

        out = spread_images(out_rows_at)

        dx = gather_images(cotangent)
        sums = [None] * LAYERS
        prompt_parts = [None] * LAYERS
        grads = [None] * LAYERS
        for layer in reversed(range(LAYERS)):
            xp, a, qkv, mixed, lse, xm, c, act, slope = kept[layer]
            near, far, _ = attn_w[layer]
            bufs, _ = mlp_w[layer]
            dz, dh, part, sum_mlp, upb = mlp_backward(layer, dx, slope, bufs)
            other = send(part, other_core)
            s1, s2, keep = mlp_weights(c, dz, act, dh)
            got = plane_reduce(s1, s2, keep)
            total = got[0]
            got = got.astype(bf16)
            for k in range(1, tensor_size):
                total = total + send(got[k], along(k)).astype(f32)
            for b in range(2, bits):
                total = total + send(total.astype(bf16), across(b)).astype(f32)
            mlp_all = lax.all_gather(total.astype(bf16), "dp", axis=0)[: 2 * QUARTERS]
            grad_in = dz if layer == LAYERS - 1 else dx
            mid, dy, dqkv, part, sum_attn, pair = attn_backward(
                layer, grad_in, part, other, xm, vec(gains[layer, 1]), qkv, lse, near, far
            )
            other = send(part, other_core)
            s1, s2, keep = attn_weights(a, dqkv, dy, mixed)
            got = plane_reduce(s1, s2, keep)
            low = got.astype(bf16)
            near_sum = send(low[1], near_of).astype(f32)
            far_sum = send(low[0], far_of).astype(f32)
            total = jnp.where(first_core, got[0], far_sum) + near_sum
            half = attn_rows // 2
            mine = jnp.where(first_core, total[:half], total[half:])
            theirs = jnp.where(first_core, total[half:], total[:half]).astype(bf16)
            total = mine + send(theirs, other_core).astype(f32)
            for b in range(2, bits):
                total = total + send(total.astype(bf16), across(b)).astype(f32)
            attn_all = lax.all_gather(total.astype(bf16), "dp", axis=0)[: 2 * QUARTERS]
            dx, at, sum_norm = norm_backward(
                layer == 0, mid, part, other, xp, vec(gains[layer, 0])
            )
            grads[layer] = (mlp_all, attn_all)
            norms = jnp.stack(
                [sum_norm[0], sum_attn[0], sum_norm[1], sum_attn[1], sum_attn[2], sum_mlp[0]]
            )
            sums[layer] = (norms, upb[0], pair[0])
            at = at[:, 1 : 1 + PROMPTS]
            owner = (plane ^ jnp.arange(planes)) * 2 + core
            task_list = owner[:, None] * per_dev + jnp.arange(per_dev)[None, :]
            hot = (task_list[:, :, None] == tasks[None, None, :, layer]).astype(f32)
            prompt_parts[layer] = sum(
                hot[:, :, i, None, None] * at[i][None, None] for i in range(images)
            ).reshape(planes, per_dev * PROMPTS, width)

        grad_tokens = spread_images(lambda start: cut(dx, start, rows_local, 1))

        norms = 0.5 * jnp.stack([s[0] for s in sums])
        shards = jnp.arange(tensor_size)
        hot = ((shards[:, None] ^ shards[None, :]) == z).astype(f32)
        upb = jnp.stack([s[1] for s in sums]).reshape(LAYERS, tensor_size, half_units)
        upb = jnp.einsum("sk,lkj->lsj", hot, upb, precision=lax.Precision.HIGHEST)
        upb = join(upb, jnp.zeros_like(upb), 2)
        pair = jnp.stack([s[2] for s in sums]).reshape(LAYERS, 2, heads, 3, HEAD_DIM)
        pair = jnp.stack([pair[:, :, :, 0], pair[:, :, :, 2]], axis=3)
        pair = pair.reshape(LAYERS, 2, heads * 2 * HEAD_DIM)
        index = jnp.stack([jnp.where(first_core, z, z ^ 3), z ^ (1 + core)])
        hot = (shards[:, None] == index[None, :]).astype(f32)
        pair = jnp.einsum("sb,lbj->lsj", hot, pair, precision=lax.Precision.HIGHEST)
        flat = jnp.concatenate([norms.reshape(-1), upb.reshape(-1), pair.reshape(-1)])
        flat = flat.reshape(-1, width)
        small_rows = flat.shape[0]
        flat = flat + send(flat.astype(bf16), other_core).astype(f32)
        wanted = jnp.concatenate(prompt_parts, axis=1).astype(bf16)
        for step in range(bits):
            pairs = wanted.reshape((wanted.shape[0] // 2, 2) + wanted.shape[1:])
            payload = jnp.concatenate([pairs[:, 1].reshape(-1, width), flat.astype(bf16)], axis=0)
            got = send(payload, across(step)).astype(f32)
            flat = flat.astype(bf16).astype(f32) + got[-small_rows:]
            wanted = (
                pairs[:, 0].astype(f32) + got[:-small_rows].reshape(pairs[:, 0].shape)
            ).astype(bf16)
        tail = jnp.concatenate([wanted[0].astype(f32), flat], axis=0)
        for step in range(zbits):
            tail = tail + send(tail.astype(bf16), along(1 << step)).astype(f32)
        block = width // tensor_size
        prompt_rows = LAYERS * per_dev * PROMPTS
        grad_prompts = cut(tail[:prompt_rows], z * block, block, 1)
        grad_prompts = grad_prompts.reshape(LAYERS, per_dev, PROMPTS, block)
        flat = tail[prompt_rows:].reshape(-1)
        sizes = [norms.size, norms.size + upb.size]
        norms = cut(flat[: sizes[0]].reshape(LAYERS, 3, 2, width), z * block, block, 3)
        grad_upb = pick(flat[sizes[0] : sizes[1]].reshape(LAYERS, tensor_size, hidden), z, 1)
        grad_pair = pick(flat[sizes[1] :].reshape(LAYERS, tensor_size, -1), z, 1)

        mlp_all = jnp.stack([g[0] for g in grads]).reshape(
            LAYERS, QUARTERS, 2, piece_rows, half_units
        )
        full_up = mlp_all[:, :, :, :wide].transpose(0, 1, 3, 2, 4).reshape(LAYERS, width, hidden)
        full_down = mlp_all[:, :, :, wide:].reshape(LAYERS, QUARTERS, 2, 2, tall, half_units)
        full_down = full_down.transpose(0, 2, 1, 4, 3, 5).reshape(LAYERS, hidden, width)
        attn_all = jnp.stack([g[1] for g in grads]).reshape(LAYERS, QUARTERS, attn_rows, width)
        full_qkv = attn_all[:, :, : in_rows // 4].reshape(LAYERS, in_rows, width).swapaxes(1, 2)
        full_out = attn_all[:, :, in_rows // 4 :].reshape(LAYERS, out_rows, width)
        return (
            out,
            grad_tokens,
            grad_prompts,
            norms[:, 0],
            norms[:, 1],
            full_qkv.astype(f32),
            grad_pair,
            full_out.astype(f32),
            norms[:, 2],
            full_up.astype(f32),
            grad_upb,
            full_down.astype(f32),
        )

    return per_device


def solution(mesh):
    placed = (
        P("dp", "tensor", None),
        P("dp", "tensor", None),
        P("dp", None),
        P("dp", None),
        P(),
        P(),
        P(),
        P(None, None, "tensor"),
        P(None, "tensor"),
        P(None, "tensor", None),
        P(),
        P(None, None, "tensor"),
        P(None, "tensor"),
        P(None, "tensor", None),
    )
    return jax.shard_map(
        build(mesh.shape["dp"], mesh.shape["tensor"]),
        mesh=mesh,
        in_specs=placed,
        out_specs=(
            P("dp", "tensor", None),
            P("dp", "tensor", None),
            P(None, "dp", None, "tensor"),
            P(None, None, "tensor"),
            P(None, None, "tensor"),
            P(None, None, "tensor"),
            P(None, "tensor"),
            P(None, "tensor", None),
            P(None, None, "tensor"),
            P(None, None, "tensor"),
            P(None, "tensor"),
            P(None, "tensor", None),
        ),
        check_vma=False,
    )
```

```python
import functools

import jax
import jax.numpy as jnp
from jax import lax
from jax.experimental import pallas as pl
from jax.experimental.pallas import tpu as pltpu
from jax.sharding import PartitionSpec as P

HEAD_DIM = 64
LAYERS = 2
PROMPTS = 50
QUARTERS = 4
PAD = 16
LIMIT = 50
PARTS = 2
TERMS = 2 * PARTS
ORDER = (
    "pa0 tok pm0 facts",
    "sa0 pa1 pm1 sm0",
    "fa0 sa1 oa0 cot",
    "fm0 <1.sa1 sm1 om0",
    "fa1 oa1 turn wm1",
    "ba1 wa1 nb1 tm1",
    "bm0 ta1 wm0 zm1",
    "za1 ba0 hm1 wa0",
    "tm0 <s.m0 ra1 nb0",
    "ca1 rs pr0 pr1",
    "zm0 <o.nb0 ta0 tf",
    "om1 za0 op hm0",
    "ra0 ca0 co1 tm",
    "<o.op te fi1 co0",
    "fi0",
)
AXES = ("group", "quarter", "core", "tensor")
ALONG = AXES[3]
START, WAIT = 1, 2
epsilon = 1e-06
bf16 = jnp.bfloat16
f32 = jnp.float32
ANY = pl.BlockSpec(memory_space=pl.ANY)
SMEM = pl.BlockSpec(memory_space=pltpu.SMEM)
VMEM = pl.BlockSpec(memory_space=pltpu.VMEM)
NEGATIVE = -1000000000.0


def nn(left, right):
    return lax.dot_general(left, right, (((1,), (0,)), ((), ())), preferred_element_type=f32)


def nt(left, right):
    return lax.dot_general(left, right, (((1,), (1,)), ((), ())), preferred_element_type=f32)


def turn(arr):
    return arr.astype(f32).T.astype(bf16)


def norm_parts(rows):
    centre = rows - jnp.mean(rows, axis=-1, keepdims=True)
    spread = jnp.mean(centre * centre, axis=-1, keepdims=True)
    scale = lax.rsqrt(spread + epsilon)
    return centre * scale, scale


def norm_back(hat, scale, gain, grad):
    inner = grad * gain
    along = jnp.mean(inner * hat, axis=-1, keepdims=True)
    return scale * (inner - jnp.mean(inner, axis=-1, keepdims=True) - hat * along)


def gate_pair(pre):
    size = jnp.abs(pre)
    below = 1.0 + 0.2316418882 * size
    t = pl.reciprocal(below, approx=True)
    t = t * (2.0 - below * t)
    bell = jnp.exp(-0.5 * pre * pre)
    poly = 0.5307027145 * t - 0.7265760135
    poly = poly * t + 0.7107068705
    poly = poly * t - 0.142248368
    poly = poly * t + 0.127414796
    rest = poly * t * bell
    below = jnp.where(pre >= 0.0, 1.0 - rest, rest)
    return pre * below, below + pre * bell * 0.3989422804014327


def cost(flops, size, trans=0):
    return pl.CostEstimate(flops=1, bytes_accessed=1, transcendentals=0)


def params(mib):
    return pltpu.CompilerParams(vmem_limit_bytes=mib << 20)


def fetch(copies, sems, first=0, phase=None):
    made = [pltpu.make_async_copy(src, dst, sems.at[first + i]) for i, (src, dst) in enumerate(copies)]
    if phase != WAIT:
        for copy in made:
            copy.start()
    if phase != START:
        for copy in made:
            copy.wait()


def rows16(start, size):
    return pl.ds(pl.multiple_of(start, 16), size)


def fact(info, mine, theirs, image, column):
    return jnp.where(info[0] == (info[1] >> 1), mine[image, column], theirs[image, column])


def attn_fetch(layer, info, own_qkv, own_out, bufs, w_qkv, w_out, sems, phase=None):
    own_qkv, own_out = own_qkv.at[layer], own_out.at[layer]
    near, far = [buf.at[0] for buf in bufs], [buf.at[1] for buf in bufs]
    rows_in, rows_out = own_qkv.shape[0], own_out.shape[0]
    part_in, part_out = rows_in // QUARTERS, rows_out // QUARTERS

    def pieces(bufs, block):
        copies = []
        for i in range(QUARTERS):
            quarter = info[2 + i]
            src = bufs[i]
            if w_qkv is not None:
                rows = rows16(block * rows_in + part_in * quarter, part_in)
                copies.append((src.at[pl.ds(0, part_in)], w_qkv.at[rows]))
            if w_out is not None:
                rows = rows16(block * rows_out + part_out * quarter, part_out)
                copies.append((src.at[pl.ds(part_in, part_out)], w_out.at[rows]))
        return copies

    @pl.when(info[0] == 0)
    def _():
        own = []
        if w_qkv is not None:
            own.append((own_qkv, w_qkv.at[pl.ds(0, rows_in)]))
        if w_out is not None:
            own.append((own_out, w_out.at[pl.ds(0, rows_out)]))
        fetch(own + pieces(near, 1), sems, 0, phase)

    @pl.when(info[0] != 0)
    def _():
        fetch(pieces(far, 0) + pieces(near, 1), sems, 0, phase)


def mlp_fetch(
    layer, info, own_up, own_down, bufs, w_up, w_down, sems, bias_rows=None, phase=None
):
    own_down = own_down.at[layer]
    width = own_down.shape[1]
    half = own_down.shape[0] // 2
    wide, tall = width // QUARTERS, half // QUARTERS
    split = width // 2
    start = info[0] * half
    copies = []
    if w_down is not None:
        copies.append((own_down.at[rows16(start, half)], w_down.at[pl.ds(0, half)]))
    if bias_rows is not None:
        last = bufs[0].shape[1] - PAD
        copies.append((bufs[0].at[:, pl.ds(last, PAD), :], bias_rows))
    if own_up is not None:
        columns = pl.ds(pl.multiple_of(start, 128), half)
        copies.append((own_up.at[layer, :, columns], w_up.at[:, pl.ds(0, half)]))
    for i in range(QUARTERS):
        quarter = info[2 + i]
        for k in range(bufs[i].shape[0]):
            src = bufs[i].at[k]
            units = rows16((k + 1) * half + tall * quarter, tall)
            if own_up is not None:
                columns = pl.ds((k + 1) * half, half)
                copies.append(
                    (src.at[pl.ds(0, wide)], w_up.at[rows16(wide * quarter, wide), columns])
                )
            if w_down is not None:
                lower = src.at[pl.ds(wide + tall, tall)]
                copies.append((src.at[pl.ds(wide, tall)], w_down.at[units, pl.ds(0, split)]))
                copies.append((lower, w_down.at[units, pl.ds(split, split)]))
    fetch(copies, sems, 0, phase)


def unit_bias(layer, info, bias_ref, bias_rows, k):
    half = bias_ref.shape[1] // 2
    if k == 0:
        one, two = bias_ref[layer : layer + 1, :half], bias_ref[layer : layer + 1, half:]
    else:
        one, two = bias_rows[k - 1, 0:1, :], bias_rows[k - 1, 1:2, :]
    return jnp.where(info[0] == 0, one, two).astype(f32)


def fetch_parts(refs, held, sems, first=0):
    size = refs[0].shape[0]
    fetch([(ref, held.at[pl.ds(i * size, size)]) for i, ref in enumerate(refs)], sems, first)


def both(held, step):
    half = held.shape[0] // 2
    rows = half // 3
    start = pl.multiple_of(rows * step, 16)
    return held[pl.ds(start, rows), :].astype(f32) + held[pl.ds(half + start, rows), :].astype(f32)


def put_part(refs, step, value):
    rows, size = value.shape[0], refs[0].shape[0]
    for i in range(size * len(refs) // rows):

        @pl.when(step == i)
        def _(i=i):
            done = 0
            while done < rows:
                ref, at = divmod(i * rows + done, size)
                count = min(rows - done, size - at)
                refs[ref][at : at + count, :] = value[done : done + count]
                done += count


def head_masks(rows, cols, axis):
    place = lax.broadcasted_iota(jnp.int32, (rows, cols), axis)
    return place < HEAD_DIM


def image_copies(info, bufs, rows):
    block = bufs[0].shape[1]
    core, odd = info[0], info[1] & 1
    places = [2 * core + odd, 2 * core + 1 - odd, 2 * (1 - core) + odd, 2 * (1 - core) + 1 - odd]
    return [
        (bufs[i], rows.at[:, rows16(block * places[i], block), :]) for i in range(len(bufs))
    ]


def attn_forward_kernel(layer, info, mine, theirs, *refs):
    later = layer > 0
    x_refs = refs[: 1 + TERMS if later else 4]
    refs = refs[len(x_refs) :]
    prompt_ref, gain_ref, shift_ref, branch_ref, bias_ref, own_qkv, own_out = refs[:7]
    bufs = refs[7:11]
    xp_ref, a_ref, qkv_ref, mix_ref, lse_ref = refs[11:16]
    w_qkv, bias_rows, sems, held = refs[16:20]
    step = pl.program_id(0)

    @pl.when(step == 0)
    def _():
        attn_fetch(layer, info, own_qkv, own_out, bufs, w_qkv, None, sems, START)
        last = bufs[0].shape[1] - PAD
        fetch([(bufs[0].at[:, pl.ds(last, PAD)], bias_rows)], sems, 24)
        if later:
            fetch_parts(x_refs[1:], held, sems, 25)
        else:
            fetch(image_copies(info, x_refs, held), sems, 25)

    if later:
        after = branch_ref[layer - 1, 1:2, :].astype(f32)
        rows = x_refs[0][0] + (both(held, step) + after)
    else:
        rows = held[step].astype(f32)
    top = 64
    places, tasks = prompt_ref.shape[1], prompt_ref.shape[1] // PROMPTS
    place = lax.broadcasted_iota(jnp.int32, (top, places), 0)
    entry = lax.broadcasted_iota(jnp.int32, (top, places), 1)
    task = fact(info, mine, theirs, step, 1 + layer)
    hot = (entry == (place - 1) * tasks + task) & (place >= 1) & (place <= PROMPTS)
    placed = nn(jnp.where(hot, 1.0, 0.0).astype(bf16), prompt_ref[0])
    place = lax.broadcasted_iota(jnp.int32, placed.shape, 0)
    here = (place >= 1) & (place <= PROMPTS)
    rows = jnp.concatenate([jnp.where(here, placed, rows[:top]), rows[top:]], axis=0)
    xp_ref[0] = rows
    hat, _ = norm_parts(rows)
    gain, shift = gain_ref[layer, 0:1, :].astype(f32), shift_ref[layer, 0:1, :].astype(f32)
    normed = (hat * gain + shift).astype(bf16)
    a_ref[0] = normed

    @pl.when(step == 0)
    def _():
        attn_fetch(layer, info, own_qkv, own_out, bufs, w_qkv, None, sems, WAIT)

    qkv = nt(normed, w_qkv[...])
    size = bias_ref.shape[1]
    first = jnp.where(info[0] == 0, bias_ref[layer : layer + 1, :], bias_rows[1, 0:1, :size]).astype(f32)
    lines = jnp.concatenate([first, bias_rows[0, 0:1, :size].astype(f32)], axis=1)
    low_line = head_masks(1, 128, 1)
    seq = rows.shape[0]
    low = head_masks(seq, 128, 1)
    low_t = head_masks(128, seq, 0)
    valid = lax.broadcasted_iota(jnp.int32, (seq, seq), 0) < fact(info, mine, theirs, step, 0)
    pairs = w_qkv.shape[0] // 384
    for p in range(pairs):
        blocks = [qkv[:, 384 * p + 128 * j : 384 * p + 128 * (j + 1)] for j in range(3)]
        one, two = (lines[:, 256 * p + 128 * h : 256 * p + 128 * (h + 1)] for h in range(2))
        turned = [
            pltpu.roll(jnp.broadcast_to(line, (8, 128)), HEAD_DIM, 1)[0:1] for line in (one, two)
        ]
        none = jnp.zeros_like(one)
        biases = [
            jnp.where(low_line, one, none),
            jnp.where(low_line, turned[0], turned[1]),
            jnp.where(low_line, none, two),
        ]
        blocks = [block + bias for block, bias in zip(blocks, biases)]
        scale = HEAD_DIM**-0.5
        blocks[0] = blocks[0] * jnp.where(low_line, scale, 1.0)
        blocks[1] = blocks[1] * jnp.where(low_line, 1.0, scale)
        query = jnp.where(low, blocks[0], blocks[1]).astype(bf16)
        key = pltpu.roll(jnp.where(low, blocks[2], blocks[0]), HEAD_DIM, 1).astype(bf16)
        value_t = jnp.where(low, blocks[1], blocks[2])
        qkv_ref[0, :, 384 * p : 384 * p + 128] = query
        qkv_ref[0, :, 384 * p + 128 : 384 * p + 256] = key
        qkv_ref[0, :, 384 * p + 256 : 384 * p + 384] = value_t.astype(bf16)
        value_t = value_t.T.astype(bf16)
        outs = []
        for h in range(2):
            lanes = low if h == 0 else jnp.logical_not(low)
            one_key = jnp.where(lanes, key, jnp.zeros_like(key))
            scores = jnp.where(valid, nt(one_key, query), NEGATIVE)
            peak = jnp.max(scores, axis=0, keepdims=True)
            exps = jnp.exp(scores - peak)
            total = jnp.sum(exps, axis=0, keepdims=True)
            lse_ref[0, 2 * p + h : 2 * p + h + 1, :] = peak + jnp.log(total)
            outs.append(nn(value_t, exps.astype(bf16)) * (1.0 / total))
        mixed = jnp.where(low_t, outs[0], outs[1]).T.astype(bf16)
        mix_ref[0, :, 128 * p : 128 * (p + 1)] = mixed


def attn_out_kernel(layer, info, mix_ref, own_qkv, own_out, *refs):
    bufs, parts, w_out, sems = refs[:4], refs[4:-2], refs[-2], refs[-1]
    step = pl.program_id(0)

    @pl.when(step == 0)
    def _():
        attn_fetch(layer, info, own_qkv, own_out, bufs, None, w_out, sems)

    put_part(parts, step, nn(mix_ref[0], w_out[...]).astype(bf16))


def mlp_start(layer, xp_ref, total, gain_ref, shift_ref, branch_ref, xm_ref, c_ref):
    before = branch_ref[layer, 0:1, :].astype(f32)
    rows = xp_ref[0] + (total + before)
    xm_ref[0] = rows
    hat, _ = norm_parts(rows)
    gain, shift = gain_ref[layer, 1:2, :].astype(f32), shift_ref[layer, 1:2, :].astype(f32)
    normed = (hat * gain + shift).astype(bf16)
    c_ref[0] = normed
    return normed


def split_refs(refs):
    return refs[1 + TERMS : 4 + TERMS], *refs[4 + TERMS : 7 + TERMS]


def mlp_forward_kernel(layer, info, *refs):
    xp_ref, terms, norms, bias_ref, own_up, own_down = refs[0], refs[1 : 1 + TERMS], *split_refs(refs)
    bufs = refs[7 + TERMS : 11 + TERMS]
    xm_ref, c_ref, act_ref, slope_ref, w_up, sems, bias_rows, held = refs[11 + TERMS :]
    step = pl.program_id(0)

    @pl.when(step == 0)
    def _():
        mlp_fetch(layer, info, own_up, own_down, bufs, w_up, None, sems, bias_rows, START)
        fetch_parts(terms, held, sems, 56)

    normed = mlp_start(layer, xp_ref, both(held, step), *norms, xm_ref, c_ref)

    @pl.when(step == 0)
    def _():
        mlp_fetch(layer, info, own_up, own_down, bufs, w_up, None, sems, bias_rows, WAIT)

    half = w_up.shape[1] // 4
    for k in range(4):
        here = slice(k * half, (k + 1) * half)
        pre = nn(normed, w_up[:, here]) + unit_bias(layer, info, bias_ref, bias_rows, k)
        act, slope = gate_pair(pre)
        act_ref[0, :, here] = act.astype(bf16)
        slope_ref[0, :, here] = slope.astype(bf16)


def mlp_turn_kernel(layer, info, mine, theirs, *refs):
    xp_ref, terms, norms, bias_ref, own_up, own_down = refs[0], refs[1 : 1 + TERMS], *split_refs(refs)
    bufs, cot = refs[7 + TERMS : 11 + TERMS], refs[11 + TERMS : 15 + TERMS]
    xm_ref, c_ref, act_ref, dz_ref, dh_ref, sum_ref, upb_ref = refs[15 + TERMS : 22 + TERMS]
    parts = refs[22 + TERMS : -6]
    w_up, w_down, sems, bias_rows, cot_rows, held = refs[-6:]
    step = pl.program_id(0)

    @pl.when(step == 0)
    def _():
        mlp_fetch(layer, info, own_up, own_down, bufs, w_up, w_down, sems, bias_rows, START)
        fetch_parts(terms, held, sems, 56)
        fetch(image_copies(info, cot, cot_rows), sems, 56)
        sum_ref[...] = jnp.zeros_like(sum_ref)
        upb_ref[...] = jnp.zeros_like(upb_ref)

    normed = mlp_start(layer, xp_ref, both(held, step), *norms, xm_ref, c_ref)
    grad = cot_rows[step].astype(f32)
    place = lax.broadcasted_iota(jnp.int32, grad.shape, 0)
    grad = jnp.where(place < fact(info, mine, theirs, step, 0), grad, 0.0)
    sum_ref[0:1, :] += jnp.sum(grad, axis=0, keepdims=True)
    low = grad.astype(bf16)
    dz_ref[0] = low

    @pl.when(step == 0)
    def _():
        mlp_fetch(layer, info, own_up, own_down, bufs, w_up, w_down, sems, bias_rows, WAIT)

    half = w_up.shape[1] // 4
    for k in range(4):
        here = slice(k * half, (k + 1) * half)
        pre = nn(normed, w_up[:, here]) + unit_bias(layer, info, bias_ref, bias_rows, k)
        act, slope = gate_pair(pre)
        act_ref[0, :, here] = act.astype(bf16)
        hidden = (nt(low, w_down[here, :]) * slope).astype(bf16)
        dh_ref[0, :, here] = hidden
        upb_ref[0:1, here] += jnp.sum(hidden.astype(f32), axis=0, keepdims=True)
    put_part(parts, step, nt(dh_ref[0], w_up[...]).astype(bf16))


def mlp_out_kernel(layer, info, act_ref, own_down, *refs):
    bufs, parts, w_down, sems = refs[:4], refs[4:-2], refs[-2], refs[-1]
    step = pl.program_id(0)

    @pl.when(step == 0)
    def _():
        mlp_fetch(layer, info, None, own_down, bufs, None, w_down, sems)

    put_part(parts, step, nn(act_ref[0], w_down[...]).astype(bf16))


def mlp_backward_kernel(layer, info, dx_ref, slope_ref, own_up, own_down, *refs):
    bufs = refs[:4]
    dz_ref, dh_ref, sum_ref, upb_ref = refs[4:8]
    parts = refs[8:-3]
    w_up, w_down, sems = refs[-3:]
    step = pl.program_id(0)

    @pl.when(step == 0)
    def _():
        mlp_fetch(layer, info, own_up, own_down, bufs, w_up, w_down, sems, phase=START)
        sum_ref[...] = jnp.zeros_like(sum_ref)
        upb_ref[...] = jnp.zeros_like(upb_ref)

    grad = dx_ref[0].astype(f32)
    sum_ref[0:1, :] += jnp.sum(grad, axis=0, keepdims=True)
    low = grad.astype(bf16)
    dz_ref[0] = low

    @pl.when(step == 0)
    def _():
        mlp_fetch(layer, info, own_up, own_down, bufs, w_up, w_down, sems, phase=WAIT)

    units = w_up.shape[1]
    for at in range(0, units, 384):
        hidden = nt(low, w_down[at : at + 384, :]) * slope_ref[0, :, at : at + 384].astype(f32)
        hidden = hidden.astype(bf16)
        dh_ref[0, :, at : at + 384] = hidden
        upb_ref[0:1, at : at + 384] += jnp.sum(hidden.astype(f32), axis=0, keepdims=True)
    put_part(parts, step, nt(dh_ref[0], w_up[...]).astype(bf16))


def mlp_weight_kernel(
    info, c_ref, dz_ref, act_ref, dh_ref, s1_ref, s1_late_ref, s2_ref, keep_ref, c_t, up, down
):
    step = pl.program_id(0)

    @pl.when(step == 0)
    def _():
        c_t[...] = turn(c_ref[...])

    up[...] = nn(c_t[...], dh_ref[...]).astype(bf16)
    down[...] = nn(turn(act_ref[...]), dz_ref[...]).astype(bf16)
    wide, tall = up.shape[0] // QUARTERS, down.shape[0] // QUARTERS
    split = down.shape[1] // 2

    def put(out, i):
        quarter = info[2 + i]
        out[0:wide, :] = up[rows16(wide * quarter, wide), :]
        rows = down[rows16(tall * quarter, tall), :]
        out[wide : wide + tall, :] = rows[:, :split]
        out[wide + tall :, :] = rows[:, split:]

    put(keep_ref.at[0], 0)
    put(s2_ref.at[0], 2)

    @pl.when(step < 2)
    def _():
        put(s1_ref.at[0, 0], 1)
        put(s1_ref.at[1, 0], 3)

    @pl.when(step >= 2)
    def _():
        put(s1_late_ref.at[0, 0], 1)
        put(s1_late_ref.at[1, 0], 3)


def attn_backward_kernel(
    layer, info, mine, theirs, dx_ref, xm_ref, gain_ref, qkv_ref, lse_ref, *refs
):
    terms, own_qkv, own_out = refs[:TERMS], refs[TERMS], refs[TERMS + 1]
    refs = refs[TERMS + 2 :]
    bufs = refs[:4]
    mid_ref, dy_ref, dqkv_ref, sum_ref, pair_ref = refs[4:9]
    parts = refs[9:-4]
    w_qkv, w_out, sems, held = refs[-4:]
    step = pl.program_id(0)

    @pl.when(step == 0)
    def _():
        attn_fetch(layer, info, own_qkv, own_out, bufs, w_qkv, w_out, sems, START)
        fetch_parts(terms, held, sems, 24)
        sum_ref[...] = jnp.zeros_like(sum_ref)
        pair_ref[...] = jnp.zeros_like(pair_ref)

    back = both(held, step)
    hat, scale = norm_parts(xm_ref[0])
    grad = dx_ref[0].astype(f32) + norm_back(hat, scale, gain_ref[layer, 1:2, :].astype(f32), back)
    mid_ref[0] = grad
    sum_ref[0:1, :] += jnp.sum(back * hat, axis=0, keepdims=True)
    sum_ref[1:2, :] += jnp.sum(back, axis=0, keepdims=True)
    sum_ref[2:3, :] += jnp.sum(grad, axis=0, keepdims=True)
    low_grad = grad.astype(bf16)
    dy_ref[0] = low_grad

    @pl.when(step == 0)
    def _():
        attn_fetch(layer, info, own_qkv, own_out, bufs, w_qkv, w_out, sems, WAIT)

    seq = grad.shape[0]
    d_mixed = nt(low_grad, w_out[...]).astype(bf16)
    low = head_masks(seq, 128, 1)
    low_t = head_masks(128, seq, 0)
    valid = lax.broadcasted_iota(jnp.int32, (seq, seq), 0) < fact(info, mine, theirs, step, 0)
    pairs = w_out.shape[0] // 128
    for p in range(pairs):
        query = qkv_ref[0, :, 384 * p : 384 * p + 128]
        key = qkv_ref[0, :, 384 * p + 128 : 384 * p + 256]
        value = qkv_ref[0, :, 384 * p + 256 : 384 * p + 384]
        grad_o = d_mixed[:, 128 * p : 128 * (p + 1)]
        key_t = turn(key)
        d_query, d_key, d_value = [], [], []
        for h in range(2):
            lanes = low if h == 0 else jnp.logical_not(low)
            none = jnp.zeros_like(key)
            scores = jnp.where(valid, nt(jnp.where(lanes, key, none), query), NEGATIVE)
            probs = jnp.exp(scores - lse_ref[0, 2 * p + h : 2 * p + h + 1, :])
            d_probs = nt(jnp.where(lanes, value, none), grad_o)
            along = jnp.sum(probs * d_probs, axis=0, keepdims=True)
            d_scores = (probs * (d_probs - along)).astype(bf16)
            d_value.append(nn(probs.astype(bf16), grad_o))
            d_key.append(nn(d_scores, query))
            d_query.append(nn(key_t, d_scores))
        d_query = jnp.where(low_t, d_query[0], d_query[1]).T * (HEAD_DIM**-0.5)
        d_key = pltpu.roll(jnp.where(low, d_key[0], d_key[1]), HEAD_DIM, 1)
        d_value = jnp.where(low, d_value[0], d_value[1])
        for j, block in enumerate(
            (
                jnp.where(low, d_query, d_key),
                jnp.where(low, d_value, d_query),
                jnp.where(low, d_key, d_value),
            )
        ):
            block = block.astype(bf16)
            at = 384 * p + 128 * j
            dqkv_ref[0, :, at : at + 128] = block
            pair_ref[0:1, at : at + 128] += jnp.sum(block.astype(f32), axis=0, keepdims=True)
    put_part(parts, step, nn(dqkv_ref[0], w_qkv[...]).astype(bf16))


def attn_weight_kernel(info, a_ref, dqkv_ref, dy_ref, mix_ref, s1_ref, s2_ref, keep_ref, w_in, w_out):
    for at in range(0, w_in.shape[0], 384):
        w_in[at : at + 384, :] = nn(turn(dqkv_ref[:, at : at + 384]), a_ref[...]).astype(bf16)
    w_out[...] = nn(turn(mix_ref[...]), dy_ref[...]).astype(bf16)
    rows_in, rows_out = w_in.shape[0] // 2, w_out.shape[0] // 2
    part_in, part_out = rows_in // QUARTERS, rows_out // QUARTERS
    for i, out in enumerate((keep_ref, s1_ref.at[0], s2_ref, s1_ref.at[1])):
        quarter = info[2 + i]
        for b in range(2):
            out[b, 0:part_in, :] = w_in[rows16(b * rows_in + part_in * quarter, part_in), :]
            out[b, part_in:, :] = w_out[rows16(b * rows_out + part_out * quarter, part_out), :]


def norm_backward_kernel(layer, info, mid_ref, xp_ref, gain_ref, *refs):
    terms, held, sems = refs[:TERMS], refs[-2], refs[-1]
    refs = refs[TERMS:]
    outs = refs[:1] if layer else refs[:2]
    at_ref, sum_ref = refs[len(outs) : len(outs) + 2]
    step = pl.program_id(0)

    @pl.when(step == 0)
    def _():
        fetch_parts(terms, held, sems)
        sum_ref[...] = jnp.zeros_like(sum_ref)

    back = both(held, step)
    hat, scale = norm_parts(xp_ref[0])
    grad = mid_ref[0] + norm_back(hat, scale, gain_ref[layer, 0:1, :].astype(f32), back)
    sum_ref[0:1, :] += jnp.sum(back * hat, axis=0, keepdims=True)
    sum_ref[1:2, :] += jnp.sum(back, axis=0, keepdims=True)
    top = at_ref.shape[1]
    place = lax.broadcasted_iota(jnp.int32, (top, grad.shape[1]), 0)
    here = (place >= 1) & (place <= PROMPTS)
    at_ref[0] = grad[:top]
    grad = jnp.concatenate([jnp.where(here, 0.0, grad[:top]), grad[top:]], axis=0)
    if layer:
        outs[0][0] = grad
    else:
        refs[-3][...] = grad.astype(bf16)
        send_rows(info, refs[-3], outs[0], outs[1])


def send_rows(info, rows, one_ref, two_ref):
    block = one_ref.shape[1]
    core, odd = info[0], info[1] & 1
    one_ref[0] = rows[rows16(block * (2 * core + odd), block), :]
    two_ref[0] = rows[rows16(block * (2 * core + 1 - odd), block), :]


def out_kernel(info, mine, theirs, xm_ref, branch_ref, *refs):
    terms, one_ref, two_ref, rows_held, held, sems = refs[:TERMS], *refs[TERMS:]
    step = pl.program_id(0)

    @pl.when(step == 0)
    def _():
        fetch_parts(terms, held, sems)

    after = branch_ref[LAYERS - 1, 1:2, :].astype(f32)
    rows = xm_ref[0] + (both(held, step) + after)
    place = lax.broadcasted_iota(jnp.int32, rows.shape, 0)
    here = place < fact(info, mine, theirs, step, 0)
    rows_held[...] = jnp.where(here, rows, 0.0).astype(bf16)
    send_rows(info, rows_held, one_ref, two_ref)


def facts_kernel(info, mask_ref, tasks_ref, out_ref):
    images = mask_ref.shape[0] // 2
    lane = lax.broadcasted_iota(jnp.int32, (2 * images, 128), 1)
    counts = jnp.sum(mask_ref[...].astype(f32), axis=1, keepdims=True).astype(jnp.int32)
    table = jnp.where(lane == 0, counts, 0)
    for layer in range(LAYERS):
        table = jnp.where(lane == 1 + layer, tasks_ref[:, layer : layer + 1], table)
    out_ref[...] = jnp.zeros_like(out_ref)
    out_ref[0:images, :] = jnp.where((info[1] & 1) == 0, table[:images], table[images:])


def attn_piece_kernel(layer, info, qkv_ref, out_ref, bias_ref, piece_ref, sems):
    part_in, part_out = qkv_ref.shape[1] // QUARTERS, out_ref.shape[1] // QUARTERS
    quarter = info[2]
    fetch(
        [
            (
                qkv_ref.at[layer, rows16(part_in * quarter, part_in)],
                piece_ref.at[pl.ds(0, part_in)],
            ),
            (
                out_ref.at[layer, rows16(part_out * quarter, part_out)],
                piece_ref.at[pl.ds(part_in, part_out)],
            ),
        ],
        sems,
    )
    bias = bias_ref[layer : layer + 1, :]
    bias = jnp.concatenate([bias, jnp.zeros_like(bias)], axis=1).astype(f32)
    piece_ref[part_in + part_out :, :] = jnp.broadcast_to(bias, (PAD, bias.shape[1])).astype(bf16)


def mlp_piece_kernel(layer, info, up_ref, down_ref, bias_ref, piece_ref, sems):
    width, half = up_ref.shape[1], down_ref.shape[1] // 2
    wide, tall, split = width // QUARTERS, half // QUARTERS, width // 2
    quarter, start = info[2], info[0] * half
    units = rows16(start + tall * quarter, tall)
    columns = pl.ds(pl.multiple_of(start, 128), half)
    fetch(
        [
            (up_ref.at[layer, rows16(wide * quarter, wide), columns], piece_ref.at[pl.ds(0, wide)]),
            (down_ref.at[layer, units, pl.ds(0, split)], piece_ref.at[pl.ds(wide, tall)]),
            (down_ref.at[layer, units, pl.ds(split, split)], piece_ref.at[pl.ds(wide + tall, tall)]),
        ],
        sems,
    )
    bias = bias_ref[layer : layer + 1, :].astype(f32)
    first = lax.broadcasted_iota(jnp.int32, (PAD, half), 0) == 0
    rows = jnp.where(first, bias[:, :half], bias[:, half:])
    piece_ref[wide + 2 * tall :, :] = rows.astype(bf16)


def image_piece_kernel(info, rows_ref, one_ref, two_ref, sems):
    images = one_ref.shape[0]
    odd = info[1] & 1
    fetch(
        [
            (rows_ref.at[pl.ds(odd * images, images)], one_ref),
            (rows_ref.at[pl.ds((1 - odd) * images, images)], two_ref),
        ],
        sems,
    )


def stack_kernel(*refs):
    bufs, out_ref, sems = refs[:-2], refs[-2], refs[-1]
    fetch([(buf, out_ref.at[k]) for k, buf in enumerate(bufs)], sems)


def by_half(early_ref, late_ref):
    return jnp.where(pl.program_id(0) < 2, early_ref[0, 0], late_ref[0, 0]).astype(f32)


def mlp_two_kernel(s2_ref, early_ref, late_ref, out_ref):
    out_ref[0] = (s2_ref[0].astype(f32) + by_half(early_ref, late_ref)).astype(bf16)


def add_two_kernel(s2_ref, got_ref, out_ref):
    out_ref[...] = (s2_ref[...].astype(f32) + got_ref[0].astype(f32)).astype(bf16)


def mlp_add_kernel(keep_ref, early_ref, late_ref, last_ref, own_ref, *outs):
    step = pl.program_id(0)
    total = keep_ref[0].astype(f32) + by_half(early_ref, late_ref) + last_ref[0].astype(f32)

    @pl.when(step == 0)
    def _():
        own_ref[...] = total

    for k, out in enumerate(outs):

        @pl.when(step == k + 1)
        def _(out=out):
            out[...] = total.astype(bf16)


def attn_add_kernel(keep_ref, got_ref, last_ref, own_ref, near_ref, far_ref):
    def total(b):
        return keep_ref[b].astype(f32) + got_ref[0, b].astype(f32) + last_ref[b].astype(f32)

    first = total(0)
    own_ref[...] = first
    far_ref[...] = first.astype(bf16)
    near_ref[...] = total(1).astype(bf16)


def attn_merge_kernel(info, own_ref, near_ref, far_ref, mine_ref, theirs_ref):
    half = mine_ref.shape[0]
    near = near_ref[...].astype(f32)

    @pl.when(info[0] == 0)
    def _():
        total = own_ref[...] + near
        mine_ref[...] = total[:half]
        theirs_ref[...] = total[half:].astype(bf16)

    @pl.when(info[0] != 0)
    def _():
        total = far_ref[...].astype(f32) + near
        mine_ref[...] = total[half:]
        theirs_ref[...] = total[:half].astype(bf16)


def sum_kernel(own_ref, *refs):
    total = own_ref[...].astype(f32)
    for ref in refs[:-1]:
        total += ref[...].astype(f32)
    refs[-1][...] = total.astype(refs[-1].dtype)


def pack_kernel(mine_ref, got_ref, units_ref, out_ref):
    total = (mine_ref[...] + got_ref[...].astype(f32)).astype(bf16)
    units, rows = units_ref.shape[0], total.shape[0]
    half = out_ref.shape[1]
    out_ref[0:units, :] = units_ref[...]
    out_ref[units : units + rows, :] = total[:, :half]
    out_ref[units + rows :, :] = total[:, half:]


def prompt_kernel(layer, per_dev, info, mine, theirs, at_ref, out_ref):
    top = at_ref.shape[1]
    tasks = [fact(info, mine, theirs, i, 1 + layer) for i in range(at_ref.shape[0])]
    for r in range(out_ref.shape[0]):
        for j in range(per_dev):
            task = ((info[6] ^ r) * 2 + info[0]) * per_dev + j
            total = jnp.zeros(at_ref.shape[1:], f32)
            for i, held in enumerate(tasks):
                total += jnp.where(held == task, at_ref[i], 0.0)
            out_ref[r, j * top : (j + 1) * top, :] = total.astype(bf16)


def sums_kernel(info, *refs):
    out_ref = refs[-1]
    core, z = info[0], info[1]
    half = refs[3].shape[1] // 4
    block = out_ref.shape[1] // 4
    out_ref[...] = jnp.zeros_like(out_ref)
    low = head_masks(1, 128, 1)
    for layer in range(LAYERS):
        norm, attn, mlp, upb, pair = refs[5 * layer : 5 * layer + 5]
        for i, row in enumerate((norm[0:1], attn[0:1], norm[1:2], attn[1:2], attn[2:3], mlp[0:1])):
            out_ref[6 * layer + i : 6 * layer + i + 1, :] = 0.5 * row
        heads = pair.shape[1] // (3 * HEAD_DIM)
        lines = []
        for h in range(heads):
            at = 384 * (h // 2)
            blocks = [pair[0:1, at + 128 * j : at + 128 * (j + 1)] for j in range(3)]
            middle = pltpu.roll(jnp.broadcast_to(blocks[1], (8, 128)), HEAD_DIM, 1)[0:1]
            if h % 2 == 0:
                lines.append(jnp.where(low, blocks[0], middle))
            else:
                lines.append(jnp.where(low, middle, blocks[2]))
        lines = [jnp.concatenate(lines[b * heads // 2 : (b + 1) * heads // 2], 1) for b in range(2)]
        for s in range(4):
            columns = slice(s * block, (s + 1) * block)
            line = jnp.zeros((1, half), f32)
            for k in range(4):
                line += jnp.where((z ^ s) == k, upb[0:1, k * half : (k + 1) * half], 0.0)
            at = 6 * LAYERS + 4 * layer
            for i in range(half // block):
                piece = line[:, i * block : (i + 1) * block]
                for c in range(2):
                    row = at + c * (half // block) + i
                    out_ref[row : row + 1, columns] = jnp.where(core == c, piece, 0.0)
            line = jnp.zeros_like(lines[0])
            for b in range(2):
                line += jnp.where((z ^ s) == jnp.where(core == 0, b, 3 - b), lines[b], 0.0)
            at = 10 * LAYERS + 2 * layer
            for i in range(2):
                out_ref[at + i : at + i + 1, columns] = line[:, i * block : (i + 1) * block]


def tail_first_kernel(planes, *refs):
    prompts, flat_ref, got_ref = refs[:LAYERS], refs[LAYERS], refs[LAYERS + 1]
    outs = refs[LAYERS + 2 :]
    flat = flat_ref[...] + got_ref[...].astype(f32)
    size = prompts[0].shape[1]
    for r in range(planes):
        for i, ref in enumerate(prompts):
            outs[r][i * size : (i + 1) * size, :] = ref[r].astype(outs[r].dtype)
        outs[r][LAYERS * size :, :] = flat.astype(outs[r].dtype)


def tail_middle_kernel(shards, info, own_ref, *refs):
    outs = refs[-shards:]
    total = own_ref[...]
    for ref in refs[:-shards]:
        total += ref[...].astype(f32)
    block = total.shape[1] // shards
    for s in range(shards):
        piece = total[:, s * block : (s + 1) * block]
        for k in range(shards):

            @pl.when((info[1] ^ k) == s)
            def _(k=k, piece=piece):
                outs[k][...] = piece.astype(outs[k].dtype)


def tail_end_kernel(per_dev, own_ref, *refs):
    got, outs = refs[:-6], refs[-6:]
    total = own_ref[...]
    for ref in got:
        total += ref[...].astype(f32)
    prompts_ref, gain_ref, bias_ref, branch_ref, units_ref, heads_ref = outs
    top, block = 64, total.shape[1]
    for layer in range(LAYERS):
        for j in range(per_dev):
            at = (layer * per_dev + j) * top
            prompts_ref[layer, j] = total[at : at + top][1 : 1 + PROMPTS]
        at = LAYERS * per_dev * top
        for i, ref in enumerate((gain_ref, bias_ref, branch_ref)):
            row = at + 6 * layer + 2 * i
            ref[layer] = total[row : row + 2]
        for i in range(4):
            row = at + 6 * LAYERS + 4 * layer + i
            units_ref[layer : layer + 1, i * block : (i + 1) * block] = total[row : row + 1]
        for i in range(2):
            row = at + 10 * LAYERS + 2 * layer + i
            heads_ref[layer : layer + 1, i * block : (i + 1) * block] = total[row : row + 1]


def collect_kernel(info, *refs):
    bufs, out_ref, sems = refs[:-2], refs[-2], refs[-1]
    fetch([(buf, out_ref.at[info[2 + r]]) for r, buf in enumerate(bufs)], sems)


def finish_kernel(info, mine_ref, theirs_ref, *refs):
    first = info[0] == 0
    halves = (mine_ref[0], theirs_ref[0])
    whole_ref = (jnp.where(first, *halves), jnp.where(first, *halves[::-1]))
    up_ref, down_ref, qkv_ref, out_ref = refs[-4:]
    wide = up_ref.shape[1]
    half = halves[0].shape[1]
    tall = down_ref.shape[3]
    part_in = qkv_ref.shape[1]
    split = down_ref.shape[4] // 2
    rows = (part_in + out_ref.shape[1]) // 2
    for c in range(2):
        up_ref[0, :, c * half : (c + 1) * half] = whole_ref[c][:wide].astype(f32)
        down_ref[0, c, 0, :, :split] = whole_ref[c][wide : wide + tall].astype(f32)
        down_ref[0, c, 0, :, split:] = whole_ref[c][wide + tall : wide + 2 * tall].astype(f32)
    for side in range(2):
        at = wide + 2 * tall + side * rows
        columns = slice(side * half, (side + 1) * half)
        both_rows = [whole_ref[c][at : at + rows].astype(f32) for c in range(2)]
        qkv_ref[0, :rows, columns] = both_rows[0]
        qkv_ref[0, rows:, columns] = both_rows[1][: part_in - rows]
        out_ref[0, :, columns] = both_rows[1][part_in - rows :]


def reversed_bits(value, bits):
    return sum(((value >> b) & 1) << (bits - 1 - b) for b in range(bits))


def call(kernel, deps, args, in_specs, **options):
    skip = len(deps)
    return pl.pallas_call(
        lambda *refs: kernel(*refs[skip:]), in_specs=[ANY] * skip + in_specs, **options
    )(*deps, *args)


def build(dp_size, tensor_size):
    planes = dp_size // 2
    bits = planes.bit_length() - 1
    zbits = tensor_size.bit_length() - 1

    def send(arr, target):
        pairs = []
        for dp in range(dp_size):
            for z in range(tensor_size):
                to = target(dp >> 1, dp & 1, z)
                if to is not None:
                    plane, core, depth = to
                    pairs.append((dp * tensor_size + z, (plane * 2 + core) * tensor_size + depth))
        return lax.ppermute(arr, AXES, pairs)

    def other_core(p, c, z):
        return p, 1 - c, z

    def along(k):
        return lambda p, c, z: (p, c, z ^ k)

    def across(bit):
        return lambda p, c, z: (p ^ (1 << bit), c, z)

    def flip(step):
        return lambda p, c, z: (p ^ (1 << ((1 - step) if c else step)), c, z)

    def near_of(p, c, z):
        return p, c, z ^ (1 + c)

    def far_of(p, c, z):
        return (p, c, z ^ 3) if c else None

    def plane_gather(piece):
        one = send(piece, flip(0))
        two = send(piece, flip(1))
        return [piece, one, two, send(one, flip(1))]

    def per_device(
        tokens,
        cotangent,
        task_ids,
        key_mask,
        prompts,
        norm_gain,
        norm_bias,
        qkv_weight,
        qv_bias,
        out_weight,
        branch_bias,
        up_weight,
        up_bias,
        down_weight,
    ):
        group, rows_local, width = tokens.shape
        images = group // 2
        seq = rows_local * tensor_size
        in_rows = qkv_weight.shape[2]
        heads = in_rows // (3 * HEAD_DIM)
        out_rows = heads * HEAD_DIM
        inner = 2 * out_rows
        hidden = up_weight.shape[2]
        half_units = hidden // 2
        units = half_units * tensor_size
        wide, tall = width // QUARTERS, half_units // QUARTERS
        task_count = prompts.shape[1]
        per_dev = task_count // dp_size
        z = lax.axis_index(ALONG)
        core = lax.axis_index(AXES[2])
        quarter = lax.axis_index(AXES[1])
        plane = lax.axis_index(AXES[0]) * QUARTERS + quarter
        first_core = core == 0
        odd = z & 1
        all_rows = images * seq
        top = 64

        def pick(arr, index, axis):
            return lax.dynamic_index_in_dim(arr, index, axis, keepdims=False)

        def join(mine, theirs, axis):
            return jnp.where(
                first_core,
                jnp.concatenate([mine, theirs], axis),
                jnp.concatenate([theirs, mine], axis),
            )

        def image_pieces(deps, arr):
            return call(
                image_piece_kernel,
                deps,
                (info, arr),
                [SMEM, ANY],
                out_specs=[VMEM] * 2,
                out_shape=[out_of(images, rows_local, width)] * 2,
                scratch_shapes=[pltpu.SemaphoreType.DMA((2,))],
                cost_estimate=cost(0, 2 << 20),
            )

        def gather_images(one, two):
            got_one = send(one, lambda p, c, d: (p, d >> 1, 2 * c + (d & 1)))
            got_two = send(two, lambda p, c, d: (p, d >> 1, 2 * c + 1 - (d & 1)))
            return got_one, got_two, send(got_one, other_core), send(got_two, other_core)

        def spread_images(one, two):
            return [
                send(one, lambda p, c, d: (p, d >> 1, 2 * c + (d & 1))),
                send(two, lambda p, c, d: (p, d >> 1, 2 * c + 1 - (d & 1))),
            ]

        def in_order(got_one, got_two):
            return jnp.where(
                odd == 0,
                jnp.concatenate([got_one, got_two], 0),
                jnp.concatenate([got_two, got_one], 0),
            )

        ranks = [
            quarter ^ jnp.where(first_core, r, reversed_bits(r, 2)) for r in range(QUARTERS)
        ]
        info = jnp.stack([core, z] + ranks + [plane]).astype(jnp.int32)

        def exchange(parts):
            return (*parts, *(send(part, other_core) for part in parts))

        def out_of(*shape, dtype=bf16):
            return jax.ShapeDtypeStruct(shape, dtype)

        qkv_rows = qkv_weight.swapaxes(1, 2)
        by_task = prompts.swapaxes(1, 2).reshape(LAYERS, PROMPTS * task_count, width)

        def facts_table(deps):
            return call(
                facts_kernel,
                deps,
                (info, key_mask, task_ids),
                [SMEM, VMEM, VMEM],
                out_specs=VMEM,
                out_shape=out_of(8, 128, dtype=jnp.int32),
                cost_estimate=cost(0, 0),
            )

        def attn_piece(deps, layer):
            last = in_rows // 4 + out_rows // 4
            piece = call(
                functools.partial(attn_piece_kernel, layer),
                deps,
                (info, qkv_rows, out_weight, qv_bias),
                [SMEM, ANY, ANY, VMEM],
                out_specs=VMEM,
                out_shape=out_of(last + PAD, width),
                scratch_shapes=[pltpu.SemaphoreType.DMA((2,))],
                cost_estimate=cost(0, 3 << 20),
            )
            return [piece]

        def attn_stack(deps, near, far):
            stacked = call(
                stack_kernel,
                deps,
                (near, far),
                [ANY] * 2,
                out_specs=VMEM,
                out_shape=out_of(2, *near.shape),
                scratch_shapes=[pltpu.SemaphoreType.DMA((2,))],
                cost_estimate=cost(0, 0),
            )
            return [stacked]

        def mlp_piece(deps, layer):
            piece = call(
                functools.partial(mlp_piece_kernel, layer),
                deps,
                (info, up_weight, down_weight, up_bias),
                [SMEM, ANY, ANY, VMEM],
                out_specs=VMEM,
                out_shape=out_of(wide + 2 * tall + PAD, half_units),
                scratch_shapes=[pltpu.SemaphoreType.DMA((3,))],
                cost_estimate=cost(0, 1 << 20),
            )
            return [piece]

        def mlp_stack(deps, got):
            stacked = call(
                stack_kernel,
                deps,
                got,
                [ANY] * len(got),
                out_specs=VMEM,
                out_shape=out_of(len(got), *got[0].shape),
                scratch_shapes=[pltpu.SemaphoreType.DMA((len(got),))],
                cost_estimate=cost(0, 0),
            )
            return [stacked]

        def image_block(size):
            return pl.BlockSpec((1, seq, size), lambda i: (i, 0, 0))

        def fixed(*shape):
            return pl.BlockSpec(shape, lambda i: (0,) * len(shape))

        rows_w, rows_w32 = out_of(images, seq, width), out_of(images, seq, width, dtype=f32)
        wide_block = image_block(width)
        attn_scratch = [
            pltpu.VMEM((2 * in_rows, width), bf16),
            pltpu.VMEM((inner, width), bf16),
            pltpu.SemaphoreType.DMA((32,)),
        ]
        terms_held = pltpu.VMEM((2 * all_rows, width), bf16)
        terms_sems = pltpu.SemaphoreType.DMA((TERMS,))

        def parts_specs(count):
            return [fixed(all_rows // count, width)] * count

        def parts_shapes(count):
            return [out_of(all_rows // count, width)] * count

        bias_scratch = pltpu.VMEM((tensor_size - 1, PAD, half_units), bf16)
        three = fixed(LAYERS, 2, width)
        two_rows = pl.BlockSpec((1, rows_local, width), lambda i: (i, 0, 0))
        two_blocks = out_of(images, rows_local, width)
        mlp_scratch = [
            pltpu.VMEM((width, units), bf16),
            pltpu.VMEM((units, width), bf16),
            pltpu.SemaphoreType.DMA((64,)),
        ]
        mm = 2 * all_rows * width
        heads_flops = 2 * images * 2 * heads * seq * seq * 128

        def attn_forward(layer, deps, x, bufs):
            later = layer > 0
            return call(
                functools.partial(attn_forward_kernel, layer),
                deps,
                (*facts(), *x, by_task, norm_gain, norm_bias, branch_bias, qv_bias)
                + (qkv_rows, out_weight, *bufs),
                [SMEM] * 3
                + ([wide_block] + [ANY] * TERMS if later else [ANY] * 4)
                + [pl.BlockSpec((1, PROMPTS * task_count, width), lambda i: (layer, 0, 0))]
                + [three] * 3
                + [fixed(*qv_bias.shape)]
                + [ANY] * 6,
                grid=(images,),
                out_specs=[
                    wide_block,
                    wide_block,
                    image_block(2 * in_rows),
                    image_block(inner),
                    pl.BlockSpec((1, 8, seq), lambda i: (i, 0, 0)),
                ],
                out_shape=[
                    rows_w32,
                    rows_w,
                    out_of(images, seq, 2 * in_rows),
                    out_of(images, seq, inner),
                    out_of(images, 8, seq, dtype=f32),
                ],
                scratch_shapes=attn_scratch[:1]
                + [pltpu.VMEM((2, PAD, width), bf16), attn_scratch[2]]
                + [terms_held if later else pltpu.VMEM((images, seq, width), bf16)],
                compiler_params=params(LIMIT),
                cost_estimate=cost(mm * (3 * inner + inner) + 2 * heads_flops, 12 << 20, 1 << 20),
                name="attn_forward",
            )

        def attn_out(layer, deps, mixed, bufs):
            return call(
                functools.partial(attn_out_kernel, layer),
                deps,
                (info, mixed, qkv_rows, out_weight, *bufs),
                [SMEM, image_block(inner)] + [ANY] * 6,
                grid=(images,),
                out_specs=parts_specs(PARTS),
                out_shape=parts_shapes(PARTS),
                scratch_shapes=attn_scratch[1:],
                compiler_params=params(LIMIT),
                cost_estimate=cost(0, 0),
                name="attn_out",
            )

        def mlp_forward(layer, deps, xp, terms, bufs):
            return call(
                functools.partial(mlp_forward_kernel, layer),
                deps,
                (info, xp, *terms, norm_gain, norm_bias, branch_bias, up_bias)
                + (up_weight, down_weight, *bufs),
                [SMEM, wide_block] + [ANY] * TERMS + [three] * 3 + [fixed(*up_bias.shape)] + [ANY] * 6,
                grid=(images,),
                out_specs=[wide_block, wide_block, image_block(units), image_block(units)],
                out_shape=[
                    rows_w32,
                    rows_w,
                    out_of(images, seq, units),
                    out_of(images, seq, units),
                ],
                scratch_shapes=[mlp_scratch[0], mlp_scratch[2], bias_scratch, terms_held],
                compiler_params=params(LIMIT),
                cost_estimate=cost(mm * 2 * units, 18 << 20, 1 << 20),
                name="mlp_forward",
            )

        def mlp_turn(layer, deps, xp, terms, bufs, cot):
            return call(
                functools.partial(mlp_turn_kernel, layer),
                deps,
                (*facts(), xp, *terms, norm_gain, norm_bias, branch_bias, up_bias)
                + (up_weight, down_weight, *bufs, *cot),
                [SMEM] * 3 + [wide_block] + [ANY] * TERMS + [three] * 3 + [fixed(*up_bias.shape)] + [ANY] * 10,
                grid=(images,),
                out_specs=[
                    wide_block,
                    wide_block,
                    image_block(units),
                    wide_block,
                    image_block(units),
                    fixed(8, width),
                    fixed(8, units),
                ]
                + parts_specs(PARTS),
                out_shape=[
                    rows_w32,
                    rows_w,
                    out_of(images, seq, units),
                    rows_w,
                    out_of(images, seq, units),
                    out_of(8, width, dtype=f32),
                    out_of(8, units, dtype=f32),
                ]
                + parts_shapes(PARTS),
                scratch_shapes=mlp_scratch
                + [bias_scratch, pltpu.VMEM((images, seq, width), bf16), terms_held],
                compiler_params=params(LIMIT),
                cost_estimate=cost(mm * 3 * units, 20 << 20, 1 << 20),
                name="mlp_turn",
            )

        def mlp_out(layer, deps, act, bufs):
            return call(
                functools.partial(mlp_out_kernel, layer),
                deps,
                (info, act, down_weight, *bufs),
                [SMEM, image_block(units)] + [ANY] * 5,
                grid=(images,),
                out_specs=parts_specs(PARTS),
                out_shape=parts_shapes(PARTS),
                scratch_shapes=mlp_scratch[1:],
                compiler_params=params(LIMIT),
                cost_estimate=cost(mm * units, 8 << 20),
                name="mlp_out",
            )

        def mlp_backward(layer, deps, dx, slope, bufs):
            return call(
                functools.partial(mlp_backward_kernel, layer),
                deps,
                (info, dx, slope, up_weight, down_weight, *bufs),
                [SMEM, wide_block, image_block(units)] + [ANY] * 6,
                grid=(images,),
                out_specs=[wide_block, image_block(units), fixed(8, width), fixed(8, units)]
                + parts_specs(PARTS),
                out_shape=[
                    rows_w,
                    out_of(images, seq, units),
                    out_of(8, width, dtype=f32),
                    out_of(8, units, dtype=f32),
                ]
                + parts_shapes(PARTS),
                scratch_shapes=mlp_scratch,
                compiler_params=params(LIMIT),
                cost_estimate=cost(mm * 2 * units, 16 << 20),
                name="mlp_backward",
            )

        piece_rows = wide + 2 * tall

        def early(first, *rest, at=0):
            return pl.BlockSpec((first, 1, *rest), lambda k: (at, jnp.minimum(k, 1), 0, 0))

        def late(first, *rest, at=0):
            return pl.BlockSpec((first, 1, *rest), lambda k: (at, jnp.maximum(k - 2, 0), 0, 0))


        def mlp_weights(deps, c, dz, act, dh):
            flat = lambda arr: arr.reshape(all_rows, arr.shape[2])
            by_shard = pl.BlockSpec((all_rows, half_units), lambda k: (0, k))
            return call(
                mlp_weight_kernel,
                deps,
                (info, flat(c), flat(dz), flat(act), flat(dh)),
                [SMEM, fixed(all_rows, width), fixed(all_rows, width), by_shard, by_shard],
                grid=(tensor_size,),
                out_specs=[
                    early(2, piece_rows, half_units),
                    late(2, piece_rows, half_units),
                    pl.BlockSpec((1, piece_rows, half_units), lambda k: (k, 0, 0)),
                    pl.BlockSpec((1, piece_rows, half_units), lambda k: (k, 0, 0)),
                ],
                out_shape=[
                    out_of(2, tensor_size // 2, piece_rows, half_units),
                    out_of(2, tensor_size // 2, piece_rows, half_units),
                    out_of(tensor_size, piece_rows, half_units),
                    out_of(tensor_size, piece_rows, half_units),
                ],
                scratch_shapes=[
                    pltpu.VMEM((width, all_rows), bf16),
                    pltpu.VMEM((width, half_units), bf16),
                    pltpu.VMEM((half_units, width), bf16),
                ],
                compiler_params=params(LIMIT),
                cost_estimate=cost(mm * 2 * units, 14 << 20),
                name="mlp_weights",
            )

        def attn_backward(layer, deps, dx, terms, xm, qkv, lse, bufs):
            return call(
                functools.partial(attn_backward_kernel, layer),
                deps,
                (*facts(), dx, xm, norm_gain, qkv, lse, *terms)
                + (qkv_rows, out_weight, *bufs),
                [SMEM] * 3
                + [wide_block] * 2
                + [three, image_block(2 * in_rows)]
                + [pl.BlockSpec((1, 8, seq), lambda i: (i, 0, 0))]
                + [ANY] * (TERMS + 6),
                grid=(images,),
                out_specs=[
                    wide_block,
                    wide_block,
                    image_block(2 * in_rows),
                    fixed(8, width),
                    fixed(8, 2 * in_rows),
                ]
                + parts_specs(PARTS),
                out_shape=[
                    rows_w32,
                    rows_w,
                    out_of(images, seq, 2 * in_rows),
                    out_of(8, width, dtype=f32),
                    out_of(8, 2 * in_rows, dtype=f32),
                ]
                + parts_shapes(PARTS),
                scratch_shapes=attn_scratch + [terms_held],
                compiler_params=params(LIMIT),
                cost_estimate=cost(mm * (3 * inner + inner) + 5 * heads_flops, 15 << 20, 1 << 20),
                name="attn_backward",
            )

        attn_rows = in_rows // 4 + out_rows // 4

        def attn_weights(deps, a, dqkv, dy, mixed):
            flat = lambda arr: arr.reshape(all_rows, arr.shape[2])
            return call(
                attn_weight_kernel,
                deps,
                (info, flat(a), flat(dqkv), flat(dy), flat(mixed)),
                [SMEM] + [VMEM] * 4,
                out_specs=[VMEM] * 3,
                out_shape=[
                    out_of(2, 2, attn_rows, width),
                    out_of(2, attn_rows, width),
                    out_of(2, attn_rows, width),
                ],
                scratch_shapes=[
                    pltpu.VMEM((2 * in_rows, width), bf16),
                    pltpu.VMEM((inner, width), bf16),
                ],
                compiler_params=params(LIMIT),
                cost_estimate=cost(mm * (3 * inner + inner), 10 << 20),
                name="attn_weights",
            )

        def norm_backward(layer, deps, mid, terms, xp):
            return call(
                functools.partial(norm_backward_kernel, layer),
                deps,
                (info, mid, xp, norm_gain, *terms),
                [SMEM] + [wide_block] * 2 + [three] + [ANY] * TERMS,
                grid=(images,),
                out_specs=([wide_block] if layer else [two_rows] * 2)
                + [pl.BlockSpec((1, top, width), lambda i: (i, 0, 0)), fixed(8, width)],
                out_shape=([rows_w32] if layer else [two_blocks] * 2)
                + [out_of(images, top, width, dtype=f32), out_of(8, width, dtype=f32)],
                scratch_shapes=([] if layer else [pltpu.VMEM((seq, width), bf16)])
                + [terms_held, terms_sems],
                compiler_params=params(LIMIT),
                cost_estimate=cost(20 * all_rows * width, 9 << 20),
                name="norm_backward",
            )

        def out_pieces(deps, xm, terms):
            return call(
                out_kernel,
                deps,
                (*facts(), xm, branch_bias, *terms),
                [SMEM] * 3 + [wide_block, three] + [ANY] * TERMS,
                grid=(images,),
                out_specs=[two_rows] * 2,
                out_shape=[two_blocks] * 2,
                scratch_shapes=[pltpu.VMEM((seq, width), bf16), terms_held, terms_sems],
                compiler_params=params(LIMIT),
                cost_estimate=cost(0, 0),
            )

        def finish(layer, deps, whole, before):
            return call(
                finish_kernel,
                deps,
                (info, whole, send(whole, other_core), *before),
                [SMEM]
                + [pl.BlockSpec((1,) + whole.shape[1:], lambda q: (q, 0, 0))] * 2
                + [ANY] * len(before),
                grid=(QUARTERS,),
                out_specs=[
                    pl.BlockSpec((1, wide, hidden), lambda q: (layer, q, 0)),
                    pl.BlockSpec((1, 2, 1, tall, width), lambda q: (layer, 0, q, 0, 0)),
                    pl.BlockSpec((1, in_rows // QUARTERS, width), lambda q: (layer, q, 0)),
                    pl.BlockSpec((1, out_rows // QUARTERS, width), lambda q: (layer, q, 0)),
                ],
                out_shape=[
                    out_of(LAYERS, width, hidden, dtype=f32),
                    out_of(LAYERS, 2, QUARTERS, tall, width, dtype=f32),
                    out_of(LAYERS, in_rows, width, dtype=f32),
                    out_of(LAYERS, out_rows, width, dtype=f32),
                ],
                input_output_aliases={len(deps) + 3 + i: i for i in range(len(before))},
                compiler_params=params(LIMIT),
                cost_estimate=cost(0, 0),
                name="finish",
            )

        def pack(deps, mine, got, units_sum):
            rows = units_sum.shape[0] + 2 * mine.shape[0]
            return call(
                pack_kernel,
                deps,
                (mine, got, units_sum),
                [VMEM] * 3,
                out_specs=VMEM,
                out_shape=out_of(rows, half_units),
                compiler_params=params(LIMIT),
                cost_estimate=cost(0, 0),
            )

        def add_two(deps, s2, got):
            grid = s2.shape[0]
            block = (1,) + s2.shape[1:]
            return call(
                lambda a, b, o: add_two_kernel(a, b.at[0], o),
                deps,
                (s2, got),
                [
                    pl.BlockSpec(block, lambda i: (i, 0, 0)),
                    pl.BlockSpec((1,) + block, lambda i: (1, i, 0, 0)),
                ],
                grid=(grid,),
                out_specs=pl.BlockSpec(block, lambda i: (i, 0, 0)),
                out_shape=out_of(*s2.shape),
                compiler_params=params(LIMIT),
                cost_estimate=cost(0, 0),
                name="add_two",
            )

        def mlp_two(deps, s2, got):
            block = (1,) + s2.shape[1:]
            return call(
                mlp_two_kernel,
                deps,
                (s2, *got),
                [
                    pl.BlockSpec(block, lambda i: (i, 0, 0)),
                    early(1, *s2.shape[1:], at=1),
                    late(1, *s2.shape[1:], at=1),
                ],
                grid=(tensor_size,),
                out_specs=pl.BlockSpec(block, lambda i: (i, 0, 0)),
                out_shape=out_of(*s2.shape),
                compiler_params=params(LIMIT),
                cost_estimate=cost(0, 0),
                name="mlp_two",
            )

        def mlp_add(deps, keep, got, last):
            block = (1,) + keep.shape[1:]
            piece = keep.shape[1:]
            return call(
                mlp_add_kernel,
                deps,
                (keep, *got, last),
                [
                    pl.BlockSpec(block, lambda i: (i, 0, 0)),
                    early(1, *piece),
                    late(1, *piece),
                    pl.BlockSpec(block, lambda i: (i, 0, 0)),
                ],
                grid=(tensor_size,),
                out_specs=[fixed(*piece)] * tensor_size,
                out_shape=[out_of(*piece, dtype=f32)] + [out_of(*piece)] * (tensor_size - 1),
                compiler_params=params(LIMIT),
                cost_estimate=cost(0, 0),
                name="mlp_add",
            )

        def attn_add(deps, keep, got, last):
            piece = keep.shape[1:]
            return call(
                attn_add_kernel,
                deps,
                (keep, got, last),
                [
                    fixed(*keep.shape),
                    pl.BlockSpec((1,) + keep.shape, lambda i: (0, 0, 0, 0)),
                    fixed(*keep.shape),
                ],
                grid=(1,),
                out_specs=[fixed(*piece)] * 3,
                out_shape=[out_of(*piece, dtype=f32)] + [out_of(*piece)] * 2,
                compiler_params=params(LIMIT),
                cost_estimate=cost(0, 0),
                name="attn_add",
            )

        def attn_merge(deps, own, near, far):
            half = (own.shape[0] // 2,) + own.shape[1:]
            return call(
                attn_merge_kernel,
                deps,
                (info, own, near, far),
                [SMEM] + [VMEM] * 3,
                out_specs=[VMEM] * 2,
                out_shape=[out_of(*half, dtype=f32), out_of(*half)],
                compiler_params=params(LIMIT),
                cost_estimate=cost(0, 0),
                name="attn_merge",
            )

        def add_up(deps, own, *others, dtype=bf16):
            return call(
                sum_kernel,
                deps,
                (own, *others),
                [VMEM] * (1 + len(others)),
                out_specs=VMEM,
                out_shape=out_of(*own.shape, dtype=dtype),
                compiler_params=params(LIMIT),
                cost_estimate=cost(0, 0),
            )

        def prompt_rows_of(layer, deps, at):
            return call(
                functools.partial(prompt_kernel, layer, per_dev),
                deps,
                (*facts(), at),
                [SMEM] * 3 + [VMEM],
                out_specs=VMEM,
                out_shape=out_of(planes, per_dev * top, width),
                compiler_params=params(LIMIT),
                cost_estimate=cost(0, 0),
            )

        def row_sums(deps, sums):
            return call(
                sums_kernel,
                deps,
                (info, *sums),
                [SMEM] + [VMEM] * len(sums),
                out_specs=VMEM,
                out_shape=out_of(12 * LAYERS, width, dtype=f32),
                compiler_params=params(LIMIT),
                cost_estimate=cost(0, 0),
            )

        def tail_first(deps, parts, flat, got):
            rows = LAYERS * per_dev * top + flat.shape[0]
            return call(
                functools.partial(tail_first_kernel, planes),
                deps,
                (*parts, flat, got),
                [VMEM] * (len(parts) + 2),
                out_specs=[VMEM] * planes,
                out_shape=[out_of(rows, width, dtype=f32)] + [out_of(rows, width)] * (planes - 1),
                compiler_params=params(LIMIT),
                cost_estimate=cost(0, 0),
            )

        def tail_middle(deps, own, got):
            rows, block = own.shape[0], width // tensor_size
            return call(
                functools.partial(tail_middle_kernel, tensor_size),
                deps,
                (info, own, *got),
                [SMEM] + [VMEM] * (1 + len(got)),
                out_specs=[VMEM] * tensor_size,
                out_shape=[out_of(rows, block, dtype=f32)]
                + [out_of(rows, block)] * (tensor_size - 1),
                compiler_params=params(LIMIT),
                cost_estimate=cost(0, 0),
            )

        def collect(deps, piece):
            return call(
                collect_kernel,
                deps,
                (info, *plane_gather(piece)),
                [SMEM] + [ANY] * QUARTERS,
                out_specs=VMEM,
                out_shape=out_of(QUARTERS, *piece.shape),
                scratch_shapes=[pltpu.SemaphoreType.DMA((QUARTERS,))],
                compiler_params=params(LIMIT),
                cost_estimate=cost(0, 0),
            )

        out, sent, last = {}, {}, []

        def once(name, make):
            if name not in sent:
                sent[name] = make()
            return sent[name]

        def moved(name, arr, target):
            return once(name, lambda: send(arr, target))

        def terms(name):
            parts = out[name][-PARTS:]
            return once("e>" + name, lambda: exchange(parts))

        def pair_z(name):
            near, far = out[name][1], out[name][2]
            return moved(name + ">n", near, near_of), moved(name + ">f", far, far_of)

        def shards(name, first):
            pieces = out[name][first:]
            return [moved("%s>%d" % (name, k), p, along(k + 1)) for k, p in enumerate(pieces)]

        def bufs(name):
            return once("b>" + name, lambda: plane_gather(out[name][0]))

        def facts():
            return info, out["facts"][0], moved("facts>", out["facts"][0], other_core)

        def x_of(name):
            return once("x>" + name, lambda: gather_images(*out[name]))

        def near_far(name):
            piece = out[name][0]
            return moved(name + ">n", piece, near_of), moved(name + ">f", piece, far_of)

        def stack_mlp(deps, name):
            piece = out[name][0]
            got = [moved("%s>%d" % (name, k), piece, along(k)) for k in range(1, tensor_size)]
            return mlp_stack(deps, got)

        def spread(name):
            return once("spread>" + name, lambda: spread_images(*out[name][:2]))

        def s1(name):
            if name[0] == "a":
                return moved("one>" + name, out["w" + name][0], flip(0))
            return [moved("one%d>%s" % (i, name), out["w" + name][i], flip(0)) for i in range(2)]

        def last_of(name):
            return moved("two>" + name, out["t" + name][0], flip(1))

        def forward_0(deps):
            return attn_forward(0, deps, x_of("tok"), bufs("sa0"))

        def forward_1(deps):
            return attn_forward(1, deps, (out["fm0"][0], *terms("om0")), bufs("sa1"))

        def mlp_0(deps):
            return mlp_forward(0, deps, out["fa0"][0], terms("oa0"), bufs("sm0"))

        def turn_1(deps):
            return mlp_turn(1, deps, out["fa1"][0], terms("oa1"), bufs("sm1"), x_of("cot"))

        def weights_m1(deps):
            return mlp_weights(deps, *(out["turn"][i] for i in (1, 3, 2, 4)))

        def weights_m0(deps):
            return mlp_weights(deps, out["fm0"][1], out["bm0"][0], out["fm0"][2], out["bm0"][1])

        def backward_a1(deps):
            _, _, qkv, _, lse = out["fa1"]
            dz, xm = out["turn"][3], out["turn"][0]
            return attn_backward(1, deps, dz, terms("turn"), xm, qkv, lse, bufs("sa1"))

        def backward_a0(deps):
            _, _, qkv, _, lse = out["fa0"]
            xm, dx = out["fm0"][0], out["nb1"][0]
            return attn_backward(0, deps, dx, terms("bm0"), xm, qkv, lse, bufs("sa0"))

        def weights_a(deps, layer):
            forward, back = out["fa%d" % layer], out["ba%d" % layer]
            return attn_weights(deps, forward[1], back[2], back[1], forward[3])

        def norm_b(deps, layer):
            back = out["ba%d" % layer]
            return norm_backward(layer, deps, back[0], terms("ba%d" % layer), out["fa%d" % layer][0])

        def two(deps, name):
            add = mlp_two if name[0] == "m" else add_two
            return [add(deps, out["w" + name][-2], s1(name))]

        def z_add(deps, name):
            add = mlp_add if name[0] == "m" else attn_add
            return add(deps, out["w" + name][-1], s1(name), last_of(name))

        def over_groups(arr):
            for b in range(2, bits):
                arr = (arr.astype(f32) + send(arr, across(b)).astype(f32)).astype(bf16)
            return [arr]

        def z_sum(deps, name):
            return [add_up(deps, out["z" + name][0], *shards("z" + name, 1))]

        def merge(deps, name):
            return attn_merge(deps, out["z" + name][0], *pair_z("z" + name))

        def pack_of(deps, layer):
            mine, theirs = out["ra%d" % layer]
            got = moved("core>%d" % layer, theirs, other_core)
            return over_groups(pack(deps, mine, got, out["hm%d" % layer][0]))

        def sums_of(deps):
            sums = ()
            for layer, mlp in ((0, "bm0"), (1, "turn")):
                sum_mlp, upb = (out[mlp][2], out[mlp][3]) if layer == 0 else out[mlp][5:7]
                back = out["ba%d" % layer]
                sums += (out["nb%d" % layer][-1], back[3], sum_mlp, upb, back[4])
            return [row_sums(deps, sums)]

        def tail_one(deps):
            flat = out["rs"][0]
            parts = [out["pr0"][0], out["pr1"][0]]
            return tail_first(deps, parts, flat, moved("flat>", flat, other_core))

        def tail_two(deps):
            parts = out["tf"]
            got = [
                moved("tf>%d" % r, parts[r], lambda p, c, d, r=r: (p ^ r, c, d))
                for r in range(1, planes)
            ]
            return tail_middle(deps, parts[0], got)

        def tail_end(deps):
            got = shards("tm", 1)
            block = width // tensor_size
            shapes = [(LAYERS, per_dev, PROMPTS, block)] + [(LAYERS, 2, block)] * 3
            shapes += [(LAYERS, hidden), (LAYERS, 2 * out_rows)]
            return call(
                functools.partial(tail_end_kernel, per_dev),
                deps,
                (out["tm"][0], *got),
                [VMEM] * (1 + len(got)),
                out_specs=[VMEM] * len(shapes),
                out_shape=[out_of(*shape, dtype=f32) for shape in shapes],
                compiler_params=params(LIMIT),
                cost_estimate=cost(0, 0),
            )

        steps = {
            "facts": lambda d: [facts_table(d)],
            "tok": lambda d: image_pieces(d, tokens),
            "cot": lambda d: image_pieces(d, cotangent),
            "pa0": lambda d: attn_piece(d, 0),
            "pa1": lambda d: attn_piece(d, 1),
            "pm0": lambda d: mlp_piece(d, 0),
            "pm1": lambda d: mlp_piece(d, 1),
            "sa0": lambda d: attn_stack(d, *near_far("pa0")),
            "sa1": lambda d: attn_stack(d, *near_far("pa1")),
            "sm0": lambda d: stack_mlp(d, "pm0"),
            "sm1": lambda d: stack_mlp(d, "pm1"),
            "fa0": forward_0,
            "oa0": lambda d: attn_out(0, d, out["fa0"][3], bufs("sa0")),
            "fm0": mlp_0,
            "om0": lambda d: mlp_out(0, d, out["fm0"][2], bufs("sm0")),
            "fa1": forward_1,
            "oa1": lambda d: attn_out(1, d, out["fa1"][3], bufs("sa1")),
            "turn": turn_1,
            "wm1": weights_m1,
            "ba1": backward_a1,
            "wa1": lambda d: weights_a(d, 1),
            "nb1": lambda d: norm_b(d, 1),
            "tm1": lambda d: two(d, "m1"),
            "bm0": lambda d: mlp_backward(0, d, out["nb1"][0], out["fm0"][3], bufs("sm0")),
            "ta1": lambda d: two(d, "a1"),
            "wm0": weights_m0,
            "zm1": lambda d: z_add(d, "m1"),
            "za1": lambda d: z_add(d, "a1"),
            "ba0": backward_a0,
            "hm1": lambda d: z_sum(d, "m1"),
            "ra1": lambda d: merge(d, "a1"),
            "ca1": lambda d: pack_of(d, 1),
            "wa0": lambda d: weights_a(d, 0),
            "tm0": lambda d: two(d, "m0"),
            "nb0": lambda d: norm_b(d, 0),
            "rs": sums_of,
            "pr0": lambda d: [prompt_rows_of(0, d, out["nb0"][2])],
            "pr1": lambda d: [prompt_rows_of(1, d, out["nb1"][1])],
            "ta0": lambda d: two(d, "a0"),
            "zm0": lambda d: z_add(d, "m0"),
            "za0": lambda d: z_add(d, "a0"),
            "hm0": lambda d: z_sum(d, "m0"),
            "ra0": lambda d: merge(d, "a0"),
            "ca0": lambda d: pack_of(d, 0),
            "co1": lambda d: [collect(d, out["ca1"][0])],
            "co0": lambda d: [collect(d, out["ca0"][0])],
            "fi1": lambda d: finish(1, d, out["co1"][0], ()),
            "fi0": lambda d: finish(0, d, out["co0"][0], out["fi1"]),
            "tf": tail_one,
            "tm": tail_two,
            "te": tail_end,
            "om1": lambda d: mlp_out(1, d, out["turn"][2], bufs("sm1")),
            "op": lambda d: out_pieces(d, out["turn"][0], terms("om1")),
        }
        arrivals = {
            "f": lambda name: [facts()[2]],
            "o": spread,
            "t": lambda name: shards("tm", 1),
            "x": lambda name: x_of(name)[:2],
            "y": lambda name: x_of(name)[2:],
            "p": near_far,
            "1": lambda name: [bufs(name)[1]],
            "2": lambda name: [bufs(name)[2]],
            "3": lambda name: [bufs(name)[3]],
            "e": lambda name: terms(name)[PARTS:],
            "s": lambda name: [s1(name)],
            "l": lambda name: [last_of(name)],
            "z": lambda name: shards("z" + name, 1),
            "q": lambda name: pair_z("z" + name),
        }
        for name in " ".join(ORDER).split():
            if name[0] == "<":
                last += jax.tree.leaves(arrivals[name[1]](name[3:]))
                continue
            out[name] = steps[name](tuple(last))
            last = [out[name][0]]

        full_up, full_down, full_qkv, full_out = out["fi0"]
        grad_tokens = in_order(*spread("nb0"))
        out_rows_sent = in_order(*spread("op"))
        grad_prompts, grad_gain, grad_bias, grad_branch, grad_upb, grad_pair = out["te"]
        full_qkv = full_qkv.swapaxes(1, 2)
        return (
            out_rows_sent,
            grad_tokens,
            grad_prompts,
            grad_gain,
            grad_bias,
            full_qkv,
            grad_pair,
            full_out,
            grad_branch,
            full_up,
            grad_upb,
            full_down.reshape(LAYERS, hidden, width),
        )

    return per_device


def solution(mesh):
    dp_size, tensor_size = mesh.shape["dp"], mesh.shape[ALONG]
    shape = (dp_size // (2 * QUARTERS), QUARTERS, 2, tensor_size)
    mesh = jax.sharding.Mesh(mesh.devices.reshape(shape), AXES)
    dp = AXES[:3]
    placed = (
        P(dp, ALONG, None),
        P(dp, ALONG, None),
        P(dp, None),
        P(dp, None),
        P(),
        P(),
        P(),
        P(None, None, ALONG),
        P(None, ALONG),
        P(None, ALONG, None),
        P(),
        P(None, None, ALONG),
        P(None, ALONG),
        P(None, ALONG, None),
    )
    return jax.shard_map(
        build(dp_size, tensor_size),
        mesh=mesh,
        in_specs=placed,
        out_specs=(
            P(dp, ALONG, None),
            P(dp, ALONG, None),
            P(None, dp, None, ALONG),
            P(None, None, ALONG),
            P(None, None, ALONG),
            P(None, None, ALONG),
            P(None, ALONG),
            P(None, ALONG, None),
            P(None, None, ALONG),
            P(None, None, ALONG),
            P(None, ALONG),
            P(None, ALONG, None),
        ),
        check_vma=False,
    )
```

```python
import functools

import jax
import jax.numpy as jnp
from jax import lax
from jax.experimental import pallas as pl
from jax.experimental.pallas import tpu as pltpu
from jax.sharding import PartitionSpec as P

HEAD_DIM = 64
LAYERS = 2
PROMPTS = 50
QUARTERS = 4
PAD = 16
LIMIT = 50
PARTS = 2
TERMS = 2 * PARTS
ORDER = (
    "pa0 pm0 tok facts",
    "sa0 pa1 pm1 sm0",
    "fa0 sa1 oa0 cot",
    "fm0 <1.sa1 sm1 om0",
    "fa1 oa1 turn wm1",
    "ba1 wa1 nb1 tm1",
    "bm0 ta1 wm0 zm1",
    "za1 ba0 hm1 wa0",
    "tm0 <s.m0 ra1 nb0",
    "ca1 rs pr0 pr1",
    "zm0 <o.nb0 ta0 tf",
    "om1 za0 op hm0",
    "ra0 ca0 co1 tm",
    "<o.op te fi1 co0",
    "fi0",
)
AXES = ("group", "quarter", "core", "tensor")
ALONG = AXES[3]
START, WAIT = 1, 2
epsilon = 1e-06
bf16 = jnp.bfloat16
f32 = jnp.float32
ANY = pl.BlockSpec(memory_space=pl.ANY)
SMEM = pl.BlockSpec(memory_space=pltpu.SMEM)
VMEM = pl.BlockSpec(memory_space=pltpu.VMEM)
NEGATIVE = -1000000000.0


def nn(left, right):
    return lax.dot_general(left, right, (((1,), (0,)), ((), ())), preferred_element_type=f32)


def nt(left, right):
    return lax.dot_general(left, right, (((1,), (1,)), ((), ())), preferred_element_type=f32)


def turn(arr):
    return arr.astype(f32).T.astype(bf16)


def norm_parts(rows):
    centre = rows - jnp.mean(rows, axis=-1, keepdims=True)
    spread = jnp.mean(centre * centre, axis=-1, keepdims=True)
    scale = lax.rsqrt(spread + epsilon)
    return centre * scale, scale


def norm_back(hat, scale, gain, grad):
    inner = grad * gain
    along = jnp.mean(inner * hat, axis=-1, keepdims=True)
    return scale * (inner - jnp.mean(inner, axis=-1, keepdims=True) - hat * along)


def gate_pair(pre):
    size = jnp.abs(pre)
    below = 1.0 + 0.2316418882 * size
    t = pl.reciprocal(below, approx=True)
    t = t * (2.0 - below * t)
    bell = jnp.exp(-0.5 * pre * pre)
    poly = 0.5307027145 * t - 0.7265760135
    poly = poly * t + 0.7107068705
    poly = poly * t - 0.142248368
    poly = poly * t + 0.127414796
    rest = poly * t * bell
    below = jnp.where(pre >= 0.0, 1.0 - rest, rest)
    return pre * below, below + pre * bell * 0.3989422804014327


def cost(flops, size, trans=0):
    return pl.CostEstimate(flops=1, bytes_accessed=1, transcendentals=0)


def params(mib):
    return pltpu.CompilerParams(vmem_limit_bytes=mib << 20)


def fetch(copies, sems, first=0, phase=None):
    made = [pltpu.make_async_copy(src, dst, sems.at[first + i]) for i, (src, dst) in enumerate(copies)]
    if phase != WAIT:
        for copy in made:
            copy.start()
    if phase != START:
        for copy in made:
            copy.wait()


def rows16(start, size):
    return pl.ds(pl.multiple_of(start, 16), size)


def fact(info, mine, theirs, image, column):
    return jnp.where(info[0] == (info[1] >> 1), mine[image, column], theirs[image, column])


def attn_fetch(layer, info, own_qkv, own_out, bufs, w_qkv, w_out, sems, phase=None):
    own_qkv, own_out = own_qkv.at[layer], own_out.at[layer]
    near, far = [buf.at[0] for buf in bufs], [buf.at[1] for buf in bufs]
    rows_in, rows_out = own_qkv.shape[0], own_out.shape[0]
    part_in, part_out = rows_in // QUARTERS, rows_out // QUARTERS

    def pieces(bufs, block):
        copies = []
        for i in range(QUARTERS):
            quarter = info[2 + i]
            src = bufs[i]
            if w_qkv is not None:
                rows = rows16(block * rows_in + part_in * quarter, part_in)
                copies.append((src.at[pl.ds(0, part_in)], w_qkv.at[rows]))
            if w_out is not None:
                rows = rows16(block * rows_out + part_out * quarter, part_out)
                copies.append((src.at[pl.ds(part_in, part_out)], w_out.at[rows]))
        return copies

    @pl.when(info[0] == 0)
    def _():
        own = []
        if w_qkv is not None:
            own.append((own_qkv, w_qkv.at[pl.ds(0, rows_in)]))
        if w_out is not None:
            own.append((own_out, w_out.at[pl.ds(0, rows_out)]))
        fetch(own + pieces(near, 1), sems, 0, phase)

    @pl.when(info[0] != 0)
    def _():
        fetch(pieces(far, 0) + pieces(near, 1), sems, 0, phase)


def mlp_fetch(
    layer, info, own_up, own_down, bufs, w_up, w_down, sems, bias_rows=None, phase=None
):
    own_down = own_down.at[layer]
    width = own_down.shape[1]
    half = own_down.shape[0] // 2
    wide, tall = width // QUARTERS, half // QUARTERS
    split = width // 2
    start = info[0] * half
    copies = []
    if w_down is not None:
        copies.append((own_down.at[rows16(start, half)], w_down.at[pl.ds(0, half)]))
    if bias_rows is not None:
        last = bufs[0].shape[1] - PAD
        copies.append((bufs[0].at[:, pl.ds(last, PAD), :], bias_rows))
    if own_up is not None:
        columns = pl.ds(pl.multiple_of(start, 128), half)
        copies.append((own_up.at[layer, :, columns], w_up.at[:, pl.ds(0, half)]))
    for i in range(QUARTERS):
        quarter = info[2 + i]
        for k in range(bufs[i].shape[0]):
            src = bufs[i].at[k]
            units = rows16((k + 1) * half + tall * quarter, tall)
            if own_up is not None:
                columns = pl.ds((k + 1) * half, half)
                copies.append(
                    (src.at[pl.ds(0, wide)], w_up.at[rows16(wide * quarter, wide), columns])
                )
            if w_down is not None:
                lower = src.at[pl.ds(wide + tall, tall)]
                copies.append((src.at[pl.ds(wide, tall)], w_down.at[units, pl.ds(0, split)]))
                copies.append((lower, w_down.at[units, pl.ds(split, split)]))
    fetch(copies, sems, 0, phase)


def unit_bias(layer, info, bias_ref, bias_rows, k):
    half = bias_ref.shape[1] // 2
    if k == 0:
        one, two = bias_ref[layer : layer + 1, :half], bias_ref[layer : layer + 1, half:]
    else:
        one, two = bias_rows[k - 1, 0:1, :], bias_rows[k - 1, 1:2, :]
    return jnp.where(info[0] == 0, one, two).astype(f32)


def fetch_parts(refs, held, sems, first=0):
    size = refs[0].shape[0]
    fetch([(ref, held.at[pl.ds(i * size, size)]) for i, ref in enumerate(refs)], sems, first)


def both(held, step):
    half = held.shape[0] // 2
    rows = half // 3
    start = pl.multiple_of(rows * step, 16)
    return held[pl.ds(start, rows), :].astype(f32) + held[pl.ds(half + start, rows), :].astype(f32)


def put_part(refs, step, value):
    rows, size = value.shape[0], refs[0].shape[0]
    for i in range(size * len(refs) // rows):

        @pl.when(step == i)
        def _(i=i):
            done = 0
            while done < rows:
                ref, at = divmod(i * rows + done, size)
                count = min(rows - done, size - at)
                refs[ref][at : at + count, :] = value[done : done + count]
                done += count


def head_masks(rows, cols, axis):
    place = lax.broadcasted_iota(jnp.int32, (rows, cols), axis)
    return place < HEAD_DIM


def image_copies(info, bufs, rows):
    block = bufs[0].shape[1]
    core, odd = info[0], info[1] & 1
    places = [2 * core + odd, 2 * core + 1 - odd, 2 * (1 - core) + odd, 2 * (1 - core) + 1 - odd]
    return [
        (bufs[i], rows.at[:, rows16(block * places[i], block), :]) for i in range(len(bufs))
    ]


def attn_forward_kernel(layer, info, mine, theirs, *refs):
    later = layer > 0
    x_refs = refs[: 1 + TERMS if later else 4]
    refs = refs[len(x_refs) :]
    prompt_ref, gain_ref, shift_ref, branch_ref, bias_ref, own_qkv, own_out = refs[:7]
    bufs = refs[7:11]
    xp_ref, a_ref, qkv_ref, mix_ref, lse_ref = refs[11:16]
    w_qkv, bias_rows, sems, held = refs[16:20]
    step = pl.program_id(0)

    @pl.when(step == 0)
    def _():
        attn_fetch(layer, info, own_qkv, own_out, bufs, w_qkv, None, sems, START)
        last = bufs[0].shape[1] - PAD
        fetch([(bufs[0].at[:, pl.ds(last, PAD)], bias_rows)], sems, 24)
        if later:
            fetch_parts(x_refs[1:], held, sems, 25)
        else:
            fetch(image_copies(info, x_refs, held), sems, 25)

    if later:
        after = branch_ref[layer - 1, 1:2, :].astype(f32)
        rows = x_refs[0][0] + (both(held, step) + after)
    else:
        rows = held[step].astype(f32)
    top = 64
    places, tasks = prompt_ref.shape[1], prompt_ref.shape[1] // PROMPTS
    place = lax.broadcasted_iota(jnp.int32, (top, places), 0)
    entry = lax.broadcasted_iota(jnp.int32, (top, places), 1)
    task = fact(info, mine, theirs, step, 1 + layer)
    hot = (entry == (place - 1) * tasks + task) & (place >= 1) & (place <= PROMPTS)
    placed = nn(jnp.where(hot, 1.0, 0.0).astype(bf16), prompt_ref[0])
    place = lax.broadcasted_iota(jnp.int32, placed.shape, 0)
    here = (place >= 1) & (place <= PROMPTS)
    rows = jnp.concatenate([jnp.where(here, placed, rows[:top]), rows[top:]], axis=0)
    xp_ref[0] = rows
    hat, _ = norm_parts(rows)
    gain, shift = gain_ref[layer, 0:1, :].astype(f32), shift_ref[layer, 0:1, :].astype(f32)
    normed = (hat * gain + shift).astype(bf16)
    a_ref[0] = normed

    @pl.when(step == 0)
    def _():
        attn_fetch(layer, info, own_qkv, own_out, bufs, w_qkv, None, sems, WAIT)

    qkv = nt(normed, w_qkv[...])
    size = bias_ref.shape[1]
    first = jnp.where(info[0] == 0, bias_ref[layer : layer + 1, :], bias_rows[1, 0:1, :size]).astype(f32)
    lines = jnp.concatenate([first, bias_rows[0, 0:1, :size].astype(f32)], axis=1)
    low_line = head_masks(1, 128, 1)
    seq = rows.shape[0]
    low = head_masks(seq, 128, 1)
    low_t = head_masks(128, seq, 0)
    valid = lax.broadcasted_iota(jnp.int32, (seq, seq), 0) < fact(info, mine, theirs, step, 0)
    pairs = w_qkv.shape[0] // 384
    for p in range(pairs):
        blocks = [qkv[:, 384 * p + 128 * j : 384 * p + 128 * (j + 1)] for j in range(3)]
        one, two = (lines[:, 256 * p + 128 * h : 256 * p + 128 * (h + 1)] for h in range(2))
        turned = [
            pltpu.roll(jnp.broadcast_to(line, (8, 128)), HEAD_DIM, 1)[0:1] for line in (one, two)
        ]
        none = jnp.zeros_like(one)
        biases = [
            jnp.where(low_line, one, none),
            jnp.where(low_line, turned[0], turned[1]),
            jnp.where(low_line, none, two),
        ]
        blocks = [block + bias for block, bias in zip(blocks, biases)]
        scale = HEAD_DIM**-0.5
        blocks[0] = blocks[0] * jnp.where(low_line, scale, 1.0)
        blocks[1] = blocks[1] * jnp.where(low_line, 1.0, scale)
        query = jnp.where(low, blocks[0], blocks[1]).astype(bf16)
        key = pltpu.roll(jnp.where(low, blocks[2], blocks[0]), HEAD_DIM, 1).astype(bf16)
        value_t = jnp.where(low, blocks[1], blocks[2])
        qkv_ref[0, :, 384 * p : 384 * p + 128] = query
        qkv_ref[0, :, 384 * p + 128 : 384 * p + 256] = key
        qkv_ref[0, :, 384 * p + 256 : 384 * p + 384] = value_t.astype(bf16)
        value_t = value_t.T.astype(bf16)
        outs = []
        for h in range(2):
            lanes = low if h == 0 else jnp.logical_not(low)
            one_key = jnp.where(lanes, key, jnp.zeros_like(key))
            scores = jnp.where(valid, nt(one_key, query), NEGATIVE)
            peak = jnp.max(scores, axis=0, keepdims=True)
            exps = jnp.exp(scores - peak)
            total = jnp.sum(exps, axis=0, keepdims=True)
            lse_ref[0, 2 * p + h : 2 * p + h + 1, :] = peak + jnp.log(total)
            outs.append(nn(value_t, exps.astype(bf16)) * (1.0 / total))
        mixed = jnp.where(low_t, outs[0], outs[1]).T.astype(bf16)
        mix_ref[0, :, 128 * p : 128 * (p + 1)] = mixed


def attn_out_kernel(layer, info, mix_ref, own_qkv, own_out, *refs):
    bufs, parts, w_out, sems = refs[:4], refs[4:-2], refs[-2], refs[-1]
    step = pl.program_id(0)

    @pl.when(step == 0)
    def _():
        attn_fetch(layer, info, own_qkv, own_out, bufs, None, w_out, sems)

    put_part(parts, step, nn(mix_ref[0], w_out[...]).astype(bf16))


def mlp_start(layer, xp_ref, total, gain_ref, shift_ref, branch_ref, xm_ref, c_ref):
    before = branch_ref[layer, 0:1, :].astype(f32)
    rows = xp_ref[0] + (total + before)
    xm_ref[0] = rows
    hat, _ = norm_parts(rows)
    gain, shift = gain_ref[layer, 1:2, :].astype(f32), shift_ref[layer, 1:2, :].astype(f32)
    normed = (hat * gain + shift).astype(bf16)
    c_ref[0] = normed
    return normed


def split_refs(refs):
    return refs[1 + TERMS : 4 + TERMS], *refs[4 + TERMS : 7 + TERMS]


def mlp_forward_kernel(layer, info, *refs):
    xp_ref, terms, norms, bias_ref, own_up, own_down = refs[0], refs[1 : 1 + TERMS], *split_refs(refs)
    bufs = refs[7 + TERMS : 11 + TERMS]
    xm_ref, c_ref, act_ref, slope_ref, w_up, sems, bias_rows, held = refs[11 + TERMS :]
    step = pl.program_id(0)

    @pl.when(step == 0)
    def _():
        mlp_fetch(layer, info, own_up, own_down, bufs, w_up, None, sems, bias_rows, START)
        fetch_parts(terms, held, sems, 56)

    normed = mlp_start(layer, xp_ref, both(held, step), *norms, xm_ref, c_ref)

    @pl.when(step == 0)
    def _():
        mlp_fetch(layer, info, own_up, own_down, bufs, w_up, None, sems, bias_rows, WAIT)

    half = w_up.shape[1] // 4
    for k in range(4):
        here = slice(k * half, (k + 1) * half)
        pre = nn(normed, w_up[:, here]) + unit_bias(layer, info, bias_ref, bias_rows, k)
        act, slope = gate_pair(pre)
        act_ref[0, :, here] = act.astype(bf16)
        slope_ref[0, :, here] = slope.astype(bf16)


def mlp_turn_kernel(layer, info, mine, theirs, *refs):
    xp_ref, terms, norms, bias_ref, own_up, own_down = refs[0], refs[1 : 1 + TERMS], *split_refs(refs)
    bufs, cot = refs[7 + TERMS : 11 + TERMS], refs[11 + TERMS : 15 + TERMS]
    xm_ref, c_ref, act_ref, dz_ref, dh_ref, sum_ref, upb_ref = refs[15 + TERMS : 22 + TERMS]
    parts = refs[22 + TERMS : -6]
    w_up, w_down, sems, bias_rows, cot_rows, held = refs[-6:]
    step = pl.program_id(0)

    @pl.when(step == 0)
    def _():
        mlp_fetch(layer, info, own_up, own_down, bufs, w_up, w_down, sems, bias_rows, START)
        fetch_parts(terms, held, sems, 56)
        fetch(image_copies(info, cot, cot_rows), sems, 56)
        sum_ref[...] = jnp.zeros_like(sum_ref)
        upb_ref[...] = jnp.zeros_like(upb_ref)

    normed = mlp_start(layer, xp_ref, both(held, step), *norms, xm_ref, c_ref)
    grad = cot_rows[step].astype(f32)
    place = lax.broadcasted_iota(jnp.int32, grad.shape, 0)
    grad = jnp.where(place < fact(info, mine, theirs, step, 0), grad, 0.0)
    sum_ref[0:1, :] += jnp.sum(grad, axis=0, keepdims=True)
    low = grad.astype(bf16)
    dz_ref[0] = low

    @pl.when(step == 0)
    def _():
        mlp_fetch(layer, info, own_up, own_down, bufs, w_up, w_down, sems, bias_rows, WAIT)

    half = w_up.shape[1] // 4
    for k in range(4):
        here = slice(k * half, (k + 1) * half)
        pre = nn(normed, w_up[:, here]) + unit_bias(layer, info, bias_ref, bias_rows, k)
        act, slope = gate_pair(pre)
        act_ref[0, :, here] = act.astype(bf16)
        hidden = (nt(low, w_down[here, :]) * slope).astype(bf16)
        dh_ref[0, :, here] = hidden
        upb_ref[0:1, here] += jnp.sum(hidden.astype(f32), axis=0, keepdims=True)
    put_part(parts, step, nt(dh_ref[0], w_up[...]).astype(bf16))


def mlp_out_kernel(layer, info, act_ref, own_down, *refs):
    bufs, parts, w_down, sems = refs[:4], refs[4:-2], refs[-2], refs[-1]
    step = pl.program_id(0)

    @pl.when(step == 0)
    def _():
        mlp_fetch(layer, info, None, own_down, bufs, None, w_down, sems)

    put_part(parts, step, nn(act_ref[0], w_down[...]).astype(bf16))


def mlp_backward_kernel(layer, info, dx_ref, slope_ref, own_up, own_down, *refs):
    bufs = refs[:4]
    dz_ref, dh_ref, sum_ref, upb_ref = refs[4:8]
    parts = refs[8:-3]
    w_up, w_down, sems = refs[-3:]
    step = pl.program_id(0)

    @pl.when(step == 0)
    def _():
        mlp_fetch(layer, info, own_up, own_down, bufs, w_up, w_down, sems, phase=START)
        sum_ref[...] = jnp.zeros_like(sum_ref)
        upb_ref[...] = jnp.zeros_like(upb_ref)

    grad = dx_ref[0].astype(f32)
    sum_ref[0:1, :] += jnp.sum(grad, axis=0, keepdims=True)
    low = grad.astype(bf16)
    dz_ref[0] = low

    @pl.when(step == 0)
    def _():
        mlp_fetch(layer, info, own_up, own_down, bufs, w_up, w_down, sems, phase=WAIT)

    units = w_up.shape[1]
    for at in range(0, units, 384):
        hidden = nt(low, w_down[at : at + 384, :]) * slope_ref[0, :, at : at + 384].astype(f32)
        hidden = hidden.astype(bf16)
        dh_ref[0, :, at : at + 384] = hidden
        upb_ref[0:1, at : at + 384] += jnp.sum(hidden.astype(f32), axis=0, keepdims=True)
    put_part(parts, step, nt(dh_ref[0], w_up[...]).astype(bf16))


def mlp_weight_kernel(
    info, c_ref, dz_ref, act_ref, dh_ref, s1_ref, s1_late_ref, s2_ref, keep_ref, c_t, up, down
):
    step = pl.program_id(0)

    @pl.when(step == 0)
    def _():
        c_t[...] = turn(c_ref[...])

    up[...] = nn(c_t[...], dh_ref[...]).astype(bf16)
    down[...] = nn(turn(act_ref[...]), dz_ref[...]).astype(bf16)
    wide, tall = up.shape[0] // QUARTERS, down.shape[0] // QUARTERS
    split = down.shape[1] // 2

    def put(out, i):
        quarter = info[2 + i]
        out[0:wide, :] = up[rows16(wide * quarter, wide), :]
        rows = down[rows16(tall * quarter, tall), :]
        out[wide : wide + tall, :] = rows[:, :split]
        out[wide + tall :, :] = rows[:, split:]

    put(keep_ref.at[0], 0)
    put(s2_ref.at[0], 2)

    @pl.when(step < 2)
    def _():
        put(s1_ref.at[0, 0], 1)
        put(s1_ref.at[1, 0], 3)

    @pl.when(step >= 2)
    def _():
        put(s1_late_ref.at[0, 0], 1)
        put(s1_late_ref.at[1, 0], 3)


def attn_backward_kernel(
    layer, info, mine, theirs, dx_ref, xm_ref, gain_ref, qkv_ref, lse_ref, *refs
):
    terms, own_qkv, own_out = refs[:TERMS], refs[TERMS], refs[TERMS + 1]
    refs = refs[TERMS + 2 :]
    bufs = refs[:4]
    mid_ref, dy_ref, dqkv_ref, sum_ref, pair_ref = refs[4:9]
    parts = refs[9:-4]
    w_qkv, w_out, sems, held = refs[-4:]
    step = pl.program_id(0)

    @pl.when(step == 0)
    def _():
        attn_fetch(layer, info, own_qkv, own_out, bufs, w_qkv, w_out, sems, START)
        fetch_parts(terms, held, sems, 24)
        sum_ref[...] = jnp.zeros_like(sum_ref)
        pair_ref[...] = jnp.zeros_like(pair_ref)

    back = both(held, step)
    hat, scale = norm_parts(xm_ref[0])
    grad = dx_ref[0].astype(f32) + norm_back(hat, scale, gain_ref[layer, 1:2, :].astype(f32), back)
    mid_ref[0] = grad
    sum_ref[0:1, :] += jnp.sum(back * hat, axis=0, keepdims=True)
    sum_ref[1:2, :] += jnp.sum(back, axis=0, keepdims=True)
    sum_ref[2:3, :] += jnp.sum(grad, axis=0, keepdims=True)
    low_grad = grad.astype(bf16)
    dy_ref[0] = low_grad

    @pl.when(step == 0)
    def _():
        attn_fetch(layer, info, own_qkv, own_out, bufs, w_qkv, w_out, sems, WAIT)

    seq = grad.shape[0]
    d_mixed = nt(low_grad, w_out[...]).astype(bf16)
    low = head_masks(seq, 128, 1)
    low_t = head_masks(128, seq, 0)
    valid = lax.broadcasted_iota(jnp.int32, (seq, seq), 0) < fact(info, mine, theirs, step, 0)
    pairs = w_out.shape[0] // 128
    for p in range(pairs):
        query = qkv_ref[0, :, 384 * p : 384 * p + 128]
        key = qkv_ref[0, :, 384 * p + 128 : 384 * p + 256]
        value = qkv_ref[0, :, 384 * p + 256 : 384 * p + 384]
        grad_o = d_mixed[:, 128 * p : 128 * (p + 1)]
        key_t = turn(key)
        d_query, d_key, d_value = [], [], []
        for h in range(2):
            lanes = low if h == 0 else jnp.logical_not(low)
            none = jnp.zeros_like(key)
            scores = jnp.where(valid, nt(jnp.where(lanes, key, none), query), NEGATIVE)
            probs = jnp.exp(scores - lse_ref[0, 2 * p + h : 2 * p + h + 1, :])
            d_probs = nt(jnp.where(lanes, value, none), grad_o)
            along = jnp.sum(probs * d_probs, axis=0, keepdims=True)
            d_scores = (probs * (d_probs - along)).astype(bf16)
            d_value.append(nn(probs.astype(bf16), grad_o))
            d_key.append(nn(d_scores, query))
            d_query.append(nn(key_t, d_scores))
        d_query = jnp.where(low_t, d_query[0], d_query[1]).T * (HEAD_DIM**-0.5)
        d_key = pltpu.roll(jnp.where(low, d_key[0], d_key[1]), HEAD_DIM, 1)
        d_value = jnp.where(low, d_value[0], d_value[1])
        for j, block in enumerate(
            (
                jnp.where(low, d_query, d_key),
                jnp.where(low, d_value, d_query),
                jnp.where(low, d_key, d_value),
            )
        ):
            block = block.astype(bf16)
            at = 384 * p + 128 * j
            dqkv_ref[0, :, at : at + 128] = block
            pair_ref[0:1, at : at + 128] += jnp.sum(block.astype(f32), axis=0, keepdims=True)
    put_part(parts, step, nn(dqkv_ref[0], w_qkv[...]).astype(bf16))


def attn_weight_kernel(info, a_ref, dqkv_ref, dy_ref, mix_ref, s1_ref, s2_ref, keep_ref, w_in, w_out):
    for at in range(0, w_in.shape[0], 384):
        w_in[at : at + 384, :] = nn(turn(dqkv_ref[:, at : at + 384]), a_ref[...]).astype(bf16)
    w_out[...] = nn(turn(mix_ref[...]), dy_ref[...]).astype(bf16)
    rows_in, rows_out = w_in.shape[0] // 2, w_out.shape[0] // 2
    part_in, part_out = rows_in // QUARTERS, rows_out // QUARTERS
    for i, out in enumerate((keep_ref, s1_ref.at[0], s2_ref, s1_ref.at[1])):
        quarter = info[2 + i]
        for b in range(2):
            out[b, 0:part_in, :] = w_in[rows16(b * rows_in + part_in * quarter, part_in), :]
            out[b, part_in:, :] = w_out[rows16(b * rows_out + part_out * quarter, part_out), :]


def norm_backward_kernel(layer, info, mid_ref, xp_ref, gain_ref, *refs):
    terms, held, sems = refs[:TERMS], refs[-2], refs[-1]
    refs = refs[TERMS:]
    outs = refs[:1] if layer else refs[:2]
    at_ref, sum_ref = refs[len(outs) : len(outs) + 2]
    step = pl.program_id(0)

    @pl.when(step == 0)
    def _():
        fetch_parts(terms, held, sems)
        sum_ref[...] = jnp.zeros_like(sum_ref)

    back = both(held, step)
    hat, scale = norm_parts(xp_ref[0])
    grad = mid_ref[0] + norm_back(hat, scale, gain_ref[layer, 0:1, :].astype(f32), back)
    sum_ref[0:1, :] += jnp.sum(back * hat, axis=0, keepdims=True)
    sum_ref[1:2, :] += jnp.sum(back, axis=0, keepdims=True)
    top = at_ref.shape[1]
    place = lax.broadcasted_iota(jnp.int32, (top, grad.shape[1]), 0)
    here = (place >= 1) & (place <= PROMPTS)
    at_ref[0] = grad[:top]
    grad = jnp.concatenate([jnp.where(here, 0.0, grad[:top]), grad[top:]], axis=0)
    if layer:
        outs[0][0] = grad
    else:
        refs[-3][...] = grad.astype(bf16)
        send_rows(info, refs[-3], outs[0], outs[1])


def send_rows(info, rows, one_ref, two_ref):
    block = one_ref.shape[1]
    core, odd = info[0], info[1] & 1
    one_ref[0] = rows[rows16(block * (2 * core + odd), block), :]
    two_ref[0] = rows[rows16(block * (2 * core + 1 - odd), block), :]


def out_kernel(info, mine, theirs, xm_ref, branch_ref, *refs):
    terms, one_ref, two_ref, rows_held, held, sems = refs[:TERMS], *refs[TERMS:]
    step = pl.program_id(0)

    @pl.when(step == 0)
    def _():
        fetch_parts(terms, held, sems)

    after = branch_ref[LAYERS - 1, 1:2, :].astype(f32)
    rows = xm_ref[0] + (both(held, step) + after)
    place = lax.broadcasted_iota(jnp.int32, rows.shape, 0)
    here = place < fact(info, mine, theirs, step, 0)
    rows_held[...] = jnp.where(here, rows, 0.0).astype(bf16)
    send_rows(info, rows_held, one_ref, two_ref)


def facts_kernel(info, mask_ref, tasks_ref, out_ref):
    images = mask_ref.shape[0] // 2
    lane = lax.broadcasted_iota(jnp.int32, (2 * images, 128), 1)
    counts = jnp.sum(mask_ref[...].astype(f32), axis=1, keepdims=True).astype(jnp.int32)
    table = jnp.where(lane == 0, counts, 0)
    for layer in range(LAYERS):
        table = jnp.where(lane == 1 + layer, tasks_ref[:, layer : layer + 1], table)
    out_ref[...] = jnp.zeros_like(out_ref)
    out_ref[0:images, :] = jnp.where((info[1] & 1) == 0, table[:images], table[images:])


def attn_piece_kernel(layer, info, qkv_ref, out_ref, bias_ref, piece_ref, sems):
    part_in, part_out = qkv_ref.shape[1] // QUARTERS, out_ref.shape[1] // QUARTERS
    quarter = info[2]
    fetch(
        [
            (
                qkv_ref.at[layer, rows16(part_in * quarter, part_in)],
                piece_ref.at[pl.ds(0, part_in)],
            ),
            (
                out_ref.at[layer, rows16(part_out * quarter, part_out)],
                piece_ref.at[pl.ds(part_in, part_out)],
            ),
        ],
        sems,
    )
    bias = bias_ref[layer : layer + 1, :]
    bias = jnp.concatenate([bias, jnp.zeros_like(bias)], axis=1).astype(f32)
    piece_ref[part_in + part_out :, :] = jnp.broadcast_to(bias, (PAD, bias.shape[1])).astype(bf16)


def mlp_piece_kernel(layer, info, up_ref, down_ref, bias_ref, piece_ref, sems):
    width, half = up_ref.shape[1], down_ref.shape[1] // 2
    wide, tall, split = width // QUARTERS, half // QUARTERS, width // 2
    quarter, start = info[2], info[0] * half
    units = rows16(start + tall * quarter, tall)
    columns = pl.ds(pl.multiple_of(start, 128), half)
    fetch(
        [
            (up_ref.at[layer, rows16(wide * quarter, wide), columns], piece_ref.at[pl.ds(0, wide)]),
            (down_ref.at[layer, units, pl.ds(0, split)], piece_ref.at[pl.ds(wide, tall)]),
            (down_ref.at[layer, units, pl.ds(split, split)], piece_ref.at[pl.ds(wide + tall, tall)]),
        ],
        sems,
    )
    bias = bias_ref[layer : layer + 1, :].astype(f32)
    first = lax.broadcasted_iota(jnp.int32, (PAD, half), 0) == 0
    rows = jnp.where(first, bias[:, :half], bias[:, half:])
    piece_ref[wide + 2 * tall :, :] = rows.astype(bf16)


def image_piece_kernel(info, rows_ref, one_ref, two_ref, sems):
    images = one_ref.shape[0]
    odd = info[1] & 1
    fetch(
        [
            (rows_ref.at[pl.ds(odd * images, images)], one_ref),
            (rows_ref.at[pl.ds((1 - odd) * images, images)], two_ref),
        ],
        sems,
    )


def stack_kernel(*refs):
    bufs, out_ref, sems = refs[:-2], refs[-2], refs[-1]
    fetch([(buf, out_ref.at[k]) for k, buf in enumerate(bufs)], sems)


def by_half(early_ref, late_ref):
    return jnp.where(pl.program_id(0) < 2, early_ref[0, 0], late_ref[0, 0]).astype(f32)


def mlp_two_kernel(s2_ref, early_ref, late_ref, out_ref):
    out_ref[0] = (s2_ref[0].astype(f32) + by_half(early_ref, late_ref)).astype(bf16)


def add_two_kernel(s2_ref, got_ref, out_ref):
    out_ref[...] = (s2_ref[...].astype(f32) + got_ref[0].astype(f32)).astype(bf16)


def mlp_add_kernel(keep_ref, early_ref, late_ref, last_ref, own_ref, *outs):
    step = pl.program_id(0)
    total = keep_ref[0].astype(f32) + by_half(early_ref, late_ref) + last_ref[0].astype(f32)

    @pl.when(step == 0)
    def _():
        own_ref[...] = total

    for k, out in enumerate(outs):

        @pl.when(step == k + 1)
        def _(out=out):
            out[...] = total.astype(bf16)


def attn_add_kernel(keep_ref, got_ref, last_ref, own_ref, near_ref, far_ref):
    def total(b):
        return keep_ref[b].astype(f32) + got_ref[0, b].astype(f32) + last_ref[b].astype(f32)

    first = total(0)
    own_ref[...] = first
    far_ref[...] = first.astype(bf16)
    near_ref[...] = total(1).astype(bf16)


def attn_merge_kernel(info, own_ref, near_ref, far_ref, mine_ref, theirs_ref):
    half = mine_ref.shape[0]
    near = near_ref[...].astype(f32)

    @pl.when(info[0] == 0)
    def _():
        total = own_ref[...] + near
        mine_ref[...] = total[:half]
        theirs_ref[...] = total[half:].astype(bf16)

    @pl.when(info[0] != 0)
    def _():
        total = far_ref[...].astype(f32) + near
        mine_ref[...] = total[half:]
        theirs_ref[...] = total[:half].astype(bf16)


def sum_kernel(own_ref, *refs):
    total = own_ref[...].astype(f32)
    for ref in refs[:-1]:
        total += ref[...].astype(f32)
    refs[-1][...] = total.astype(refs[-1].dtype)


def pack_kernel(mine_ref, got_ref, units_ref, out_ref):
    total = (mine_ref[...] + got_ref[...].astype(f32)).astype(bf16)
    units, rows = units_ref.shape[0], total.shape[0]
    half = out_ref.shape[1]
    out_ref[0:units, :] = units_ref[...]
    out_ref[units : units + rows, :] = total[:, :half]
    out_ref[units + rows :, :] = total[:, half:]


def prompt_kernel(layer, per_dev, info, mine, theirs, at_ref, out_ref):
    top = at_ref.shape[1]
    tasks = [fact(info, mine, theirs, i, 1 + layer) for i in range(at_ref.shape[0])]
    for r in range(out_ref.shape[0]):
        for j in range(per_dev):
            task = ((info[6] ^ r) * 2 + info[0]) * per_dev + j
            total = jnp.zeros(at_ref.shape[1:], f32)
            for i, held in enumerate(tasks):
                total += jnp.where(held == task, at_ref[i], 0.0)
            out_ref[r, j * top : (j + 1) * top, :] = total.astype(bf16)


def sums_kernel(info, *refs):
    out_ref = refs[-1]
    core, z = info[0], info[1]
    half = refs[3].shape[1] // 4
    block = out_ref.shape[1] // 4
    out_ref[...] = jnp.zeros_like(out_ref)
    low = head_masks(1, 128, 1)
    for layer in range(LAYERS):
        norm, attn, mlp, upb, pair = refs[5 * layer : 5 * layer + 5]
        for i, row in enumerate((norm[0:1], attn[0:1], norm[1:2], attn[1:2], attn[2:3], mlp[0:1])):
            out_ref[6 * layer + i : 6 * layer + i + 1, :] = 0.5 * row
        heads = pair.shape[1] // (3 * HEAD_DIM)
        lines = []
        for h in range(heads):
            at = 384 * (h // 2)
            blocks = [pair[0:1, at + 128 * j : at + 128 * (j + 1)] for j in range(3)]
            middle = pltpu.roll(jnp.broadcast_to(blocks[1], (8, 128)), HEAD_DIM, 1)[0:1]
            if h % 2 == 0:
                lines.append(jnp.where(low, blocks[0], middle))
            else:
                lines.append(jnp.where(low, middle, blocks[2]))
        lines = [jnp.concatenate(lines[b * heads // 2 : (b + 1) * heads // 2], 1) for b in range(2)]
        for s in range(4):
            columns = slice(s * block, (s + 1) * block)
            line = jnp.zeros((1, half), f32)
            for k in range(4):
                line += jnp.where((z ^ s) == k, upb[0:1, k * half : (k + 1) * half], 0.0)
            at = 6 * LAYERS + 4 * layer
            for i in range(half // block):
                piece = line[:, i * block : (i + 1) * block]
                for c in range(2):
                    row = at + c * (half // block) + i
                    out_ref[row : row + 1, columns] = jnp.where(core == c, piece, 0.0)
            line = jnp.zeros_like(lines[0])
            for b in range(2):
                line += jnp.where((z ^ s) == jnp.where(core == 0, b, 3 - b), lines[b], 0.0)
            at = 10 * LAYERS + 2 * layer
            for i in range(2):
                out_ref[at + i : at + i + 1, columns] = line[:, i * block : (i + 1) * block]


def tail_first_kernel(planes, *refs):
    prompts, flat_ref, got_ref = refs[:LAYERS], refs[LAYERS], refs[LAYERS + 1]
    outs = refs[LAYERS + 2 :]
    flat = flat_ref[...] + got_ref[...].astype(f32)
    size = prompts[0].shape[1]
    for r in range(planes):
        for i, ref in enumerate(prompts):
            outs[r][i * size : (i + 1) * size, :] = ref[r].astype(outs[r].dtype)
        outs[r][LAYERS * size :, :] = flat.astype(outs[r].dtype)


def tail_middle_kernel(shards, info, own_ref, *refs):
    outs = refs[-shards:]
    total = own_ref[...]
    for ref in refs[:-shards]:
        total += ref[...].astype(f32)
    block = total.shape[1] // shards
    for s in range(shards):
        piece = total[:, s * block : (s + 1) * block]
        for k in range(shards):

            @pl.when((info[1] ^ k) == s)
            def _(k=k, piece=piece):
                outs[k][...] = piece.astype(outs[k].dtype)


def tail_end_kernel(per_dev, own_ref, *refs):
    got, outs = refs[:-6], refs[-6:]
    total = own_ref[...]
    for ref in got:
        total += ref[...].astype(f32)
    prompts_ref, gain_ref, bias_ref, branch_ref, units_ref, heads_ref = outs
    top, block = 64, total.shape[1]
    for layer in range(LAYERS):
        for j in range(per_dev):
            at = (layer * per_dev + j) * top
            prompts_ref[layer, j] = total[at : at + top][1 : 1 + PROMPTS]
        at = LAYERS * per_dev * top
        for i, ref in enumerate((gain_ref, bias_ref, branch_ref)):
            row = at + 6 * layer + 2 * i
            ref[layer] = total[row : row + 2]
        for i in range(4):
            row = at + 6 * LAYERS + 4 * layer + i
            units_ref[layer : layer + 1, i * block : (i + 1) * block] = total[row : row + 1]
        for i in range(2):
            row = at + 10 * LAYERS + 2 * layer + i
            heads_ref[layer : layer + 1, i * block : (i + 1) * block] = total[row : row + 1]


def collect_kernel(info, *refs):
    bufs, out_ref, sems = refs[:-2], refs[-2], refs[-1]
    fetch([(buf, out_ref.at[info[2 + r]]) for r, buf in enumerate(bufs)], sems)


def finish_kernel(info, mine_ref, theirs_ref, *refs):
    first = info[0] == 0
    halves = (mine_ref[0], theirs_ref[0])
    whole_ref = (jnp.where(first, *halves), jnp.where(first, *halves[::-1]))
    up_ref, down_ref, qkv_ref, out_ref = refs[-4:]
    wide = up_ref.shape[1]
    half = halves[0].shape[1]
    tall = down_ref.shape[3]
    part_in = qkv_ref.shape[1]
    split = down_ref.shape[4] // 2
    rows = (part_in + out_ref.shape[1]) // 2
    for c in range(2):
        up_ref[0, :, c * half : (c + 1) * half] = whole_ref[c][:wide].astype(f32)
        down_ref[0, c, 0, :, :split] = whole_ref[c][wide : wide + tall].astype(f32)
        down_ref[0, c, 0, :, split:] = whole_ref[c][wide + tall : wide + 2 * tall].astype(f32)
    for side in range(2):
        at = wide + 2 * tall + side * rows
        columns = slice(side * half, (side + 1) * half)
        both_rows = [whole_ref[c][at : at + rows].astype(f32) for c in range(2)]
        qkv_ref[0, :rows, columns] = both_rows[0]
        qkv_ref[0, rows:, columns] = both_rows[1][: part_in - rows]
        out_ref[0, :, columns] = both_rows[1][part_in - rows :]


def reversed_bits(value, bits):
    return sum(((value >> b) & 1) << (bits - 1 - b) for b in range(bits))


def call(kernel, deps, args, in_specs, **options):
    skip = len(deps)
    return pl.pallas_call(
        lambda *refs: kernel(*refs[skip:]), in_specs=[ANY] * skip + in_specs, **options
    )(*deps, *args)


def build(dp_size, tensor_size):
    planes = dp_size // 2
    bits = planes.bit_length() - 1
    zbits = tensor_size.bit_length() - 1

    def send(arr, target):
        pairs = []
        for dp in range(dp_size):
            for z in range(tensor_size):
                to = target(dp >> 1, dp & 1, z)
                if to is not None:
                    plane, core, depth = to
                    pairs.append((dp * tensor_size + z, (plane * 2 + core) * tensor_size + depth))
        return lax.ppermute(arr, AXES, pairs)

    def other_core(p, c, z):
        return p, 1 - c, z

    def along(k):
        return lambda p, c, z: (p, c, z ^ k)

    def across(bit):
        return lambda p, c, z: (p ^ (1 << bit), c, z)

    def flip(step):
        return lambda p, c, z: (p ^ (1 << ((1 - step) if c else step)), c, z)

    def near_of(p, c, z):
        return p, c, z ^ (1 + c)

    def far_of(p, c, z):
        return (p, c, z ^ 3) if c else None

    def plane_gather(piece):
        one = send(piece, flip(0))
        two = send(piece, flip(1))
        return [piece, one, two, send(one, flip(1))]

    def per_device(
        tokens,
        cotangent,
        task_ids,
        key_mask,
        prompts,
        norm_gain,
        norm_bias,
        qkv_weight,
        qv_bias,
        out_weight,
        branch_bias,
        up_weight,
        up_bias,
        down_weight,
    ):
        group, rows_local, width = tokens.shape
        images = group // 2
        seq = rows_local * tensor_size
        in_rows = qkv_weight.shape[2]
        heads = in_rows // (3 * HEAD_DIM)
        out_rows = heads * HEAD_DIM
        inner = 2 * out_rows
        hidden = up_weight.shape[2]
        half_units = hidden // 2
        units = half_units * tensor_size
        wide, tall = width // QUARTERS, half_units // QUARTERS
        task_count = prompts.shape[1]
        per_dev = task_count // dp_size
        z = lax.axis_index(ALONG)
        core = lax.axis_index(AXES[2])
        quarter = lax.axis_index(AXES[1])
        plane = lax.axis_index(AXES[0]) * QUARTERS + quarter
        first_core = core == 0
        odd = z & 1
        all_rows = images * seq
        top = 64

        def pick(arr, index, axis):
            return lax.dynamic_index_in_dim(arr, index, axis, keepdims=False)

        def join(mine, theirs, axis):
            return jnp.where(
                first_core,
                jnp.concatenate([mine, theirs], axis),
                jnp.concatenate([theirs, mine], axis),
            )

        def image_pieces(deps, arr):
            return call(
                image_piece_kernel,
                deps,
                (info, arr),
                [SMEM, ANY],
                out_specs=[VMEM] * 2,
                out_shape=[out_of(images, rows_local, width)] * 2,
                scratch_shapes=[pltpu.SemaphoreType.DMA((2,))],
                cost_estimate=cost(0, 2 << 20),
            )

        def gather_images(one, two):
            got_one = send(one, lambda p, c, d: (p, d >> 1, 2 * c + (d & 1)))
            got_two = send(two, lambda p, c, d: (p, d >> 1, 2 * c + 1 - (d & 1)))
            return got_one, got_two, send(got_one, other_core), send(got_two, other_core)

        def spread_images(one, two):
            return [
                send(one, lambda p, c, d: (p, d >> 1, 2 * c + (d & 1))),
                send(two, lambda p, c, d: (p, d >> 1, 2 * c + 1 - (d & 1))),
            ]

        def in_order(got_one, got_two):
            return jnp.where(
                odd == 0,
                jnp.concatenate([got_one, got_two], 0),
                jnp.concatenate([got_two, got_one], 0),
            )

        ranks = [
            quarter ^ jnp.where(first_core, r, reversed_bits(r, 2)) for r in range(QUARTERS)
        ]
        info = jnp.stack([core, z] + ranks + [plane]).astype(jnp.int32)

        def exchange(parts):
            return (*parts, *(send(part, other_core) for part in parts))

        def out_of(*shape, dtype=bf16):
            return jax.ShapeDtypeStruct(shape, dtype)

        qkv_rows = qkv_weight.swapaxes(1, 2)
        by_task = prompts.swapaxes(1, 2).reshape(LAYERS, PROMPTS * task_count, width)

        def facts_table(deps):
            return call(
                facts_kernel,
                deps,
                (info, key_mask, task_ids),
                [SMEM, VMEM, VMEM],
                out_specs=VMEM,
                out_shape=out_of(8, 128, dtype=jnp.int32),
                cost_estimate=cost(0, 0),
            )

        def attn_piece(deps, layer):
            last = in_rows // 4 + out_rows // 4
            piece = call(
                functools.partial(attn_piece_kernel, layer),
                deps,
                (info, qkv_rows, out_weight, qv_bias),
                [SMEM, ANY, ANY, VMEM],
                out_specs=VMEM,
                out_shape=out_of(last + PAD, width),
                scratch_shapes=[pltpu.SemaphoreType.DMA((2,))],
                cost_estimate=cost(0, 3 << 20),
            )
            return [piece]

        def attn_stack(deps, near, far):
            stacked = call(
                stack_kernel,
                deps,
                (near, far),
                [ANY] * 2,
                out_specs=VMEM,
                out_shape=out_of(2, *near.shape),
                scratch_shapes=[pltpu.SemaphoreType.DMA((2,))],
                cost_estimate=cost(0, 0),
            )
            return [stacked]

        def mlp_piece(deps, layer):
            piece = call(
                functools.partial(mlp_piece_kernel, layer),
                deps,
                (info, up_weight, down_weight, up_bias),
                [SMEM, ANY, ANY, VMEM],
                out_specs=VMEM,
                out_shape=out_of(wide + 2 * tall + PAD, half_units),
                scratch_shapes=[pltpu.SemaphoreType.DMA((3,))],
                cost_estimate=cost(0, 1 << 20),
            )
            return [piece]

        def mlp_stack(deps, got):
            stacked = call(
                stack_kernel,
                deps,
                got,
                [ANY] * len(got),
                out_specs=VMEM,
                out_shape=out_of(len(got), *got[0].shape),
                scratch_shapes=[pltpu.SemaphoreType.DMA((len(got),))],
                cost_estimate=cost(0, 0),
            )
            return [stacked]

        def image_block(size):
            return pl.BlockSpec((1, seq, size), lambda i: (i, 0, 0))

        def fixed(*shape):
            return pl.BlockSpec(shape, lambda i: (0,) * len(shape))

        rows_w, rows_w32 = out_of(images, seq, width), out_of(images, seq, width, dtype=f32)
        wide_block = image_block(width)
        attn_scratch = [
            pltpu.VMEM((2 * in_rows, width), bf16),
            pltpu.VMEM((inner, width), bf16),
            pltpu.SemaphoreType.DMA((32,)),
        ]
        terms_held = pltpu.VMEM((2 * all_rows, width), bf16)
        terms_sems = pltpu.SemaphoreType.DMA((TERMS,))

        def parts_specs(count):
            return [fixed(all_rows // count, width)] * count

        def parts_shapes(count):
            return [out_of(all_rows // count, width)] * count

        bias_scratch = pltpu.VMEM((tensor_size - 1, PAD, half_units), bf16)
        three = fixed(LAYERS, 2, width)
        two_rows = pl.BlockSpec((1, rows_local, width), lambda i: (i, 0, 0))
        two_blocks = out_of(images, rows_local, width)
        mlp_scratch = [
            pltpu.VMEM((width, units), bf16),
            pltpu.VMEM((units, width), bf16),
            pltpu.SemaphoreType.DMA((64,)),
        ]
        mm = 2 * all_rows * width
        heads_flops = 2 * images * 2 * heads * seq * seq * 128

        def attn_forward(layer, deps, x, bufs):
            later = layer > 0
            return call(
                functools.partial(attn_forward_kernel, layer),
                deps,
                (*facts(), *x, by_task, norm_gain, norm_bias, branch_bias, qv_bias)
                + (qkv_rows, out_weight, *bufs),
                [SMEM] * 3
                + ([wide_block] + [ANY] * TERMS if later else [ANY] * 4)
                + [pl.BlockSpec((1, PROMPTS * task_count, width), lambda i: (layer, 0, 0))]
                + [three] * 3
                + [fixed(*qv_bias.shape)]
                + [ANY] * 6,
                grid=(images,),
                out_specs=[
                    wide_block,
                    wide_block,
                    image_block(2 * in_rows),
                    image_block(inner),
                    pl.BlockSpec((1, 8, seq), lambda i: (i, 0, 0)),
                ],
                out_shape=[
                    rows_w32,
                    rows_w,
                    out_of(images, seq, 2 * in_rows),
                    out_of(images, seq, inner),
                    out_of(images, 8, seq, dtype=f32),
                ],
                scratch_shapes=attn_scratch[:1]
                + [pltpu.VMEM((2, PAD, width), bf16), attn_scratch[2]]
                + [terms_held if later else pltpu.VMEM((images, seq, width), bf16)],
                compiler_params=params(LIMIT),
                cost_estimate=cost(mm * (3 * inner + inner) + 2 * heads_flops, 12 << 20, 1 << 20),
                name="attn_forward",
            )

        def attn_out(layer, deps, mixed, bufs):
            return call(
                functools.partial(attn_out_kernel, layer),
                deps,
                (info, mixed, qkv_rows, out_weight, *bufs),
                [SMEM, image_block(inner)] + [ANY] * 6,
                grid=(images,),
                out_specs=parts_specs(PARTS),
                out_shape=parts_shapes(PARTS),
                scratch_shapes=attn_scratch[1:],
                compiler_params=params(LIMIT),
                cost_estimate=cost(0, 0),
                name="attn_out",
            )

        def mlp_forward(layer, deps, xp, terms, bufs):
            return call(
                functools.partial(mlp_forward_kernel, layer),
                deps,
                (info, xp, *terms, norm_gain, norm_bias, branch_bias, up_bias)
                + (up_weight, down_weight, *bufs),
                [SMEM, wide_block] + [ANY] * TERMS + [three] * 3 + [fixed(*up_bias.shape)] + [ANY] * 6,
                grid=(images,),
                out_specs=[wide_block, wide_block, image_block(units), image_block(units)],
                out_shape=[
                    rows_w32,
                    rows_w,
                    out_of(images, seq, units),
                    out_of(images, seq, units),
                ],
                scratch_shapes=[mlp_scratch[0], mlp_scratch[2], bias_scratch, terms_held],
                compiler_params=params(LIMIT),
                cost_estimate=cost(mm * 2 * units, 18 << 20, 1 << 20),
                name="mlp_forward",
            )

        def mlp_turn(layer, deps, xp, terms, bufs, cot):
            return call(
                functools.partial(mlp_turn_kernel, layer),
                deps,
                (*facts(), xp, *terms, norm_gain, norm_bias, branch_bias, up_bias)
                + (up_weight, down_weight, *bufs, *cot),
                [SMEM] * 3 + [wide_block] + [ANY] * TERMS + [three] * 3 + [fixed(*up_bias.shape)] + [ANY] * 10,
                grid=(images,),
                out_specs=[
                    wide_block,
                    wide_block,
                    image_block(units),
                    wide_block,
                    image_block(units),
                    fixed(8, width),
                    fixed(8, units),
                ]
                + parts_specs(PARTS),
                out_shape=[
                    rows_w32,
                    rows_w,
                    out_of(images, seq, units),
                    rows_w,
                    out_of(images, seq, units),
                    out_of(8, width, dtype=f32),
                    out_of(8, units, dtype=f32),
                ]
                + parts_shapes(PARTS),
                scratch_shapes=mlp_scratch
                + [bias_scratch, pltpu.VMEM((images, seq, width), bf16), terms_held],
                compiler_params=params(LIMIT),
                cost_estimate=cost(mm * 3 * units, 20 << 20, 1 << 20),
                name="mlp_turn",
            )

        def mlp_out(layer, deps, act, bufs):
            return call(
                functools.partial(mlp_out_kernel, layer),
                deps,
                (info, act, down_weight, *bufs),
                [SMEM, image_block(units)] + [ANY] * 5,
                grid=(images,),
                out_specs=parts_specs(PARTS),
                out_shape=parts_shapes(PARTS),
                scratch_shapes=mlp_scratch[1:],
                compiler_params=params(LIMIT),
                cost_estimate=cost(mm * units, 8 << 20),
                name="mlp_out",
            )

        def mlp_backward(layer, deps, dx, slope, bufs):
            return call(
                functools.partial(mlp_backward_kernel, layer),
                deps,
                (info, dx, slope, up_weight, down_weight, *bufs),
                [SMEM, wide_block, image_block(units)] + [ANY] * 6,
                grid=(images,),
                out_specs=[wide_block, image_block(units), fixed(8, width), fixed(8, units)]
                + parts_specs(PARTS),
                out_shape=[
                    rows_w,
                    out_of(images, seq, units),
                    out_of(8, width, dtype=f32),
                    out_of(8, units, dtype=f32),
                ]
                + parts_shapes(PARTS),
                scratch_shapes=mlp_scratch,
                compiler_params=params(LIMIT),
                cost_estimate=cost(mm * 2 * units, 16 << 20),
                name="mlp_backward",
            )

        piece_rows = wide + 2 * tall

        def early(first, *rest, at=0):
            return pl.BlockSpec((first, 1, *rest), lambda k: (at, jnp.minimum(k, 1), 0, 0))

        def late(first, *rest, at=0):
            return pl.BlockSpec((first, 1, *rest), lambda k: (at, jnp.maximum(k - 2, 0), 0, 0))


        def mlp_weights(deps, c, dz, act, dh):
            flat = lambda arr: arr.reshape(all_rows, arr.shape[2])
            by_shard = pl.BlockSpec((all_rows, half_units), lambda k: (0, k))
            return call(
                mlp_weight_kernel,
                deps,
                (info, flat(c), flat(dz), flat(act), flat(dh)),
                [SMEM, fixed(all_rows, width), fixed(all_rows, width), by_shard, by_shard],
                grid=(tensor_size,),
                out_specs=[
                    early(2, piece_rows, half_units),
                    late(2, piece_rows, half_units),
                    pl.BlockSpec((1, piece_rows, half_units), lambda k: (k, 0, 0)),
                    pl.BlockSpec((1, piece_rows, half_units), lambda k: (k, 0, 0)),
                ],
                out_shape=[
                    out_of(2, tensor_size // 2, piece_rows, half_units),
                    out_of(2, tensor_size // 2, piece_rows, half_units),
                    out_of(tensor_size, piece_rows, half_units),
                    out_of(tensor_size, piece_rows, half_units),
                ],
                scratch_shapes=[
                    pltpu.VMEM((width, all_rows), bf16),
                    pltpu.VMEM((width, half_units), bf16),
                    pltpu.VMEM((half_units, width), bf16),
                ],
                compiler_params=params(LIMIT),
                cost_estimate=cost(mm * 2 * units, 14 << 20),
                name="mlp_weights",
            )

        def attn_backward(layer, deps, dx, terms, xm, qkv, lse, bufs):
            return call(
                functools.partial(attn_backward_kernel, layer),
                deps,
                (*facts(), dx, xm, norm_gain, qkv, lse, *terms)
                + (qkv_rows, out_weight, *bufs),
                [SMEM] * 3
                + [wide_block] * 2
                + [three, image_block(2 * in_rows)]
                + [pl.BlockSpec((1, 8, seq), lambda i: (i, 0, 0))]
                + [ANY] * (TERMS + 6),
                grid=(images,),
                out_specs=[
                    wide_block,
                    wide_block,
                    image_block(2 * in_rows),
                    fixed(8, width),
                    fixed(8, 2 * in_rows),
                ]
                + parts_specs(PARTS),
                out_shape=[
                    rows_w32,
                    rows_w,
                    out_of(images, seq, 2 * in_rows),
                    out_of(8, width, dtype=f32),
                    out_of(8, 2 * in_rows, dtype=f32),
                ]
                + parts_shapes(PARTS),
                scratch_shapes=attn_scratch + [terms_held],
                compiler_params=params(LIMIT),
                cost_estimate=cost(mm * (3 * inner + inner) + 5 * heads_flops, 15 << 20, 1 << 20),
                name="attn_backward",
            )

        attn_rows = in_rows // 4 + out_rows // 4

        def attn_weights(deps, a, dqkv, dy, mixed):
            flat = lambda arr: arr.reshape(all_rows, arr.shape[2])
            return call(
                attn_weight_kernel,
                deps,
                (info, flat(a), flat(dqkv), flat(dy), flat(mixed)),
                [SMEM] + [VMEM] * 4,
                out_specs=[VMEM] * 3,
                out_shape=[
                    out_of(2, 2, attn_rows, width),
                    out_of(2, attn_rows, width),
                    out_of(2, attn_rows, width),
                ],
                scratch_shapes=[
                    pltpu.VMEM((2 * in_rows, width), bf16),
                    pltpu.VMEM((inner, width), bf16),
                ],
                compiler_params=params(LIMIT),
                cost_estimate=cost(mm * (3 * inner + inner), 10 << 20),
                name="attn_weights",
            )

        def norm_backward(layer, deps, mid, terms, xp):
            return call(
                functools.partial(norm_backward_kernel, layer),
                deps,
                (info, mid, xp, norm_gain, *terms),
                [SMEM] + [wide_block] * 2 + [three] + [ANY] * TERMS,
                grid=(images,),
                out_specs=([wide_block] if layer else [two_rows] * 2)
                + [pl.BlockSpec((1, top, width), lambda i: (i, 0, 0)), fixed(8, width)],
                out_shape=([rows_w32] if layer else [two_blocks] * 2)
                + [out_of(images, top, width, dtype=f32), out_of(8, width, dtype=f32)],
                scratch_shapes=([] if layer else [pltpu.VMEM((seq, width), bf16)])
                + [terms_held, terms_sems],
                compiler_params=params(LIMIT),
                cost_estimate=cost(20 * all_rows * width, 9 << 20),
                name="norm_backward",
            )

        def out_pieces(deps, xm, terms):
            return call(
                out_kernel,
                deps,
                (*facts(), xm, branch_bias, *terms),
                [SMEM] * 3 + [wide_block, three] + [ANY] * TERMS,
                grid=(images,),
                out_specs=[two_rows] * 2,
                out_shape=[two_blocks] * 2,
                scratch_shapes=[pltpu.VMEM((seq, width), bf16), terms_held, terms_sems],
                compiler_params=params(LIMIT),
                cost_estimate=cost(0, 0),
            )

        def finish(layer, deps, whole, before):
            return call(
                finish_kernel,
                deps,
                (info, whole, send(whole, other_core), *before),
                [SMEM]
                + [pl.BlockSpec((1,) + whole.shape[1:], lambda q: (q, 0, 0))] * 2
                + [ANY] * len(before),
                grid=(QUARTERS,),
                out_specs=[
                    pl.BlockSpec((1, wide, hidden), lambda q: (layer, q, 0)),
                    pl.BlockSpec((1, 2, 1, tall, width), lambda q: (layer, 0, q, 0, 0)),
                    pl.BlockSpec((1, in_rows // QUARTERS, width), lambda q: (layer, q, 0)),
                    pl.BlockSpec((1, out_rows // QUARTERS, width), lambda q: (layer, q, 0)),
                ],
                out_shape=[
                    out_of(LAYERS, width, hidden, dtype=f32),
                    out_of(LAYERS, 2, QUARTERS, tall, width, dtype=f32),
                    out_of(LAYERS, in_rows, width, dtype=f32),
                    out_of(LAYERS, out_rows, width, dtype=f32),
                ],
                input_output_aliases={len(deps) + 3 + i: i for i in range(len(before))},
                compiler_params=params(LIMIT),
                cost_estimate=cost(0, 0),
                name="finish",
            )

        def pack(deps, mine, got, units_sum):
            rows = units_sum.shape[0] + 2 * mine.shape[0]
            return call(
                pack_kernel,
                deps,
                (mine, got, units_sum),
                [VMEM] * 3,
                out_specs=VMEM,
                out_shape=out_of(rows, half_units),
                compiler_params=params(LIMIT),
                cost_estimate=cost(0, 0),
            )

        def add_two(deps, s2, got):
            grid = s2.shape[0]
            block = (1,) + s2.shape[1:]
            return call(
                lambda a, b, o: add_two_kernel(a, b.at[0], o),
                deps,
                (s2, got),
                [
                    pl.BlockSpec(block, lambda i: (i, 0, 0)),
                    pl.BlockSpec((1,) + block, lambda i: (1, i, 0, 0)),
                ],
                grid=(grid,),
                out_specs=pl.BlockSpec(block, lambda i: (i, 0, 0)),
                out_shape=out_of(*s2.shape),
                compiler_params=params(LIMIT),
                cost_estimate=cost(0, 0),
                name="add_two",
            )

        def mlp_two(deps, s2, got):
            block = (1,) + s2.shape[1:]
            return call(
                mlp_two_kernel,
                deps,
                (s2, *got),
                [
                    pl.BlockSpec(block, lambda i: (i, 0, 0)),
                    early(1, *s2.shape[1:], at=1),
                    late(1, *s2.shape[1:], at=1),
                ],
                grid=(tensor_size,),
                out_specs=pl.BlockSpec(block, lambda i: (i, 0, 0)),
                out_shape=out_of(*s2.shape),
                compiler_params=params(LIMIT),
                cost_estimate=cost(0, 0),
                name="mlp_two",
            )

        def mlp_add(deps, keep, got, last):
            block = (1,) + keep.shape[1:]
            piece = keep.shape[1:]
            return call(
                mlp_add_kernel,
                deps,
                (keep, *got, last),
                [
                    pl.BlockSpec(block, lambda i: (i, 0, 0)),
                    early(1, *piece),
                    late(1, *piece),
                    pl.BlockSpec(block, lambda i: (i, 0, 0)),
                ],
                grid=(tensor_size,),
                out_specs=[fixed(*piece)] * tensor_size,
                out_shape=[out_of(*piece, dtype=f32)] + [out_of(*piece)] * (tensor_size - 1),
                compiler_params=params(LIMIT),
                cost_estimate=cost(0, 0),
                name="mlp_add",
            )

        def attn_add(deps, keep, got, last):
            piece = keep.shape[1:]
            return call(
                attn_add_kernel,
                deps,
                (keep, got, last),
                [
                    fixed(*keep.shape),
                    pl.BlockSpec((1,) + keep.shape, lambda i: (0, 0, 0, 0)),
                    fixed(*keep.shape),
                ],
                grid=(1,),
                out_specs=[fixed(*piece)] * 3,
                out_shape=[out_of(*piece, dtype=f32)] + [out_of(*piece)] * 2,
                compiler_params=params(LIMIT),
                cost_estimate=cost(0, 0),
                name="attn_add",
            )

        def attn_merge(deps, own, near, far):
            half = (own.shape[0] // 2,) + own.shape[1:]
            return call(
                attn_merge_kernel,
                deps,
                (info, own, near, far),
                [SMEM] + [VMEM] * 3,
                out_specs=[VMEM] * 2,
                out_shape=[out_of(*half, dtype=f32), out_of(*half)],
                compiler_params=params(LIMIT),
                cost_estimate=cost(0, 0),
                name="attn_merge",
            )

        def add_up(deps, own, *others, dtype=bf16):
            return call(
                sum_kernel,
                deps,
                (own, *others),
                [VMEM] * (1 + len(others)),
                out_specs=VMEM,
                out_shape=out_of(*own.shape, dtype=dtype),
                compiler_params=params(LIMIT),
                cost_estimate=cost(0, 0),
            )

        def prompt_rows_of(layer, deps, at):
            return call(
                functools.partial(prompt_kernel, layer, per_dev),
                deps,
                (*facts(), at),
                [SMEM] * 3 + [VMEM],
                out_specs=VMEM,
                out_shape=out_of(planes, per_dev * top, width),
                compiler_params=params(LIMIT),
                cost_estimate=cost(0, 0),
            )

        def row_sums(deps, sums):
            return call(
                sums_kernel,
                deps,
                (info, *sums),
                [SMEM] + [VMEM] * len(sums),
                out_specs=VMEM,
                out_shape=out_of(12 * LAYERS, width, dtype=f32),
                compiler_params=params(LIMIT),
                cost_estimate=cost(0, 0),
            )

        def tail_first(deps, parts, flat, got):
            rows = LAYERS * per_dev * top + flat.shape[0]
            return call(
                functools.partial(tail_first_kernel, planes),
                deps,
                (*parts, flat, got),
                [VMEM] * (len(parts) + 2),
                out_specs=[VMEM] * planes,
                out_shape=[out_of(rows, width, dtype=f32)] + [out_of(rows, width)] * (planes - 1),
                compiler_params=params(LIMIT),
                cost_estimate=cost(0, 0),
            )

        def tail_middle(deps, own, got):
            rows, block = own.shape[0], width // tensor_size
            return call(
                functools.partial(tail_middle_kernel, tensor_size),
                deps,
                (info, own, *got),
                [SMEM] + [VMEM] * (1 + len(got)),
                out_specs=[VMEM] * tensor_size,
                out_shape=[out_of(rows, block, dtype=f32)]
                + [out_of(rows, block)] * (tensor_size - 1),
                compiler_params=params(LIMIT),
                cost_estimate=cost(0, 0),
            )

        def collect(deps, piece):
            return call(
                collect_kernel,
                deps,
                (info, *plane_gather(piece)),
                [SMEM] + [ANY] * QUARTERS,
                out_specs=VMEM,
                out_shape=out_of(QUARTERS, *piece.shape),
                scratch_shapes=[pltpu.SemaphoreType.DMA((QUARTERS,))],
                compiler_params=params(LIMIT),
                cost_estimate=cost(0, 0),
            )

        out, sent, last = {}, {}, []

        def once(name, make):
            if name not in sent:
                sent[name] = make()
            return sent[name]

        def moved(name, arr, target):
            return once(name, lambda: send(arr, target))

        def terms(name):
            parts = out[name][-PARTS:]
            return once("e>" + name, lambda: exchange(parts))

        def pair_z(name):
            near, far = out[name][1], out[name][2]
            return moved(name + ">n", near, near_of), moved(name + ">f", far, far_of)

        def shards(name, first):
            pieces = out[name][first:]
            return [moved("%s>%d" % (name, k), p, along(k + 1)) for k, p in enumerate(pieces)]

        def bufs(name):
            return once("b>" + name, lambda: plane_gather(out[name][0]))

        def facts():
            return info, out["facts"][0], moved("facts>", out["facts"][0], other_core)

        def x_of(name):
            return once("x>" + name, lambda: gather_images(*out[name]))

        def near_far(name):
            piece = out[name][0]
            return moved(name + ">n", piece, near_of), moved(name + ">f", piece, far_of)

        def stack_mlp(deps, name):
            piece = out[name][0]
            got = [moved("%s>%d" % (name, k), piece, along(k)) for k in range(1, tensor_size)]
            return mlp_stack(deps, got)

        def spread(name):
            return once("spread>" + name, lambda: spread_images(*out[name][:2]))

        def s1(name):
            if name[0] == "a":
                return moved("one>" + name, out["w" + name][0], flip(0))
            return [moved("one%d>%s" % (i, name), out["w" + name][i], flip(0)) for i in range(2)]

        def last_of(name):
            return moved("two>" + name, out["t" + name][0], flip(1))

        def forward_0(deps):
            return attn_forward(0, deps, x_of("tok"), bufs("sa0"))

        def forward_1(deps):
            return attn_forward(1, deps, (out["fm0"][0], *terms("om0")), bufs("sa1"))

        def mlp_0(deps):
            return mlp_forward(0, deps, out["fa0"][0], terms("oa0"), bufs("sm0"))

        def turn_1(deps):
            return mlp_turn(1, deps, out["fa1"][0], terms("oa1"), bufs("sm1"), x_of("cot"))

        def weights_m1(deps):
            return mlp_weights(deps, *(out["turn"][i] for i in (1, 3, 2, 4)))

        def weights_m0(deps):
            return mlp_weights(deps, out["fm0"][1], out["bm0"][0], out["fm0"][2], out["bm0"][1])

        def backward_a1(deps):
            _, _, qkv, _, lse = out["fa1"]
            dz, xm = out["turn"][3], out["turn"][0]
            return attn_backward(1, deps, dz, terms("turn"), xm, qkv, lse, bufs("sa1"))

        def backward_a0(deps):
            _, _, qkv, _, lse = out["fa0"]
            xm, dx = out["fm0"][0], out["nb1"][0]
            return attn_backward(0, deps, dx, terms("bm0"), xm, qkv, lse, bufs("sa0"))

        def weights_a(deps, layer):
            forward, back = out["fa%d" % layer], out["ba%d" % layer]
            return attn_weights(deps, forward[1], back[2], back[1], forward[3])

        def norm_b(deps, layer):
            back = out["ba%d" % layer]
            return norm_backward(layer, deps, back[0], terms("ba%d" % layer), out["fa%d" % layer][0])

        def two(deps, name):
            add = mlp_two if name[0] == "m" else add_two
            return [add(deps, out["w" + name][-2], s1(name))]

        def z_add(deps, name):
            add = mlp_add if name[0] == "m" else attn_add
            return add(deps, out["w" + name][-1], s1(name), last_of(name))

        def over_groups(arr):
            for b in range(2, bits):
                arr = (arr.astype(f32) + send(arr, across(b)).astype(f32)).astype(bf16)
            return [arr]

        def z_sum(deps, name):
            return [add_up(deps, out["z" + name][0], *shards("z" + name, 1))]

        def merge(deps, name):
            return attn_merge(deps, out["z" + name][0], *pair_z("z" + name))

        def pack_of(deps, layer):
            mine, theirs = out["ra%d" % layer]
            got = moved("core>%d" % layer, theirs, other_core)
            return over_groups(pack(deps, mine, got, out["hm%d" % layer][0]))

        def sums_of(deps):
            sums = ()
            for layer, mlp in ((0, "bm0"), (1, "turn")):
                sum_mlp, upb = (out[mlp][2], out[mlp][3]) if layer == 0 else out[mlp][5:7]
                back = out["ba%d" % layer]
                sums += (out["nb%d" % layer][-1], back[3], sum_mlp, upb, back[4])
            return [row_sums(deps, sums)]

        def tail_one(deps):
            flat = out["rs"][0]
            parts = [out["pr0"][0], out["pr1"][0]]
            return tail_first(deps, parts, flat, moved("flat>", flat, other_core))

        def tail_two(deps):
            parts = out["tf"]
            got = [
                moved("tf>%d" % r, parts[r], lambda p, c, d, r=r: (p ^ r, c, d))
                for r in range(1, planes)
            ]
            return tail_middle(deps, parts[0], got)

        def tail_end(deps):
            got = shards("tm", 1)
            block = width // tensor_size
            shapes = [(LAYERS, per_dev, PROMPTS, block)] + [(LAYERS, 2, block)] * 3
            shapes += [(LAYERS, hidden), (LAYERS, 2 * out_rows)]
            return call(
                functools.partial(tail_end_kernel, per_dev),
                deps,
                (out["tm"][0], *got),
                [VMEM] * (1 + len(got)),
                out_specs=[VMEM] * len(shapes),
                out_shape=[out_of(*shape, dtype=f32) for shape in shapes],
                compiler_params=params(LIMIT),
                cost_estimate=cost(0, 0),
            )

        steps = {
            "facts": lambda d: [facts_table(d)],
            "tok": lambda d: image_pieces(d, tokens),
            "cot": lambda d: image_pieces(d, cotangent),
            "pa0": lambda d: attn_piece(d, 0),
            "pa1": lambda d: attn_piece(d, 1),
            "pm0": lambda d: mlp_piece(d, 0),
            "pm1": lambda d: mlp_piece(d, 1),
            "sa0": lambda d: attn_stack(d, *near_far("pa0")),
            "sa1": lambda d: attn_stack(d, *near_far("pa1")),
            "sm0": lambda d: stack_mlp(d, "pm0"),
            "sm1": lambda d: stack_mlp(d, "pm1"),
            "fa0": forward_0,
            "oa0": lambda d: attn_out(0, d, out["fa0"][3], bufs("sa0")),
            "fm0": mlp_0,
            "om0": lambda d: mlp_out(0, d, out["fm0"][2], bufs("sm0")),
            "fa1": forward_1,
            "oa1": lambda d: attn_out(1, d, out["fa1"][3], bufs("sa1")),
            "turn": turn_1,
            "wm1": weights_m1,
            "ba1": backward_a1,
            "wa1": lambda d: weights_a(d, 1),
            "nb1": lambda d: norm_b(d, 1),
            "tm1": lambda d: two(d, "m1"),
            "bm0": lambda d: mlp_backward(0, d, out["nb1"][0], out["fm0"][3], bufs("sm0")),
            "ta1": lambda d: two(d, "a1"),
            "wm0": weights_m0,
            "zm1": lambda d: z_add(d, "m1"),
            "za1": lambda d: z_add(d, "a1"),
            "ba0": backward_a0,
            "hm1": lambda d: z_sum(d, "m1"),
            "ra1": lambda d: merge(d, "a1"),
            "ca1": lambda d: pack_of(d, 1),
            "wa0": lambda d: weights_a(d, 0),
            "tm0": lambda d: two(d, "m0"),
            "nb0": lambda d: norm_b(d, 0),
            "rs": sums_of,
            "pr0": lambda d: [prompt_rows_of(0, d, out["nb0"][2])],
            "pr1": lambda d: [prompt_rows_of(1, d, out["nb1"][1])],
            "ta0": lambda d: two(d, "a0"),
            "zm0": lambda d: z_add(d, "m0"),
            "za0": lambda d: z_add(d, "a0"),
            "hm0": lambda d: z_sum(d, "m0"),
            "ra0": lambda d: merge(d, "a0"),
            "ca0": lambda d: pack_of(d, 0),
            "co1": lambda d: [collect(d, out["ca1"][0])],
            "co0": lambda d: [collect(d, out["ca0"][0])],
            "fi1": lambda d: finish(1, d, out["co1"][0], ()),
            "fi0": lambda d: finish(0, d, out["co0"][0], out["fi1"]),
            "tf": tail_one,
            "tm": tail_two,
            "te": tail_end,
            "om1": lambda d: mlp_out(1, d, out["turn"][2], bufs("sm1")),
            "op": lambda d: out_pieces(d, out["turn"][0], terms("om1")),
        }
        arrivals = {
            "f": lambda name: [facts()[2]],
            "o": spread,
            "t": lambda name: shards("tm", 1),
            "x": lambda name: x_of(name)[:2],
            "y": lambda name: x_of(name)[2:],
            "p": near_far,
            "1": lambda name: [bufs(name)[1]],
            "2": lambda name: [bufs(name)[2]],
            "3": lambda name: [bufs(name)[3]],
            "e": lambda name: terms(name)[PARTS:],
            "s": lambda name: [s1(name)],
            "l": lambda name: [last_of(name)],
            "z": lambda name: shards("z" + name, 1),
            "q": lambda name: pair_z("z" + name),
        }
        for name in " ".join(ORDER).split():
            if name[0] == "<":
                last += jax.tree.leaves(arrivals[name[1]](name[3:]))
                continue
            out[name] = steps[name](tuple(last))
            last = [out[name][0]]

        full_up, full_down, full_qkv, full_out = out["fi0"]
        grad_tokens = in_order(*spread("nb0"))
        out_rows_sent = in_order(*spread("op"))
        grad_prompts, grad_gain, grad_bias, grad_branch, grad_upb, grad_pair = out["te"]
        full_qkv = full_qkv.swapaxes(1, 2)
        return (
            out_rows_sent,
            grad_tokens,
            grad_prompts,
            grad_gain,
            grad_bias,
            full_qkv,
            grad_pair,
            full_out,
            grad_branch,
            full_up,
            grad_upb,
            full_down.reshape(LAYERS, hidden, width),
        )

    return per_device


def solution(mesh):
    dp_size, tensor_size = mesh.shape["dp"], mesh.shape[ALONG]
    shape = (dp_size // (2 * QUARTERS), QUARTERS, 2, tensor_size)
    mesh = jax.sharding.Mesh(mesh.devices.reshape(shape), AXES)
    dp = AXES[:3]
    placed = (
        P(dp, ALONG, None),
        P(dp, ALONG, None),
        P(dp, None),
        P(dp, None),
        P(),
        P(),
        P(),
        P(None, None, ALONG),
        P(None, ALONG),
        P(None, ALONG, None),
        P(),
        P(None, None, ALONG),
        P(None, ALONG),
        P(None, ALONG, None),
    )
    return jax.shard_map(
        build(dp_size, tensor_size),
        mesh=mesh,
        in_specs=placed,
        out_specs=(
            P(dp, ALONG, None),
            P(dp, ALONG, None),
            P(None, dp, None, ALONG),
            P(None, None, ALONG),
            P(None, None, ALONG),
            P(None, None, ALONG),
            P(None, ALONG),
            P(None, ALONG, None),
            P(None, None, ALONG),
            P(None, None, ALONG),
            P(None, ALONG),
            P(None, ALONG, None),
        ),
        check_vma=False,
    )
```
